32 devices in a mesh: wide: 8 (over z, y), narrow: 4 (over x, core).
Axes of the slice: x: 2, y: 2, z: 4, core: 2. Of those that a mesh axis runs over, the one named last changes fastest.
Arguments:
- hidden_in: bfloat16 [8192, 768], P(('wide', 'narrow')), may hold values from -6 to 6
- segments: int32 [8192], P(('wide', 'narrow')), may hold values from 0 to 3, as said below
- routing: int32 [8192, 1], P(('wide', 'narrow')), may hold values from 0 to 7, as said below
- first_gain: float32 [768], P(('wide', 'narrow')), may hold values from 0.5 to 1.5
- first_bias: float32 [768], P(('wide', 'narrow')), may hold values from -0.5 to 0.5
- second_gain: float32 [768], P(('wide', 'narrow')), may hold values from 0.5 to 1.5
- second_bias: float32 [768], P(('wide', 'narrow')), may hold values from -0.5 to 0.5
- w_query: float32 [768, 768], P(('wide', 'narrow')), may hold values from -0.21875 to 0.21875
- w_key: float32 [768, 768], P(('wide', 'narrow')), may hold values from -0.21875 to 0.21875
- w_value: float32 [768, 768], P(('wide', 'narrow')), may hold values from -0.21875 to 0.21875
- w_out: float32 [768, 768], P(('wide', 'narrow')), may hold values from -0.875 to 0.875
- w_router: float32 [768, 8], P(('wide', 'narrow')), may hold values from -0.15625 to 0.15625
- w_in: float32 [8, 768, 3072], P('wide', None, 'narrow'), may hold values from -0.21875 to 0.21875
- w_back: float32 [8, 3072, 768], P('wide', 'narrow'), may hold values from -0.109375 to 0.109375
- cotangent: bfloat16 [8192, 768], P(('wide', 'narrow')), may hold values from -6 to 6
Outputs:
- block_out: float32 [8192, 768], P(('wide', 'narrow'))
- balance_loss: float32 [], replicated
- grad_hidden_in: float32 [8192, 768], P(('wide', 'narrow'))
- grad_first_gain: float32 [768], P(('wide', 'narrow'))
- grad_first_bias: float32 [768], P(('wide', 'narrow'))
- grad_second_gain: float32 [768], P(('wide', 'narrow'))
- grad_second_bias: float32 [768], P(('wide', 'narrow'))
- grad_w_query: float32 [768, 768], P(('wide', 'narrow'))
- grad_w_key: float32 [768, 768], P(('wide', 'narrow'))
- grad_w_value: float32 [768, 768], P(('wide', 'narrow'))
- grad_w_out: float32 [768, 768], P(('wide', 'narrow'))
- grad_w_router: float32 [768, 8], P(('wide', 'narrow'))
- grad_w_in: float32 [8, 768, 3072], P('wide', None, 'narrow')
- grad_w_back: float32 [8, 3072, 768], P('wide', 'narrow')
The draws below stay inside these ranges and needn't reach their ends.
Inputs may be any that keep to these rules, and one draw needn't show every extreme that they name: `segments`: each group of 1024 consecutive tokens is either one sequence (all 0) or consecutive sequences of 256 tokens numbered 0, 1, 2 and so on; half of the groups are of each kind. `routing`: among the 256 rows of one device no expert is named by more than 64 rows; on every device some expert is named by exactly 64 rows.
All inputs are finite; a program needn't handle non-finite values.
Results may differ from the reference program's by a relative error of at most 0.015.
Values may be sent and summed in bfloat16 or wider, within the bound.
No kernel may reach another device: no remote copies, remote signals or barrier semaphores. Data moves between devices by JAX's collectives and lax.ppermute only.
A program may use at most 192 MiB of HBM per device.

```python
import jax
import jax.numpy as jnp
from jax import lax

D = 768
FF = 3072
HEADS = 12
HEAD_DIM = 64
SHORT = 256
TOK_DEV = 256
EXPERTS = 8
CAP = 64
GROUP = 1024
TOKENS = 8192
N_WIDE = 8
N_NARROW = 4


def draw_segments(key, part):
    key = jax.random.fold_in(key, 11)
    order = jax.random.permutation(key, TOKENS // GROUP)
    long_group = order < TOKENS // GROUP // 2
    places = jnp.arange(GROUP, dtype=jnp.int32)
    short_ids = places // SHORT
    seg_ids = jnp.where(long_group[:, None], 0, short_ids[None, :])
    return seg_ids.reshape(TOKENS).astype(jnp.int32)


def draw_routing(key, part):
    key = jax.random.fold_in(key, 23)
    block_count = TOKENS // TOK_DEV
    key_side, key_hot, key_extra, key_mix = jax.random.split(key, 4)
    rising = jax.random.permutation(key_side, EXPERTS) < EXPERTS // 2
    span = max(block_count - 1, 1)
    block_ids = jnp.arange(block_count, dtype=jnp.int32)
    weights = jnp.where(rising[None, :], span + 2 * block_ids[:, None], 3 * span - 2 * block_ids[:, None]).astype(jnp.int32)
    hot_ids = jax.random.randint(key_hot, (block_count,), 0, EXPERTS)
    is_hot = jnp.arange(EXPERTS, dtype=jnp.int32)[None, :] == hot_ids[:, None]
    weights = jnp.where(is_hot, 0, weights)
    remain = TOK_DEV - CAP
    quota = remain * weights // jnp.sum(weights, axis=1, keepdims=True)
    leftover = remain - jnp.sum(quota, axis=1, keepdims=True)
    priority = jax.vmap(lambda one_key: jax.random.permutation(one_key, EXPERTS))(jax.random.split(key_extra, block_count))
    priority = jnp.where(is_hot, EXPERTS, priority)
    ranks = jnp.argsort(jnp.argsort(priority, axis=1), axis=1)
    loads = jnp.where(is_hot, CAP, quota + (ranks < leftover).astype(jnp.int32))
    ends = jnp.cumsum(loads, axis=1)
    places = jnp.arange(TOK_DEV, dtype=jnp.int32)
    expert_ids = jnp.sum((places[None, :, None] >= ends[:, None, :]).astype(jnp.int32), axis=2)
    shuffles = jax.vmap(lambda one_key: jax.random.permutation(one_key, TOK_DEV))(jax.random.split(key_mix, block_count))
    expert_ids = jnp.take_along_axis(expert_ids, shuffles, axis=1)
    return expert_ids.reshape(TOKENS, 1).astype(jnp.int32)


def block_scale(rng, shape, pieces, smallest, largest):
    level = 1.0
    for axis_at, parts in pieces:
        heights = jax.random.uniform(jax.random.fold_in(jax.random.fold_in(rng, 6), axis_at), (parts,), jnp.float32, smallest / len(pieces), largest / len(pieces))
        level = level * jnp.repeat(jnp.exp(heights), shape[axis_at] // parts).reshape((-1,) + (1,) * (len(shape) - 1 - axis_at))
    return level


def noise(key, dims, scale, most, cuts=(), held_as=jnp.bfloat16):
    values = scale * jax.random.normal(key, dims, jnp.float32)
    if cuts:
        values = values * block_scale(key, dims, cuts, -0.22, 0.18)
    return jnp.clip(values, -most, most).astype(held_as)


def setup_inputs(seed: int = 0) -> dict:
    seeds = jax.random.split(jax.random.key(seed), 16)
    return {
        "hidden_in": noise(seeds[0], (TOKENS, D), 1.0, 6.0, ((0, 32),)),
        "segments": draw_segments(jax.random.fold_in(seeds[15], 71), 0),
        "routing": draw_routing(jax.random.fold_in(seeds[15], 71), 0),
        "first_gain": jnp.clip(1.0 + 0.1 * jax.random.normal(seeds[3], (D,), jnp.float32), 0.5, 1.5),
        "first_bias": noise(seeds[4], (D,), 0.1, 0.5, ((0, 32),), jnp.float32),
        "second_gain": jnp.clip(1.0 + 0.1 * jax.random.normal(seeds[5], (D,), jnp.float32), 0.5, 1.5),
        "second_bias": noise(seeds[6], (D,), 0.1, 0.5, ((0, 32),), jnp.float32),
        "w_query": noise(seeds[7], (D, D), D ** -0.5, 0.21875, ((0, 32),), jnp.float32),
        "w_key": noise(seeds[8], (D, D), D ** -0.5, 0.21875, ((0, 32),), jnp.float32),
        "w_value": noise(seeds[9], (D, D), D ** -0.5, 0.21875, ((0, 32),), jnp.float32),
        "w_out": noise(seeds[10], (D, D), (D // 16) ** -0.5, 0.875, ((0, 32),), jnp.float32),
        "w_router": noise(seeds[11], (D, EXPERTS), (2 * D) ** -0.5, 0.15625, ((0, 32),), jnp.float32),
        "w_in": noise(seeds[12], (EXPERTS, D, FF), D ** -0.5, 0.21875, ((0, 8), (2, 4)), jnp.float32),
        "w_back": noise(seeds[13], (EXPERTS, FF, D), FF ** -0.5, 0.109375, ((0, 8), (1, 4)), jnp.float32),
        "cotangent": noise(seeds[14], (TOKENS, D), 1.0, 6.0, ((0, 32),)),
    }


EPSILON = 1e-05
FLOOR_SCORE = -1e+30
SCALE_FACTOR = 0.125
BALANCE_WEIGHT = 0.01

@jax.custom_vjp
def low(v):
    return lax.optimization_barrier(v.astype(jnp.bfloat16)).astype(jnp.float32)

@jax.custom_vjp
def low_back(v):
    return v

def low_keep(v):
    return (low(v), None)

def low_pass(kept, grad):
    return (grad,)

def back_keep(v):
    return (v, None)

def back_low(kept, grad):
    return (low(grad),)
low.defvjp(low_keep, low_pass)
low_back.defvjp(back_keep, back_low)

def matmul(left, right):
    return jnp.dot(left, right, preferred_element_type=jnp.float32, precision=lax.Precision.HIGHEST)

def layer_norm(values, norm_gain, norm_shift):
    centered = values - lax.optimization_barrier(jnp.mean(values, axis=1, keepdims=True))
    inverse = lax.rsqrt(lax.optimization_barrier(jnp.mean(centered * centered, axis=1, keepdims=True)) + EPSILON)
    return centered * inverse * norm_gain + norm_shift

def group_attention(operands):
    queries, keys, values, seg_ids = operands
    scores = low_back(SCALE_FACTOR * jnp.einsum('qhd,khd->hqk', queries, keys, precision=lax.Precision.HIGHEST))
    places = jnp.arange(seg_ids.shape[0], dtype=jnp.int32)
    allowed = (seg_ids[None, :] == seg_ids[:, None]) & (places[None, :] <= places[:, None])
    scores = jnp.where(allowed[None], scores, FLOOR_SCORE)
    prob_low = low(jax.nn.softmax(scores, axis=2))
    return jnp.einsum('hqk,khd->qhd', prob_low, values, precision=lax.Precision.HIGHEST)

def expert_apply(operands):
    rows, first_w, second_w = operands
    pre_act = low_back(matmul(rows, first_w))
    activ = low(jax.nn.gelu(pre_act, approximate=False))
    return matmul(activ, second_w)

def reference(hidden_in, segments, routing, first_gain, first_bias, second_gain, second_bias, w_query, w_key, w_value, w_out, w_router, w_in, w_back, cotangent):
    total_rows = TOKENS
    device_count = N_WIDE * N_NARROW
    chosen = routing[:, 0].astype(jnp.int32)
    hot_int = (routing == jnp.arange(EXPERTS, dtype=jnp.int32)[None, :]).astype(jnp.int32)
    running = jnp.cumsum(hot_int.reshape(device_count, TOK_DEV, EXPERTS), axis=1).reshape(total_rows, EXPERTS) - hot_int
    slots = lax.optimization_barrier(jnp.sum(running * hot_int, axis=1)).astype(jnp.int32)
    source = (jnp.arange(total_rows, dtype=jnp.int32) // TOK_DEV).astype(jnp.int32)
    placed = ((chosen * device_count + source) * CAP + slots).astype(jnp.int32)
    hot = hot_int.astype(jnp.float32)
    counts = lax.optimization_barrier(jnp.sum(hot, axis=0))
    deviation = (counts - total_rows / EXPERTS) * (EXPERTS / total_rows)
    head_shape = (N_WIDE, GROUP, HEADS, HEAD_DIM)

    def forward(inputs, gain_a, bias_a, gain_b, bias_b, query_w, key_w, value_w, out_w, router_w, in_w, back_w):
        gain_a = low(gain_a)
        bias_a = low(bias_a)
        gain_b = low(gain_b)
        bias_b = low(bias_b)
        query_w = low(query_w)
        key_w = low(key_w)
        value_w = low(value_w)
        out_w = low(out_w)
        router_w = low(router_w)
        in_w = low(in_w)
        back_w = low(back_w)
        normed = low(layer_norm(inputs, gain_a, bias_a))
        queries = low_back(low(matmul(normed, query_w)))
        keys = low_back(low(matmul(normed, key_w)))
        values = low_back(low(matmul(normed, value_w)))
        attended = lax.map(jax.checkpoint(group_attention), (queries.reshape(head_shape), keys.reshape(head_shape), values.reshape(head_shape), segments.reshape(N_WIDE, GROUP)))
        attended = low_back(low(attended.reshape(total_rows, D)))
        mixed = inputs + low_back(matmul(attended, out_w))
        second = low(layer_norm(mixed, gain_b, bias_b))
        logits = low_back(matmul(second, router_w))
        gates = jax.nn.sigmoid(lax.optimization_barrier(jnp.sum(logits * hot, axis=1)))
        gate_sums = lax.optimization_barrier(jnp.sum(hot * gates[:, None], axis=0))
        balance = EXPERTS / total_rows * jnp.sum(deviation * gate_sums)
        buffer = jnp.zeros((EXPERTS * device_count * CAP, D), jnp.float32).at[placed].set(second)
        results = lax.map(jax.checkpoint(expert_apply), (buffer.reshape(EXPERTS, device_count * CAP, D), in_w, back_w))
        expert_out = low_back(results.reshape(EXPERTS * device_count * CAP, D)[placed])
        return (mixed + gates[:, None] * expert_out, balance)
    (block_out, balance), pullback = jax.vjp(forward, hidden_in.astype(jnp.float32), first_gain.astype(jnp.float32), first_bias.astype(jnp.float32), second_gain.astype(jnp.float32), second_bias.astype(jnp.float32), w_query.astype(jnp.float32), w_key.astype(jnp.float32), w_value.astype(jnp.float32), w_out.astype(jnp.float32), w_router.astype(jnp.float32), w_in.astype(jnp.float32), w_back.astype(jnp.float32))
    gradients = pullback((cotangent.astype(jnp.float32), jnp.ones_like(balance) * BALANCE_WEIGHT))
    return (block_out, balance, gradients[0], gradients[1], gradients[2], gradients[3], gradients[4], gradients[5], gradients[6], gradients[7], gradients[8], gradients[9], gradients[10], gradients[11])
```

```python
import jax
import jax.numpy as jnp
from jax import lax
from jax.experimental import pallas as pl
from jax.experimental.pallas import tpu as pltpu
from jax.sharding import PartitionSpec as P

HEADS = 12
HEAD_DIM = 64
EPSILON = 1e-05
FLOOR_SCORE = -1e30
SCALE_FACTOR = 0.125
BALANCE_WEIGHT = 0.01
BOTH = ("wide", "narrow")
BF = jnp.bfloat16
F32 = jnp.float32


def dot(left, right):
    return jnp.dot(left, right, preferred_element_type=F32)


def dot_nt(left, right):
    return lax.dot_general(left, right, (((1,), (1,)), ((), ())), preferred_element_type=F32)


def dot_tn(left, right):
    return lax.dot_general(left, right, (((0,), (0,)), ((), ())), preferred_element_type=F32)


def norm_parts(values):
    centered = values - jnp.mean(values, axis=1, keepdims=True)
    inverse = lax.rsqrt(jnp.mean(centered * centered, axis=1, keepdims=True) + EPSILON)
    return centered * inverse, inverse


def norm_back(incoming, unit, inverse, gain):
    scaled = incoming * gain
    return inverse * (
        scaled
        - jnp.mean(scaled, axis=1, keepdims=True)
        - unit * jnp.mean(scaled * unit, axis=1, keepdims=True)
    )


def to_all(values, axes):
    return lax.all_to_all(values, axes, split_axis=0, concat_axis=0, tiled=True)


SMALL = pl.CostEstimate(flops=1000, bytes_accessed=1000, transcendentals=0)
LARGE = pl.CostEstimate(flops=int(2.5e10), bytes_accessed=int(3e7), transcendentals=0)
FILLERS = ("place_cotangent", "cast_weights")


class Held:
    def __init__(self, ref, copy, fetched):
        self.ref, self.copy, self.waiting = ref, copy, fetched

    def get(self):
        if self.waiting:
            self.copy.wait()
            self.waiting = False
        return self.ref

    def push(self):
        self.copy.start()
        self.waiting = True

    @property
    def shape(self):
        return self.ref.shape

    @property
    def dtype(self):
        return self.ref.dtype

    def __getitem__(self, at):
        return self.get()[at]

    def __setitem__(self, at, value):
        self.ref[at] = value


def run(body, outs, ins, name, scratch=(), limit=16, first_smem=False):
    outs = list(outs)
    lead = 1 if first_smem else 0
    moved = list(ins[lead:]) + outs
    buffers = [pltpu.VMEM(value.shape, value.dtype) for value in moved]
    count, fetched = len(moved), len(ins) - lead

    def kernel(*refs):
        smem_refs, arrays = refs[:lead], refs[lead : lead + count]
        own, semaphores = refs[lead + count : lead + 2 * count], refs[lead + 2 * count]
        held = []
        for i in range(count):
            source, target = (arrays[i], own[i]) if i < fetched else (own[i], arrays[i])
            copy = pltpu.make_async_copy(source, target, semaphores.at[i])
            if i < fetched:
                copy.start()
            held.append(Held(own[i], copy, i < fetched))
        body(*smem_refs, *held, *refs[lead + 2 * count + 1 :])
        for item in held[fetched:]:
            if not item.waiting:
                item.push()
        for item in held:
            item.get()

    hbm = pl.BlockSpec(memory_space=pltpu.HBM)
    return pl.pallas_call(
        kernel,
        out_shape=outs,
        in_specs=([smem()] if first_smem else []) + [hbm] * fetched,
        out_specs=[hbm] * len(outs),
        scratch_shapes=[*buffers, pltpu.SemaphoreType.DMA((count,)), *scratch],
        compiler_params=pltpu.CompilerParams(vmem_limit_bytes=60 * 1024 * 1024),
        cost_estimate=LARGE if name in FILLERS else SMALL,
        name=name,
    )(*ins)


def near(body, outs, ins, name, far):
    count = len(ins)
    buffers = [pltpu.VMEM(outs[i].shape, outs[i].dtype) for i in far]

    def kernel(*refs):
        results = list(refs[count : count + len(outs)])
        held = []
        for slot, i in enumerate(far):
            own = refs[count + len(outs) + slot]
            copy = pltpu.make_async_copy(own, results[i], refs[-1].at[slot])
            results[i] = Held(own, copy, False)
            held.append(results[i])
        body(*refs[:count], *results)
        for item in held:
            if not item.waiting:
                item.push()
        for item in held:
            item.get()

    spec = {True: pl.BlockSpec(memory_space=pltpu.HBM), False: pl.BlockSpec(memory_space=pltpu.VMEM)}
    return pl.pallas_call(
        kernel,
        out_shape=outs,
        in_specs=[spec[False] for _ in ins],
        out_specs=[spec[i in far] for i in range(len(outs))],
        scratch_shapes=[*buffers, pltpu.SemaphoreType.DMA((len(far),))],
        compiler_params=pltpu.CompilerParams(vmem_limit_bytes=20 * 1024 * 1024),
        cost_estimate=SMALL,
        name=name,
    )(*ins)


def shape(dims, dtype):
    return jax.ShapeDtypeStruct(dims, dtype)


def smem():
    return pl.BlockSpec(memory_space=pltpu.SMEM)


def earlier_keys(size):
    key = lax.broadcasted_iota(jnp.int32, (size, size), 0)
    query = lax.broadcasted_iota(jnp.int32, (size, size), 1)
    return key <= query


def attention_kernel(
    narrow, own_heads, piece, side_block, side_at, experts,
    where_ref, x_refs, weights_ref,
    first_ref, q_ref, k_ref, v_ref, att_ref, lse_ref, rows_ref, stat_ref, side_ref,
):
    rows, width = x_refs[0].shape
    at_wide, at_narrow = where_ref[0], where_ref[1]
    side = weights_ref[:, side_block * 128 : side_block * 128 + 128]
    side_ref[...] = side
    lane = lax.broadcasted_iota(jnp.int32, (8, 128), 1)
    which = lax.broadcasted_iota(jnp.int32, (8, 128), 0)
    wanted = jnp.where(which < 4, side_at + which, side_at + 4 + at_wide)
    pick = jnp.where(lane == wanted, 1.0, 0.0)
    vectors = dot_nt(pick, side.astype(F32))
    rows_ref[...] = vectors
    stat_rows = stat_ref.shape[0]
    column = lax.broadcasted_iota(jnp.int32, (stat_rows, width), 1)
    which = lax.broadcasted_iota(jnp.int32, (stat_rows, width), 0)
    segment_row = (at_wide * narrow + which) * piece
    wanted = jnp.where(which < narrow, segment_row, column - lax.rem(column, piece))
    stat = dot(jnp.where(column == wanted, 1.0, 0.0), side.astype(F32))
    stat_ref[...] = stat
    seg_lane = side_at + 4 + 2 * experts
    segs = [stat[i : i + 1, seg_lane : seg_lane + 1] for i in range(narrow)]
    gain, bias = vectors[0:1], vectors[1:2]
    for place in range(narrow):
        unit, _ = norm_parts(x_refs[place][...].astype(F32))
        first_ref[at_narrow ^ place] = (unit * gain + bias).astype(BF)
    first_ref.push()
    own_width = own_heads * HEAD_DIM
    for block in range(narrow):
        at = pl.ds(block * rows, rows)
        qkv = dot(first_ref.ref[block], weights_ref[...])
        for head in range(own_heads):
            low, high = head * HEAD_DIM, (head + 1) * HEAD_DIM
            q_ref[head, at] = (qkv[:, low:high].astype(BF).astype(F32) * SCALE_FACTOR).astype(BF)
            k_ref[head, at] = qkv[:, own_width + low : own_width + high].astype(BF)
            v_ref[head, at] = qkv[:, 2 * own_width + low : 2 * own_width + high].astype(BF)
    for ref in (q_ref, k_ref, v_ref):
        ref.push()
    mask = earlier_keys(rows)
    for head in range(own_heads):
        for block in range(narrow):
            at = pl.ds(block * rows, rows)
            query = q_ref.ref[head, at]
            scores = []
            for other in range(block + 1):
                score = dot_nt(k_ref.ref[head, pl.ds(other * rows, rows)], query)
                if other == block:
                    score = jnp.where(mask, score, FLOOR_SCORE)
                else:
                    score = score + jnp.where(segs[block] == segs[other], 0.0, FLOOR_SCORE)
                scores.append(score)
            top = scores[0].max(axis=0, keepdims=True)
            for score in scores[1:]:
                top = jnp.maximum(top, score.max(axis=0, keepdims=True))
            exps = [jnp.exp(score - top) for score in scores]
            total = exps[0].sum(axis=0, keepdims=True)
            for value in exps[1:]:
                total = total + value.sum(axis=0, keepdims=True)
            share = 1.0 / total
            att = None
            for other, value in enumerate(exps):
                term = dot_tn((value * share).astype(BF), v_ref.ref[head, pl.ds(other * rows, rows)])
                att = term if att is None else att + term
            att_ref[at, head * HEAD_DIM : (head + 1) * HEAD_DIM] = att.astype(BF)
            lse_ref[head, :, at] = top + jnp.log(total)


def project(where, att, out_w, narrow):
    rows, width = att.shape[0] // narrow, out_w.shape[1]

    def body(where_ref, att_ref, out_w_ref, *parts):
        for place in reversed(range(narrow)):
            at = pl.ds(pl.multiple_of((where_ref[1] ^ place) * rows, rows), rows)
            parts[place][...] = dot(att_ref[at], out_w_ref[...]).astype(parts[place].dtype)
            parts[place].push()

    outs = [shape((rows, width), BF if i & 1 else F32) for i in range(narrow)]
    return run(body, outs, [where, att, out_w], "project", first_smem=True)


def attention(where, x_blocks, weights, own_heads, piece, side_block, side_at, experts):
    narrow = len(x_blocks)
    rows, width = x_blocks[0].shape
    group = rows * narrow
    stat_rows = -(-(narrow + 1) // 8) * 8
    head_shape = jax.ShapeDtypeStruct((own_heads, group, HEAD_DIM), BF)
    outs = (
        [jax.ShapeDtypeStruct((narrow, rows, width), BF)]
        + [head_shape] * 3
        + [shape((group, own_heads * HEAD_DIM), BF)]
        + [jax.ShapeDtypeStruct((own_heads, 1, group), F32)]
        + [shape((8, width), F32), shape((stat_rows, 128), F32), shape((width, 128), BF)]
    )

    def body(where_ref, *refs):
        attention_kernel(
            narrow, own_heads, piece, side_block, side_at, experts,
            where_ref, refs[:narrow], *refs[narrow:],
        )

    return run(body, outs, [where, *x_blocks, weights], "attention_forward", first_smem=True)


def gelu_pieces(z):
    size = jnp.abs(z)
    fall = jnp.exp(z * z * -0.5)
    t = 1.0 / (1.0 + size * (0.3275911 * 0.7071067811865476))
    tail = 1.061405429 * 0.5
    for term in (-1.453152027, 1.421413741, -0.284496736, 0.254829592):
        tail = tail * t + term * 0.5
    tail = tail * t * fall
    upper = jnp.where(z < 0.0, tail, 1.0 - tail)
    return upper, z * fall * 0.3989422804014327


def expert_share(x, dy, w_in, w_back, act_ref, dz_ref, at):
    z = dot(x, w_in[...])
    upper, bump = gelu_pieces(z)
    act = (z * upper).astype(BF)
    act_ref[at] = act
    du = dot_nt(dy, w_back[...])
    dz = (du * (upper + bump)).astype(BF)
    dz_ref[at] = dz
    return dot_nt(dz, w_in[...]), jnp.sum(act.astype(F32) * du, axis=1, keepdims=True)


def row_gate(x, vectors):
    score = jnp.sum(x.astype(F32) * vectors[4:5], axis=1, keepdims=True)
    return 1.0 / (1.0 + jnp.exp(-score))


STEP = 256


def expert_first(x, g, vectors, w_in, w_back):
    count, width = x.shape
    hidden = w_in.shape[1]

    def body(x_ref, g_ref, vec, w1, w2, dx, score, dy_ref, act, dz):
        for start in range(0, count, STEP):
            at = pl.ds(start, min(STEP, count))
            rows = x_ref[at]
            dy = (row_gate(rows, vec) * g_ref[at].astype(F32)).astype(BF)
            dy_ref[at] = dy
            dx[at], score[at] = expert_share(rows, dy, w1, w2, act, dz, at)

    outs = [shape((count, width), F32), shape((count, 1), F32), shape((count, width), BF)]
    outs += [shape((count, hidden), BF)] * 2
    return near(body, outs, [x, g, vectors, w_in, w_back], "expert_first", (3, 4))


def expert_rest(info, x, dy, vectors, dx, score, ins, backs, dx_type):
    count, width = x.shape
    shares = len(ins)

    def body(info_ref, x_ref, dy_ref, vec, dx_ref, score_ref, *refs):
        w1, w2, o = refs[:shares], refs[shares : 2 * shares], refs[2 * shares :]
        total = jnp.zeros((1, width), F32)
        for start in range(0, count, STEP):
            at = pl.ds(start, min(STEP, count))
            rows, dy_rows = x_ref[at], dy_ref[at]
            o[2][at] = dy_rows
            dx, score = dx_ref[at], score_ref[at]
            for i in range(shares):
                more, part = expert_share(
                    rows, dy_rows, w1[i], w2[i], o[3 + i], o[3 + shares + i], at
                )
                dx, score = dx + more, score + part
            gate = row_gate(rows, vec)
            dlogit = (score + info_ref[0:1, 1:2] * gate) * (1.0 - gate)
            total = total + jnp.sum(rows.astype(F32) * dlogit, axis=0, keepdims=True)
            o[0][at] = (dx + dlogit * vec[4:5]).astype(dx_type)
        o[1][...] = total

    outs = [shape((count, width), dx_type), shape((1, width), F32), shape((count, width), BF)]
    outs += [shape((count, value.shape[1]), BF) for value in ins] * 2
    far = tuple(range(1, len(outs)))
    res = near(body, outs, [info, x, dy, vectors, dx, score, *ins, *backs], "expert_rest", far)
    return res[0], res[1], res[2], list(res[3 : 3 + shares]), list(res[3 + shares :])


def partner_terms(acts_s, acts_o, dy_s, dy_o):
    count = len(acts_s)

    def body(dy_s, dy_o, *refs):
        for i in range(count):
            out = refs[2 * count + i]
            out[...] = (dot_tn(refs[i][...], dy_s[...]) + dot_tn(refs[count + i][...], dy_o[...])).astype(BF)
            out.push()

    outs = [shape((a.shape[1], dy_s.shape[1]), BF) for a in acts_s]
    return list(run(body, outs, [dy_s, dy_o, *acts_s, *acts_o], "partner_terms"))


def expert_grads(x_s, x_o, dy_s, dy_o, acts_s, acts_o, dzs_s, dzs_o, backs):
    count = len(acts_s)
    rows, width = x_s.shape

    def body(*refs):
        groups = [refs[i * count : (i + 1) * count] for i in range(5)]
        act_s, act_o, back, dz_s, dz_o = groups
        xs, xo, ds, do = refs[5 * count : 5 * count + 4]
        y_o, y_s, own, *terms = refs[5 * count + 4 :]
        for out, act in ((y_o, act_o), (y_s, act_s)):
            total = dot(act[0][...], back[0][...])
            for i in range(1, count):
                total = total + dot(act[i][...], back[i][...])
            out[...] = total.astype(out.dtype)
            out.push()
        for i in reversed(range(count)):
            term = dot_tn(xs[...], dz_s[i][...]) + dot_tn(xo[...], dz_o[i][...])
            terms[i][...] = term.astype(terms[i].dtype)
            terms[i].push()
        own[...] = dot_tn(act_s[0][...], ds[...]) + dot_tn(act_o[0][...], do[...])

    outs = [shape((rows, width), BF), shape((rows, width), F32), shape(backs[0].shape, F32)]
    outs += [shape((width, a.shape[1]), BF if i else F32) for i, a in enumerate(acts_s)]
    ins = [*acts_s, *acts_o, *backs, *dzs_s, *dzs_o, x_s, x_o, dy_s, dy_o]
    res = run(body, outs, ins, "expert_grads")
    return res[0], res[1], res[2], list(res[3:])


def attention_back_kernel(
    narrow, own_heads, columns, seg_lane,
    where_ref, dr_refs, out_w_ref, q_ref, k_ref, v_ref, lse_ref, stat_ref, att_ref,
    dqkv_ref, out_terms_ref,
    dr_all, da, dk_acc, dv_acc,
):
    rows, width = dr_refs[0].shape
    group = rows * narrow
    own_width = own_heads * HEAD_DIM
    at_narrow = where_ref[1]
    for place in range(narrow):
        dr_all[at_narrow ^ place] = dr_refs[place][...]
    dqkv = dqkv_ref.ref
    segs = [stat_ref[i : i + 1, seg_lane : seg_lane + 1] for i in range(narrow)]
    mask = earlier_keys(rows)
    dqkv[:, columns - 128 :] = jnp.zeros((group, 128), BF)
    for block in range(narrow):
        at = pl.ds(block * rows, rows)
        d_att = dot_nt(dr_all[block], out_w_ref[...]).astype(BF)
        for head in range(own_heads):
            da[head, at] = d_att[:, head * HEAD_DIM : (head + 1) * HEAD_DIM]
    for head in range(own_heads):
        low, high = head * HEAD_DIM, (head + 1) * HEAD_DIM
        for block in reversed(range(narrow)):
            at = pl.ds(block * rows, rows)
            query, d_att, lse = q_ref[head, at], da[head, at], lse_ref[head, :, at]
            probs, d_probs, delta = [], [], None
            for other in range(block + 1):
                keys = pl.ds(other * rows, rows)
                score = dot_nt(k_ref[head, keys], query)
                if other == block:
                    prob = jnp.where(mask, jnp.exp(score - lse), 0.0)
                else:
                    prob = jnp.exp(
                        score - (lse + jnp.where(segs[block] == segs[other], 0.0, -FLOOR_SCORE))
                    )
                d_prob = dot_nt(v_ref[head, keys], d_att)
                part = jnp.sum(prob * d_prob, axis=0, keepdims=True)
                delta = part if delta is None else delta + part
                probs.append(prob)
                d_probs.append(d_prob)
            dq = None
            for other in range(block + 1):
                keys = pl.ds(other * rows, rows)
                d_score = (probs[other] * (d_probs[other] - delta)).astype(BF)
                term = dot_tn(d_score, k_ref[head, keys])
                dq = term if dq is None else dq + term
                dk = dot(d_score, query)
                dv = dot(probs[other].astype(BF), d_att)
                if block == narrow - 1:
                    dk_acc[keys] = dk
                    dv_acc[keys] = dv
                else:
                    dk_acc[keys] += dk
                    dv_acc[keys] += dv
            dqkv[at, low:high] = (dq * SCALE_FACTOR).astype(BF)
        dqkv[:, own_width + low : own_width + high] = dk_acc[...].astype(BF)
        dqkv[:, 2 * own_width + low : 2 * own_width + high] = dv_acc[...].astype(BF)
    dqkv_ref.push()
    out_terms_ref[...] = dot_tn(att_ref[...], dr_all[...].reshape(group, width)).astype(BF)


def attention_back(where, dr_blocks, out_w, q, k, v, lse, stat, att, columns, seg_lane):
    narrow = len(dr_blocks)
    rows, width = dr_blocks[0].shape
    group = rows * narrow
    own_heads = q.shape[0]
    outs = [shape((group, columns), BF), shape((own_heads * HEAD_DIM, width), BF)]

    def body(where_ref, *refs):
        attention_back_kernel(
            narrow, own_heads, columns, seg_lane, where_ref, refs[:narrow], *refs[narrow:]
        )

    scratch = [
        pltpu.VMEM((narrow, rows, width), BF),
        pltpu.VMEM((own_heads, group, HEAD_DIM), BF),
        pltpu.VMEM((group, HEAD_DIM), F32),
        pltpu.VMEM((group, HEAD_DIM), F32),
    ]
    ins = [where, *dr_blocks, out_w, q, k, v, lse, stat, att]
    return run(body, outs, ins, "attention_backward", scratch, first_smem=True)


def weight_terms(where, dqkv, first, weights, info, sums, routers, narrow, side_block, side_at):
    group, columns = dqkv.shape
    width = weights.shape[0]
    rows = group // narrow

    def body(where_ref, dqkv_ref, first_ref, weights_ref, info_ref, sums_ref, router_a, router_b,
             terms_ref, *parts):
        first = first_ref[...].reshape(group, width)
        side = weights_ref[:, side_block * 128 : side_block * 128 + 128].astype(F32)
        gain, bias = side[:, side_at : side_at + 1], side[:, side_at + 1 : side_at + 2]
        gain_sum, bias_sum, last = None, None, None
        for block in range(columns // 128):
            cut = slice(block * 128, block * 128 + 128)
            term = dot_tn(first, dqkv_ref[:, cut])
            weight = weights_ref[:, cut].astype(F32)
            total = jnp.sum(dqkv_ref[:, cut].astype(F32), axis=0, keepdims=True)
            gain_part, bias_part = weight * (term - bias * total), weight * total
            gain_sum = gain_part if gain_sum is None else gain_sum + gain_part
            bias_sum = bias_part if bias_sum is None else bias_sum + bias_part
            if block == side_block:
                last = term
            else:
                terms_ref[:, cut] = term.astype(BF)
        gain_sum = jnp.sum(gain_sum, axis=1, keepdims=True) / gain
        bias_sum = jnp.sum(bias_sum, axis=1, keepdims=True)
        which = lax.broadcasted_iota(jnp.int32, (8, width), 0)
        extra = jnp.where(which == 4, router_a[...] + router_b[...], sums_ref[...])
        balance = info_ref[0:1, 0:1]
        high = balance.astype(BF).astype(F32)
        extra = jnp.where(which == 5, high, jnp.where(which == 6, balance - high, extra))
        lane = lax.broadcasted_iota(jnp.int32, (8, 128), 1)
        which = lax.broadcasted_iota(jnp.int32, (8, 128), 0)
        spread = jnp.where(lane == side_at + which, 1.0, 0.0)
        lane = lax.broadcasted_iota(jnp.int32, (width, 128), 1)
        last = jnp.where(lane == side_at, gain_sum, jnp.where(lane == side_at + 1, bias_sum, last))
        last = last + dot_tn(extra, spread)
        terms_ref[:, side_block * 128 : side_block * 128 + 128] = last.astype(BF)
        terms_ref.push()
        for place in reversed(range(narrow)):
            at = pl.ds(pl.multiple_of((where_ref[1] ^ place) * rows, rows), rows)
            parts[place][...] = dot_nt(dqkv_ref[at], weights_ref[...]).astype(parts[place].dtype)
            parts[place].push()

    outs = [shape((width, columns), BF)]
    outs += [shape((rows, width), BF if i & 1 else F32) for i in range(narrow)]
    ins = [where, dqkv, first, weights, info, sums, *routers]
    res = run(body, outs, ins, "weight_terms", first_smem=True)
    return res[0], list(res[1:])


def turned(row):
    count = row.shape[1]
    at = lax.broadcasted_iota(jnp.int32, (count, count), 0)
    other = lax.broadcasted_iota(jnp.int32, (count, count), 1)
    return jnp.sum(jnp.where(at == other, row, 0.0), axis=1, keepdims=True)


def pack(weights, vectors, w_router, routing, segments, wide, narrow, own_width, columns):
    piece, width = weights[0].shape
    experts = w_router.shape[1]
    rows = routing.shape[0]
    start = 3 * own_width

    def body(wq, wk, wv, va, vb, vc, vd, wr, route, segment, sent, held):
        held[...] = jnp.zeros_like(held)
        ids = lax.broadcasted_iota(jnp.int32, (experts, rows), 0)
        counts = jnp.sum(jnp.where(route[...] == ids, 1.0, 0.0), axis=1, keepdims=True)
        sides = [turned(ref[...]) for ref in (va, vb, vc, vd)]
        sides += [turned(wr[i : i + 1]) for i in range(experts)]
        sides += [counts[i : i + 1] for i in range(experts)]
        sides += [segment[0:1, 0:1].astype(F32)]
        lane = lax.broadcasted_iota(jnp.int32, (piece, 128), 1)
        block = jnp.zeros((piece, 128), F32)
        for i, value in enumerate(sides):
            block = jnp.where(lane == start % 128 + i, value, block)
        for n in range(narrow):
            held[n, :, columns - 128 :] = block
            low, high = n * own_width, min((n + 1) * own_width, width)
            for i, ref in enumerate((wq, wk, wv)):
                if low < high:
                    held[n, :, i * own_width : i * own_width + high - low] = ref[:, low:high]

        def send(w, carry):
            for n in range(narrow):
                sent[w * narrow + n] = held[n].astype(BF)
            return carry

        lax.fori_loop(0, wide, send, 0)

    outs = [shape((wide * narrow, piece, columns), BF)]
    ins = [*weights, *[v.reshape(1, piece) for v in vectors], w_router.T]
    ins += [routing.reshape(1, rows), segments.reshape(1, rows)]
    return run(body, outs, ins, "pack", [pltpu.VMEM((narrow, piece, columns), F32)])[0]


def cast_weights(values, piece, copies):
    count = len(values)

    def body(*refs):
        ins, outs = refs[: count + 1], refs[count + 1 :]
        for i in range(copies):
            outs[count][i] = ins[count][...]
        outs[count].push()
        for i in range(count):
            outs[i][...] = ins[i][...].astype(BF)
            outs[i].push()

    outs = [shape(v.shape, BF) for v in values] + [shape((copies, *piece.shape), BF)]
    return run(body, outs, [*values, piece], "cast_weights")


def place_cotangent(routing, cotangent, experts, capacity):
    rows, width = cotangent.shape
    slots = experts * capacity

    def body(route, g, placing, moved):
        ids = lax.broadcasted_iota(jnp.int32, (rows, experts), 1)
        expert = turned(route[...].astype(F32)).astype(jnp.int32)
        hot = jnp.where(expert == ids, 1.0, 0.0)
        row = lax.broadcasted_iota(jnp.int32, (rows, rows), 0)
        column = lax.broadcasted_iota(jnp.int32, (rows, rows), 1)
        before = dot(jnp.where(row > column, 1.0, 0.0).astype(BF), hot.astype(BF))
        slot = jnp.sum(before * hot, axis=1, keepdims=True).astype(jnp.int32)
        target = expert * capacity + slot
        place = lax.broadcasted_iota(jnp.int32, (rows, slots), 1)
        spot = jnp.where(place == target, 1.0, 0.0).astype(BF)
        placing[...] = spot
        moved[...] = dot_tn(spot, g[...]).astype(BF)

    outs = [shape((rows, slots), BF), shape((slots, width), BF)]
    return run(body, outs, [routing.reshape(1, rows), cotangent], "place_cotangent")


def second_norm(x, halves, vectors, side, stat, placing, routing, where, dims):
    narrow, experts, total, side_at = dims
    rows, width = x.shape
    slots = placing.shape[1]
    count = len(halves)

    def body(where_ref, x_ref, *refs):
        vec, side_ref, stat_ref, placing_ref, route = refs[count : count + 5]
        mixed_ref, moved, gate_ref, info = refs[count + 5 :]
        mixed = x_ref[...].astype(F32)
        for ref in refs[:count]:
            mixed = mixed + ref[...].astype(F32)
        mixed_ref[...] = mixed
        unit, _ = norm_parts(mixed)
        low = (unit * vec[2:3] + vec[3:4]).astype(BF)
        moved[...] = dot_tn(placing_ref[...], low).astype(BF)
        logits = dot(low, side_ref[...])
        lane = lax.broadcasted_iota(jnp.int32, (rows, 128), 1)
        expert = turned(route[...].astype(F32)).astype(jnp.int32)
        chosen = jnp.where(lane - (side_at + 4) == expert, logits, 0.0)
        gate = 1.0 / (1.0 + jnp.exp(-jnp.sum(chosen, axis=1, keepdims=True)))
        gate_ref[...] = gate
        first = side_at + 4 + experts
        sums = jnp.sum(jnp.where(lane - first == expert, gate, 0.0), axis=0, keepdims=True)
        lane = lax.broadcasted_iota(jnp.int32, (1, 128), 1)
        counts = stat_ref[narrow : narrow + 1]
        deviation = (counts - float(total) / experts) * (experts / float(total))
        kept = (lane >= first) & (lane < first + experts)
        balance = experts / float(total) * jnp.sum(
            jnp.where(kept, deviation * sums, 0.0), axis=1, keepdims=True
        )
        own = jnp.sum(
            jnp.where(lane == first + where_ref[0], deviation, 0.0), axis=1, keepdims=True
        )
        core = jnp.where(where_ref[1] % 2 == 0, BALANCE_WEIGHT * (experts / float(total)), 0.0)
        info[...] = jnp.where(lane == 0, balance, own * core) + jnp.zeros((8, 128), F32)

    outs = [shape((rows, width), F32), shape((slots, width), BF), shape((rows, 1), F32)]
    outs.append(shape((8, 128), F32))
    ins = [where, x, *halves, vectors, side, stat, placing, routing.reshape(1, rows)]
    return run(body, outs, ins, "second_norm", first_smem=True)


def second_back(returned, placing, mixed, cotangent, vectors):
    rows, width = mixed.shape

    def body(ret, placing_ref, mixed_ref, g, vec, dr_ref, low_ref, sums):
        incoming = dot(placing_ref[...], ret[...])
        unit, inverse = norm_parts(mixed_ref[...])
        gain = jnp.sum(incoming * unit, axis=0, keepdims=True)
        bias = jnp.sum(incoming, axis=0, keepdims=True)
        dr = g[...].astype(F32) + norm_back(incoming, unit, inverse, vec[2:3])
        dr_ref[...] = dr
        low_ref[...] = dr.astype(BF)
        which = lax.broadcasted_iota(jnp.int32, (8, width), 0)
        sums[...] = jnp.where(which == 2, gain, jnp.where(which == 3, bias, 0.0))

    outs = [shape((rows, width), F32), shape((rows, width), BF), shape((8, width), F32)]
    return run(body, outs, [returned, placing, mixed, cotangent, vectors], "second_back")


def finish_rows(returned, placing, mixed, gates):
    def body(ret, placing_ref, mixed_ref, gate, out):
        out[...] = mixed_ref[...] + gate[...] * dot(placing_ref[...], ret[...])

    ins = [returned, placing, mixed, gates]
    return run(body, [shape(mixed.shape, F32)], ins, "finish_rows")[0]


def first_back(halves, x, dr, vectors):
    count = len(halves)

    def body(*refs):
        x_ref, dr_ref, vec, out = refs[count:]
        incoming = refs[0][...].astype(F32)
        for ref in refs[1:count]:
            incoming = incoming + ref[...].astype(F32)
        unit, inverse = norm_parts(x_ref[...].astype(F32))
        out[...] = dr_ref[...] + norm_back(incoming, unit, inverse, vec[0:1])

    return run(body, [shape(x.shape, F32)], [*halves, x, dr, vectors], "first_back")[0]


def unpack(came, wide, narrow, own_width, width, experts):
    piece, columns = came.shape[1:]
    start = 3 * own_width
    side_block, side_at = start // 128, start % 128

    def as_row(column):
        row = lax.broadcasted_iota(jnp.int32, (piece, piece), 0)
        other = lax.broadcasted_iota(jnp.int32, (piece, piece), 1)
        return jnp.sum(jnp.where(row == other, column, 0.0), axis=0, keepdims=True)

    def body(came_ref, gq, gk, gv, va, vb, vc, vd, gr, balance):
        every = jnp.zeros((piece, 128), F32)
        routers = []
        for n in range(narrow):
            total = jnp.zeros((piece, columns), F32)
            for w in range(wide):
                total = total + came_ref[w * narrow + n].astype(F32)
            every = every + total[:, side_block * 128 : side_block * 128 + 128]
            low, high = n * own_width, min((n + 1) * own_width, width)
            if low < high:
                for i, ref in enumerate((gq, gk, gv)):
                    ref[:, low:high] = total[:, i * own_width : i * own_width + high - low]
        for w in range(wide):
            column = jnp.zeros((piece, 1), F32)
            at = start + 4
            for n in range(narrow):
                column = column + came_ref[w * narrow + n, :, at : at + 1].astype(F32)
            gr[w : w + 1] = as_row(column)
        for i, ref in enumerate((va, vb, vc, vd)):
            ref[...] = as_row(every[:, side_at + i : side_at + i + 1])
        balance[...] = every[0:1, side_at + 5 : side_at + 6] + every[0:1, side_at + 6 : side_at + 7]

    outs = [shape((piece, width), F32)] * 3 + [shape((1, piece), F32)] * 4
    outs += [shape((experts, piece), F32), shape((1, 1), F32)]
    return run(body, outs, [came], "unpack")


def local(
    hidden_in,
    segments,
    routing,
    first_gain,
    first_bias,
    second_gain,
    second_bias,
    w_query,
    w_key,
    w_value,
    w_out,
    w_router,
    w_in,
    w_back,
    cotangent,
):
    wide = lax.axis_size("wide")
    narrow = lax.axis_size("narrow")
    devices = wide * narrow
    rows, width = hidden_in.shape
    piece = w_query.shape[0]
    experts = w_router.shape[1]
    capacity = max(2, 2 * rows // experts)
    total = rows * devices
    own_heads = -(-HEADS // narrow)
    own_width = own_heads * HEAD_DIM
    aligned = own_width * narrow == width and own_width == piece * wide
    at_wide = lax.axis_index("wide")
    at_narrow = lax.axis_index("narrow")
    where = jnp.stack([at_wide, at_narrow]).astype(jnp.int32)
    bits = [1 << level for level in range(narrow.bit_length() - 1)]
    core_bit, chip_bits = bits[:1], bits[1:]
    side_start = 3 * own_width
    side_block, side_at = side_start // 128, side_start % 128
    seg_lane = side_at + 4 + 2 * experts
    assert seg_lane < 128
    columns = side_block * 128 + 128
    gate = lax.optimization_barrier

    def swap(values, bit):
        return lax.ppermute(values, "narrow", [(i, i ^ bit) for i in range(narrow)])

    def gather_blocks(block, over):
        blocks = {0: block}
        for bit in reversed(over):
            for place in list(blocks):
                blocks[place ^ bit] = swap(blocks[place], bit)
        return blocks

    def reduce_blocks(blocks, over):
        blocks = dict(blocks)
        for bit in over:
            for place in sorted(blocks, reverse=True):
                if place & bit:
                    moved = swap(blocks.pop(place).astype(BF), bit).astype(F32)
                    blocks[place ^ bit] = blocks[place ^ bit] + moved
        return blocks

    def reduce_wide(values):
        for level in reversed(range(wide.bit_length() - 1)):
            bit = 1 << level
            half = values.shape[0] // 2
            upper = (at_wide & bit) != 0
            low, high = values[:half], values[half:]
            moved = jnp.where(upper, low, high).astype(BF)
            moved = lax.ppermute(moved, "wide", [(i, i ^ bit) for i in range(wide)])
            values = jnp.where(upper, high, low).astype(F32) + moved.astype(F32)
        return values

    def exchange(values):
        values = values.reshape(experts, capacity, width)
        return to_all(values, "wide").reshape(experts * capacity, width)

    sent = pack(
        [w_query, w_key, w_value], [first_gain, first_bias, second_gain, second_bias],
        w_router, routing, segments, wide, narrow, own_width, columns,
    )
    x_blocks = gather_blocks(hidden_in, chip_bits)
    out_low = w_out.astype(BF)
    if aligned:
        out_low = lax.ppermute(
            out_low, BOTH, [(n * wide + j, j * narrow + n) for n in range(narrow) for j in range(wide)]
        )
    far = {i: x_blocks[i] for i in x_blocks if i >= 2 and not i & 1}
    sent, out_low, far, where = gate((sent, out_low, far, where))
    x_blocks.update(far)
    weights = to_all(sent, BOTH).reshape(width, columns)
    for place in list(x_blocks):
        x_blocks[place ^ 1] = swap(x_blocks[place], 1)
    partners = [i for i in range(2, narrow, 2)]
    in_low, back_low, out_tiled = cast_weights([w_in[0], w_back[0]], out_low, wide)
    placing, g_moved = place_cotangent(routing, cotangent, experts, capacity)
    weights, in_low, back_low, g_moved, out_tiled = gate(
        (weights, in_low, back_low, g_moved, out_tiled)
    )
    in_came = [swap(in_low, i) for i in partners]
    if aligned:
        out_w = to_all(out_tiled, "wide").reshape(own_width, width)
    else:
        all_out = lax.all_gather(out_low, BOTH, axis=0, tiled=True)
        all_out = jnp.pad(all_out, ((0, own_width * narrow - width), (0, 0)))
        out_w = lax.dynamic_slice_in_dim(all_out, at_narrow * own_width, own_width, axis=0)

    x_list = [x_blocks[i] for i in range(narrow)]
    first, q, k, v, att, lse, vectors, stat, side = attention(
        where, x_list, weights, own_heads, piece, side_block, side_at, experts
    )
    att, g_moved = gate((att, g_moved))
    g_own = exchange(g_moved)
    parts = project(where, att, out_w, narrow)
    halves = reduce_blocks({i: parts[i] for i in range(narrow)}, core_bit)
    halves, in_came = gate((halves, in_came))
    halves = {i: swap(halves[i].astype(BF), i) if i else halves[i] for i in sorted(halves)}

    halves, g_own, back_low = gate((halves, g_own, back_low))
    back_came = [swap(back_low, i) for i in partners]
    mixed, x_moved, gates, info = second_norm(
        hidden_in, [halves[i] for i in sorted(halves)], vectors, side, stat, placing, routing,
        where, (narrow, experts, total, side_at),
    )
    g_other = swap(g_own, 1)
    x_own = exchange(x_moved)
    x_other = swap(x_own, 1)

    ins = [in_low, *in_came]
    backs = [back_low, *back_came]
    shares = range(len(ins))
    dx_o, score_o, dy_o, act_o, dz_o = expert_first(x_other, g_other, vectors, ins[0], backs[0])
    dx_s, score_s, dy_s, act_s, dz_s = expert_first(x_own, g_own, vectors, ins[0], backs[0])
    dx_o, router_o, dy_o, acts_o, dzs_o = expert_rest(
        info, x_other, dy_o, vectors, dx_o, score_o, ins[1:], backs[1:], BF
    )
    dx_s, router_s, dy_s, acts_s, dzs_s = expert_rest(
        info, x_own, dy_s, vectors, dx_s, score_s, ins[1:], backs[1:], F32
    )
    acts_o, acts_s, dzs_o, dzs_s = [act_o, *acts_o], [act_s, *acts_s], [dz_o, *dzs_o], [dz_s, *dzs_s]
    dx_sum = (dx_s + swap(dx_o, 1).astype(F32)).astype(BF)
    d_returned = exchange(dx_sum)
    acts_s, dx_sum = gate((acts_s, dx_sum))
    back_cut = partner_terms(acts_s[1:], acts_o[1:], dy_s, dy_o)
    back_came = [swap(back_cut[i], place) for i, place in enumerate(partners)]
    acts_o, back_cut = gate((acts_o, back_cut))
    y_o, y_s, back_part, in_part = expert_grads(
        x_own, x_other, dy_s, dy_o, acts_s, acts_o, dzs_s, dzs_o, backs
    )
    y_sum = (y_s + swap(y_o, 1).astype(F32)).astype(BF)
    d_mixed, d_mixed_low, sums = second_back(d_returned, placing, mixed, cotangent, vectors)
    d_mixed_low, back_came, y_sum, in_part = gate((d_mixed_low, back_came, y_sum, in_part))
    returned = exchange(y_sum)
    dr_blocks = gather_blocks(d_mixed_low, bits)
    dr_blocks, in_part = gate((dr_blocks, in_part))
    cut = in_part[0].shape[0] // 2
    in_first = [swap(in_part[1 + i][:cut], place) for i, place in enumerate(partners)]
    dr_list = [dr_blocks[i] for i in range(narrow)]

    d_qkv, terms_out = attention_back(
        where, dr_list, out_w, q, k, v, lse, stat, att, columns, seg_lane
    )
    d_qkv, in_first, in_part = gate((d_qkv, in_first, in_part))
    in_second = [swap(in_part[1 + i][cut:], place) for i, place in enumerate(partners)]
    terms, d_parts = weight_terms(
        where, d_qkv, first, weights, info, sums, [router_o, router_s], narrow, side_block, side_at
    )

    terms, returned, terms_out = gate((terms, returned, terms_out))
    terms = to_all(terms.reshape(devices, piece, columns), BOTH)
    if aligned:
        grad_out_w = lax.ppermute(
            reduce_wide(terms_out),
            BOTH,
            [(j * narrow + n, n * wide + j) for n in range(narrow) for j in range(wide)],
        )
    else:
        spread = jnp.zeros((own_width * narrow, width), F32)
        spread = lax.dynamic_update_slice_in_dim(
            spread, terms_out.astype(F32), at_narrow * own_width, axis=0
        )
        grad_out_w = lax.psum_scatter(spread[:width], BOTH, scatter_dimension=0, tiled=True)
    block_out = finish_rows(returned, placing, mixed, gates)
    d_halves = reduce_blocks({i: d_parts[i] for i in range(narrow)}, core_bit)
    d_halves = [swap(d_halves[i].astype(BF), i) if i else d_halves[i] for i in sorted(d_halves)]
    grad_hidden = first_back(d_halves, hidden_in, d_mixed, vectors)
    in_all = [jnp.concatenate(pair, axis=0) for pair in zip(in_first, in_second)]

    def gathered(own, came):
        for value in came:
            own = own + value.astype(F32)
        return own

    done = unpack(terms, wide, narrow, own_width, width, experts)
    return (
        block_out,
        done[8].reshape(()),
        grad_hidden,
        *[done[i].reshape(piece) for i in range(3, 7)],
        *done[:3],
        grad_out_w,
        done[7].T,
        gathered(in_part[0], in_all)[None],
        gathered(back_part, back_came)[None],
    )


def solution(mesh):
    rows = P(BOTH, None)
    vector = P(BOTH)
    placed = (rows, vector, rows) + (vector,) * 4 + (rows,) * 5
    expert_specs = (P("wide", None, "narrow"), P("wide", "narrow", None))
    return jax.shard_map(
        local,
        mesh=mesh,
        in_specs=placed + expert_specs + (rows,),
        out_specs=(rows, P(), rows) + (vector,) * 4 + (rows,) * 5 + expert_specs,
        check_vma=False,
    )
```

```python
import jax
import jax.numpy as jnp
from jax import lax
from jax.experimental import pallas as pl
from jax.experimental.pallas import tpu as pltpu
from jax.sharding import PartitionSpec as P

HEADS = 12
HEAD_DIM = 64
EPSILON = 1e-05
FLOOR_SCORE = -1e30
SCALE_FACTOR = 0.125
BALANCE_WEIGHT = 0.01
BOTH = ("wide", "narrow")
BF = jnp.bfloat16
F32 = jnp.float32


def dot(left, right):
    return jnp.dot(left, right, preferred_element_type=F32)


def dot_nt(left, right):
    return lax.dot_general(left, right, (((1,), (1,)), ((), ())), preferred_element_type=F32)


def dot_tn(left, right):
    return lax.dot_general(left, right, (((0,), (0,)), ((), ())), preferred_element_type=F32)


def norm_parts(values):
    centered = values - jnp.mean(values, axis=1, keepdims=True)
    inverse = lax.rsqrt(jnp.mean(centered * centered, axis=1, keepdims=True) + EPSILON)
    return centered * inverse, inverse


def norm_back(incoming, unit, inverse, gain):
    scaled = incoming * gain
    return inverse * (
        scaled
        - jnp.mean(scaled, axis=1, keepdims=True)
        - unit * jnp.mean(scaled * unit, axis=1, keepdims=True)
    )


def to_all(values, axes):
    return lax.all_to_all(values, axes, split_axis=0, concat_axis=0, tiled=True)


SMALL = pl.CostEstimate(flops=1000, bytes_accessed=1000, transcendentals=0)
LARGE = pl.CostEstimate(flops=int(2.5e10), bytes_accessed=int(3e7), transcendentals=0)
FILLERS = ("place_cotangent", "cast_weights", "own_terms")


class Held:
    def __init__(self, ref, copies, fetched):
        self.ref, self.copies = ref, copies
        self.waiting = list(range(len(copies))) if fetched else []
        self.started = set(self.waiting)

    def get(self):
        for i in self.waiting:
            self.copies[i].wait()
        self.waiting = []
        return self.ref

    def push(self, part=None):
        for i in range(len(self.copies)) if part is None else [part]:
            if i not in self.started and i < len(self.copies):
                self.copies[i].start()
                self.waiting.append(i)
                self.started.add(i)

    @property
    def shape(self):
        return self.ref.shape

    @property
    def dtype(self):
        return self.ref.dtype

    def __getitem__(self, at):
        return self.get()[at]

    def __setitem__(self, at, value):
        self.ref[at] = value


def run(body, outs, ins, name, scratch=(), first_smem=False, pieces=None):
    outs = list(outs)
    lead = 1 if first_smem else 0
    moved = list(ins[lead:]) + outs
    buffers = [pltpu.VMEM(value.shape, value.dtype) for value in moved]
    count, fetched = len(moved), len(ins) - lead
    cuts = [(pieces or {}).get(i - fetched, [()]) for i in range(count)]
    first = [sum(len(cut) for cut in cuts[:i]) for i in range(count + 1)]

    def kernel(*refs):
        smem_refs, arrays = refs[:lead], refs[lead : lead + count]
        own, semaphores = refs[lead + count : lead + 2 * count], refs[lead + 2 * count]
        held = []
        for i in range(count):
            source, target = (arrays[i], own[i]) if i < fetched else (own[i], arrays[i])
            copies = []
            for j, at in enumerate(cuts[i]):
                ends = (source.at[at], target.at[at]) if at else (source, target)
                copies.append(pltpu.make_async_copy(*ends, semaphores.at[first[i] + j]))
            if i < fetched:
                copies[0].start()
            held.append(Held(own[i], copies, i < fetched))
        body(*smem_refs, *held, *refs[lead + 2 * count + 1 :])
        for item in held[fetched:]:
            item.push()
        for item in held:
            item.get()

    hbm = pl.BlockSpec(memory_space=pltpu.HBM)
    return pl.pallas_call(
        kernel,
        out_shape=outs,
        in_specs=([smem()] if first_smem else []) + [hbm] * fetched,
        out_specs=[hbm] * len(outs),
        scratch_shapes=[*buffers, pltpu.SemaphoreType.DMA((first[-1],)), *scratch],
        compiler_params=pltpu.CompilerParams(vmem_limit_bytes=60 * 1024 * 1024),
        cost_estimate=LARGE if name in FILLERS else SMALL,
        name=name,
    )(*ins)


def shape(dims, dtype):
    return jax.ShapeDtypeStruct(dims, dtype)


def smem():
    return pl.BlockSpec(memory_space=pltpu.SMEM)


def earlier_keys(size):
    key = lax.broadcasted_iota(jnp.int32, (size, size), 0)
    query = lax.broadcasted_iota(jnp.int32, (size, size), 1)
    return key <= query


def attention_kernel(
    narrow, own_heads, piece, side_block, side_at, experts,
    where_ref, x_refs, weights_ref,
    first_ref, q_ref, k_ref, v_ref, att_ref, lse_ref, rows_ref, stat_ref, side_ref,
):
    rows, width = x_refs[0].shape
    at_wide, at_narrow = where_ref[0], where_ref[1]
    side = weights_ref[:, side_block * 128 : side_block * 128 + 128]
    side_ref[...] = side
    lane = lax.broadcasted_iota(jnp.int32, (8, 128), 1)
    which = lax.broadcasted_iota(jnp.int32, (8, 128), 0)
    wanted = jnp.where(which < 4, side_at + which, side_at + 4 + at_wide)
    pick = jnp.where(lane == wanted, 1.0, 0.0)
    vectors = dot_nt(pick, side.astype(F32))
    rows_ref[...] = vectors
    stat_rows = stat_ref.shape[0]
    column = lax.broadcasted_iota(jnp.int32, (stat_rows, width), 1)
    which = lax.broadcasted_iota(jnp.int32, (stat_rows, width), 0)
    segment_row = (at_wide * narrow + which) * piece
    wanted = jnp.where(which < narrow, segment_row, column - lax.rem(column, piece))
    stat = dot(jnp.where(column == wanted, 1.0, 0.0), side.astype(F32))
    stat_ref[...] = stat
    seg_lane = side_at + 4 + 2 * experts
    segs = [stat[i : i + 1, seg_lane : seg_lane + 1] for i in range(narrow)]
    gain, bias = vectors[0:1], vectors[1:2]
    for place in range(narrow):
        unit, _ = norm_parts(x_refs[place][...].astype(F32))
        first_ref[at_narrow ^ place] = (unit * gain + bias).astype(BF)
    first_ref.push()
    own_width = own_heads * HEAD_DIM
    for block in range(narrow):
        at = pl.ds(block * rows, rows)
        qkv = dot(first_ref.ref[block], weights_ref[...])
        for head in range(own_heads):
            low, high = head * HEAD_DIM, (head + 1) * HEAD_DIM
            q_ref[head, at] = (qkv[:, low:high].astype(BF).astype(F32) * SCALE_FACTOR).astype(BF)
            k_ref[head, at] = qkv[:, own_width + low : own_width + high].astype(BF)
            v_ref[head, at] = qkv[:, 2 * own_width + low : 2 * own_width + high].astype(BF)
    for ref in (q_ref, k_ref, v_ref):
        ref.push()
    mask = earlier_keys(rows)
    for head in range(own_heads):
        for block in range(narrow):
            at = pl.ds(block * rows, rows)
            query = q_ref.ref[head, at]
            scores = []
            for other in range(block + 1):
                score = dot_nt(k_ref.ref[head, pl.ds(other * rows, rows)], query)
                if other == block:
                    score = jnp.where(mask, score, FLOOR_SCORE)
                else:
                    score = score + jnp.where(segs[block] == segs[other], 0.0, FLOOR_SCORE)
                scores.append(score)
            top = scores[0].max(axis=0, keepdims=True)
            for score in scores[1:]:
                top = jnp.maximum(top, score.max(axis=0, keepdims=True))
            exps = [jnp.exp(score - top) for score in scores]
            total = exps[0].sum(axis=0, keepdims=True)
            for value in exps[1:]:
                total = total + value.sum(axis=0, keepdims=True)
            share = 1.0 / total
            att = None
            for other, value in enumerate(exps):
                term = dot_tn((value * share).astype(BF), v_ref.ref[head, pl.ds(other * rows, rows)])
                att = term if att is None else att + term
            att_ref[at, head * HEAD_DIM : (head + 1) * HEAD_DIM] = att.astype(BF)
            lse_ref[head, :, at] = top + jnp.log(total)


def project(where, att, out_w, narrow):
    rows, width = att.shape[0] // narrow, out_w.shape[1]

    def body(where_ref, att_ref, out_w_ref, *parts):
        for place in reversed(range(narrow)):
            at = pl.ds(pl.multiple_of((where_ref[1] ^ place) * rows, rows), rows)
            parts[place][...] = dot(att_ref[at], out_w_ref[...]).astype(parts[place].dtype)
            parts[place].push()

    outs = [shape((rows, width), BF if i & 1 else F32) for i in range(narrow)]
    return run(body, outs, [where, att, out_w], "project", first_smem=True)


def attention(where, x_blocks, weights, own_heads, piece, side_block, side_at, experts):
    narrow = len(x_blocks)
    rows, width = x_blocks[0].shape
    group = rows * narrow
    stat_rows = -(-(narrow + 1) // 8) * 8
    head_shape = jax.ShapeDtypeStruct((own_heads, group, HEAD_DIM), BF)
    outs = (
        [jax.ShapeDtypeStruct((narrow, rows, width), BF)]
        + [head_shape] * 3
        + [shape((group, own_heads * HEAD_DIM), BF)]
        + [jax.ShapeDtypeStruct((own_heads, 1, group), F32)]
        + [shape((8, width), F32), shape((stat_rows, 128), F32), shape((width, 128), BF)]
    )

    def body(where_ref, *refs):
        attention_kernel(
            narrow, own_heads, piece, side_block, side_at, experts,
            where_ref, refs[:narrow], *refs[narrow:],
        )

    return run(body, outs, [where, *x_blocks, weights], "attention_forward", first_smem=True)


def gelu_pieces(z):
    size = jnp.abs(z)
    fall = jnp.exp(z * z * -0.5)
    t = 1.0 / (1.0 + size * (0.3275911 * 0.7071067811865476))
    tail = 1.061405429 * 0.5
    for term in (-1.453152027, 1.421413741, -0.284496736, 0.254829592):
        tail = tail * t + term * 0.5
    tail = tail * t * fall
    upper = jnp.where(z < 0.0, tail, 1.0 - tail)
    return upper, z * fall * 0.3989422804014327


def expert_share(x, dy, w_in, w_back, act_ref, dz_ref, at):
    z, low = None, 0
    for cut in w_in:
        term = dot(x[:, low : low + cut.shape[0]], cut[...])
        z = term if z is None else z + term
        low += cut.shape[0]
    upper, bump = gelu_pieces(z)
    act = (z * upper).astype(BF)
    act_ref[at] = act
    du = dot_nt(dy, w_back[...])
    dz = (du * (upper + bump)).astype(BF)
    dz_ref[at] = dz
    dx = [dot_nt(dz, cut[...]) for cut in w_in]
    dx = dx[0] if len(dx) == 1 else jnp.concatenate(dx, axis=1)
    return dx, jnp.sum(act.astype(F32) * du, axis=1, keepdims=True)


def row_gate(x, vectors):
    score = jnp.sum(x.astype(F32) * vectors[4:5], axis=1, keepdims=True)
    return 1.0 / (1.0 + jnp.exp(-score))


STEP = 256


def expert(info, xs, gs, vectors, ins, backs):
    count, width = xs[0].shape
    hidden = backs[0].shape[0]
    shares, cuts = len(backs), len(ins[0])
    blocks = [(half, start) for half in range(2) for start in range(0, count, STEP)]

    def body(info_ref, vec, *refs):
        x_refs, w1_first, w2_first, g_refs = refs[:2], refs[2 : 2 + cuts], refs[2 + cuts], refs[3 + cuts : 5 + cuts]
        rest, o = refs[5 + cuts : 4 + shares * (cuts + 1)], refs[4 + shares * (cuts + 1) :]
        w1 = [w1_first] + [rest[i * (cuts + 1) : i * (cuts + 1) + cuts] for i in range(shares - 1)]
        w2 = [w2_first] + [rest[i * (cuts + 1) + cuts] for i in range(shares - 1)]
        dx_refs, router, dy, acts, dzs = o[:2], o[2], o[3], o[4 : 4 + shares], o[4 + shares : 4 + 2 * shares]
        back_refs = o[4 + 2 * shares : 3 + 3 * shares]
        dx_acc, score_acc = o[3 + 3 * shares :]
        router_sum = jnp.zeros((1, width), F32)
        for i in range(shares):
            for number, (half, start) in enumerate(blocks):
                at = pl.ds(start, min(STEP, count))
                rows = x_refs[half][at]
                if i == 0:
                    gate = row_gate(rows, vec)
                    dy[half, at] = (gate * g_refs[half][at].astype(F32)).astype(BF)
                    dy.push(number)
                dx, score = expert_share(
                    rows, dy.ref[half, at], w1[i], w2[i], acts[i].ref.at[half], dzs[i].ref.at[half], at
                )
                acts[i].push(number)
                dzs[i].push(number)
                if i > 0:
                    dx, score = dx + dx_acc[half, at], score + score_acc[half, at]
                if i < shares - 1:
                    dx_acc[half, at], score_acc[half, at] = dx, score
                else:
                    gate = row_gate(rows, vec)
                    dlogit = (score + info_ref[0:1, 1:2] * gate) * (1.0 - gate)
                    router_sum = router_sum + jnp.sum(
                        rows.astype(F32) * dlogit, axis=0, keepdims=True
                    )
                    dx_refs[half][at] = (dx + dlogit * vec[4:5]).astype(dx_refs[half].dtype)
                    if start + STEP >= count:
                        dx_refs[half].push()
            if i < shares - 1:
                act, grad = acts[i].ref, dy.ref
                back_refs[i][...] = (dot_tn(act[0], grad[0]) + dot_tn(act[1], grad[1])).astype(BF)
                back_refs[i].push()
        router[...] = router_sum

    outs = [shape((count, width), BF), shape((count, width), F32), shape((1, width), F32)]
    outs += [shape((2, count, width), BF)] + [shape((2, count, hidden), BF)] * (2 * shares)
    parts = len(outs)
    outs += [shape((hidden, width), BF)] * (shares - 1)
    cut = [(half, pl.ds(start, min(STEP, count))) for half, start in blocks]
    operands = [info, vectors, *xs, *ins[0], backs[0], *gs]
    for i in range(1, shares):
        operands += [*ins[i], backs[i]]
    scratch = [pltpu.VMEM((2, count, width), F32), pltpu.VMEM((2, count, 1), F32)]
    pieces = {i: cut for i in range(3, parts)}
    res = list(run(body, outs, operands, "expert", scratch, pieces=pieces))
    acts, dzs = res[4 : 4 + shares], res[4 + shares : parts]
    return res[0], res[1], res[2], res[3], acts, dzs, res[parts:]


def partner_terms(xs, acts, dzs, backs, cut):
    shares = len(acts)
    count, width, hidden = shares - 1, xs[0].shape[1], acts[0].shape[2]
    cuts = [slice(0, cut), slice(cut, width)]

    def body(*refs):
        x_refs, dz, act, back = refs[:2], refs[2 : 2 + count], refs[2 + count :][:shares], refs[2 + count + shares :][:shares]
        y_refs, outs = refs[2 + count + 2 * shares :][:2], list(refs[4 + count + 2 * shares :])
        for at in cuts:
            for i in range(count):
                out = outs.pop(0)
                term = dot_tn(x_refs[0][:, at], dz[i][0]) + dot_tn(x_refs[1][:, at], dz[i][1])
                out[...] = term.astype(BF)
                out.push()
        for half, out in enumerate(y_refs):
            total = dot(act[0][half], back[0][...])
            for i in range(1, shares):
                total = total + dot(act[i][half], back[i][...])
            out[...] = total.astype(out.dtype)
            out.push()

    outs = [shape(xs[0].shape, BF), shape(xs[0].shape, F32)]
    outs += [shape((at.stop - at.start, hidden), BF) for at in cuts for _ in range(count)]
    res = run(body, outs, [*xs, *dzs[:-1], *acts, *backs], "partner_terms")
    return res[0], res[1], [list(res[i : i + count]) for i in range(2, len(outs), count)]


def own_terms(xs, dy, act, dz):
    def body(act, dy, x_a, x_b, dz, own_back, own_in):
        own_back[...] = dot_tn(act[0], dy[0]) + dot_tn(act[1], dy[1])
        own_back.push()
        own_in[...] = dot_tn(x_a[...], dz[0]) + dot_tn(x_b[...], dz[1])

    width, hidden = xs[0].shape[1], act.shape[2]
    outs = [shape((hidden, width), F32), shape((width, hidden), F32)]
    return run(body, outs, [act, dy, *xs, dz], "own_terms")


def attention_back_kernel(
    narrow, own_heads, columns, seg_lane,
    where_ref, dr_refs, out_w_ref, q_ref, k_ref, v_ref, lse_ref, stat_ref, att_ref,
    dqkv_ref, out_terms_ref,
    dr_all, da, dk_acc, dv_acc,
):
    rows, width = dr_refs[0].shape
    group = rows * narrow
    own_width = own_heads * HEAD_DIM
    at_narrow = where_ref[1]
    for place in range(narrow):
        dr_all[at_narrow ^ place] = dr_refs[place][...]
    dqkv = dqkv_ref.ref
    segs = [stat_ref[i : i + 1, seg_lane : seg_lane + 1] for i in range(narrow)]
    mask = earlier_keys(rows)
    dqkv[:, columns - 128 :] = jnp.zeros((group, 128), BF)
    for block in range(narrow):
        at = pl.ds(block * rows, rows)
        d_att = dot_nt(dr_all[block], out_w_ref[...]).astype(BF)
        for head in range(own_heads):
            da[head, at] = d_att[:, head * HEAD_DIM : (head + 1) * HEAD_DIM]
    for head in range(own_heads):
        low, high = head * HEAD_DIM, (head + 1) * HEAD_DIM
        for block in reversed(range(narrow)):
            at = pl.ds(block * rows, rows)
            query, d_att, lse = q_ref[head, at], da[head, at], lse_ref[head, :, at]
            probs, d_probs, delta = [], [], None
            for other in range(block + 1):
                keys = pl.ds(other * rows, rows)
                score = dot_nt(k_ref[head, keys], query)
                if other == block:
                    prob = jnp.where(mask, jnp.exp(score - lse), 0.0)
                else:
                    prob = jnp.exp(
                        score - (lse + jnp.where(segs[block] == segs[other], 0.0, -FLOOR_SCORE))
                    )
                d_prob = dot_nt(v_ref[head, keys], d_att)
                part = jnp.sum(prob * d_prob, axis=0, keepdims=True)
                delta = part if delta is None else delta + part
                probs.append(prob)
                d_probs.append(d_prob)
            dq = None
            for other in range(block + 1):
                keys = pl.ds(other * rows, rows)
                d_score = (probs[other] * (d_probs[other] - delta)).astype(BF)
                term = dot_tn(d_score, k_ref[head, keys])
                dq = term if dq is None else dq + term
                dk = dot(d_score, query)
                dv = dot(probs[other].astype(BF), d_att)
                if block == narrow - 1:
                    dk_acc[keys] = dk
                    dv_acc[keys] = dv
                else:
                    dk_acc[keys] += dk
                    dv_acc[keys] += dv
            dqkv[at, low:high] = (dq * SCALE_FACTOR).astype(BF)
        dqkv[:, own_width + low : own_width + high] = dk_acc[...].astype(BF)
        dqkv[:, 2 * own_width + low : 2 * own_width + high] = dv_acc[...].astype(BF)
    dqkv_ref.push()
    out_terms_ref[...] = dot_tn(att_ref[...], dr_all[...].reshape(group, width)).astype(BF)


def attention_back(where, dr_blocks, out_w, q, k, v, lse, stat, att, columns, seg_lane):
    narrow = len(dr_blocks)
    rows, width = dr_blocks[0].shape
    group = rows * narrow
    own_heads = q.shape[0]
    outs = [shape((group, columns), BF), shape((own_heads * HEAD_DIM, width), BF)]

    def body(where_ref, *refs):
        attention_back_kernel(
            narrow, own_heads, columns, seg_lane, where_ref, refs[:narrow], *refs[narrow:]
        )

    scratch = [
        pltpu.VMEM((narrow, rows, width), BF),
        pltpu.VMEM((own_heads, group, HEAD_DIM), BF),
        pltpu.VMEM((group, HEAD_DIM), F32),
        pltpu.VMEM((group, HEAD_DIM), F32),
    ]
    ins = [where, *dr_blocks, out_w, q, k, v, lse, stat, att]
    return run(body, outs, ins, "attention_backward", scratch, first_smem=True)


def weight_terms(where, dqkv, first, weights, info, sums, routers, narrow, side_block, side_at):
    group, columns = dqkv.shape
    width = weights.shape[0]
    rows = group // narrow

    def body(where_ref, dqkv_ref, first_ref, weights_ref, info_ref, sums_ref, router,
             terms_ref, *parts):
        first = first_ref[...].reshape(group, width)
        side = weights_ref[:, side_block * 128 : side_block * 128 + 128].astype(F32)
        gain, bias = side[:, side_at : side_at + 1], side[:, side_at + 1 : side_at + 2]
        gain_sum, bias_sum, last = None, None, None
        for block in range(columns // 128):
            cut = slice(block * 128, block * 128 + 128)
            term = dot_tn(first, dqkv_ref[:, cut])
            weight = weights_ref[:, cut].astype(F32)
            total = jnp.sum(dqkv_ref[:, cut].astype(F32), axis=0, keepdims=True)
            gain_part, bias_part = weight * (term - bias * total), weight * total
            gain_sum = gain_part if gain_sum is None else gain_sum + gain_part
            bias_sum = bias_part if bias_sum is None else bias_sum + bias_part
            if block == side_block:
                last = term
            else:
                terms_ref[:, cut] = term.astype(BF)
        gain_sum = jnp.sum(gain_sum, axis=1, keepdims=True) / gain
        bias_sum = jnp.sum(bias_sum, axis=1, keepdims=True)
        which = lax.broadcasted_iota(jnp.int32, (8, width), 0)
        extra = jnp.where(which == 4, router[...], sums_ref[...])
        balance = info_ref[0:1, 0:1]
        high = balance.astype(BF).astype(F32)
        extra = jnp.where(which == 5, high, jnp.where(which == 6, balance - high, extra))
        lane = lax.broadcasted_iota(jnp.int32, (8, 128), 1)
        which = lax.broadcasted_iota(jnp.int32, (8, 128), 0)
        spread = jnp.where(lane == side_at + which, 1.0, 0.0)
        lane = lax.broadcasted_iota(jnp.int32, (width, 128), 1)
        last = jnp.where(lane == side_at, gain_sum, jnp.where(lane == side_at + 1, bias_sum, last))
        last = last + dot_tn(extra, spread)
        terms_ref[:, side_block * 128 : side_block * 128 + 128] = last.astype(BF)
        terms_ref.push()
        for place in reversed(range(narrow)):
            at = pl.ds(pl.multiple_of((where_ref[1] ^ place) * rows, rows), rows)
            parts[place][...] = dot_nt(dqkv_ref[at], weights_ref[...]).astype(parts[place].dtype)
            parts[place].push()

    outs = [shape((width, columns), BF)]
    outs += [shape((rows, width), BF if i & 1 else F32) for i in range(narrow)]
    ins = [where, dqkv, first, weights, info, sums, *routers]
    res = run(body, outs, ins, "weight_terms", first_smem=True)
    return res[0], list(res[1:])


def turned(row):
    count = row.shape[1]
    at = lax.broadcasted_iota(jnp.int32, (count, count), 0)
    other = lax.broadcasted_iota(jnp.int32, (count, count), 1)
    return jnp.sum(jnp.where(at == other, row, 0.0), axis=1, keepdims=True)


def pack(weights, vectors, w_router, routing, segments, wide, narrow, own_width, columns):
    piece, width = weights[0].shape
    experts = w_router.shape[1]
    rows = routing.shape[0]
    start = 3 * own_width

    def body(wq, wk, wv, va, vb, vc, vd, wr, route, segment, sent, held):
        held[...] = jnp.zeros_like(held)
        ids = lax.broadcasted_iota(jnp.int32, (experts, rows), 0)
        counts = jnp.sum(jnp.where(route[...] == ids, 1.0, 0.0), axis=1, keepdims=True)
        sides = [turned(ref[...]) for ref in (va, vb, vc, vd)]
        sides += [turned(wr[i : i + 1]) for i in range(experts)]
        sides += [counts[i : i + 1] for i in range(experts)]
        sides += [segment[0:1, 0:1].astype(F32)]
        lane = lax.broadcasted_iota(jnp.int32, (piece, 128), 1)
        block = jnp.zeros((piece, 128), F32)
        for i, value in enumerate(sides):
            block = jnp.where(lane == start % 128 + i, value, block)
        for n in range(narrow):
            held[n, :, columns - 128 :] = block
            low, high = n * own_width, min((n + 1) * own_width, width)
            for i, ref in enumerate((wq, wk, wv)):
                if low < high:
                    held[n, :, i * own_width : i * own_width + high - low] = ref[:, low:high]

        def send(w, carry):
            for n in range(narrow):
                sent[w * narrow + n] = held[n].astype(BF)
            return carry

        lax.fori_loop(0, wide, send, 0)

    outs = [shape((wide * narrow, piece, columns), BF)]
    ins = [*weights, *[v.reshape(1, piece) for v in vectors], w_router.T]
    ins += [routing.reshape(1, rows), segments.reshape(1, rows)]
    return run(body, outs, ins, "pack", [pltpu.VMEM((narrow, piece, columns), F32)])[0]


def cast_weights(w_in, w_back, cut):
    def body(first, second, upper, lower, back):
        upper[...] = first[:cut].astype(BF)
        upper.push()
        lower[...] = first[cut:].astype(BF)
        lower.push()
        back[...] = second[...].astype(BF)

    width, hidden = w_in.shape
    outs = [shape((cut, hidden), BF), shape((width - cut, hidden), BF), shape(w_back.shape, BF)]
    return run(body, outs, [w_in, w_back], "cast_weights")


def place_cotangent(routing, cotangent, experts, capacity, piece, copies):
    rows, width = cotangent.shape
    slots = experts * capacity

    def body(route, g, piece_ref, placing, moved, tiled):
        for i in range(copies):
            tiled[i] = piece_ref[...]
        tiled.push()
        ids = lax.broadcasted_iota(jnp.int32, (rows, experts), 1)
        expert = turned(route[...].astype(F32)).astype(jnp.int32)
        hot = jnp.where(expert == ids, 1.0, 0.0)
        row = lax.broadcasted_iota(jnp.int32, (rows, rows), 0)
        column = lax.broadcasted_iota(jnp.int32, (rows, rows), 1)
        before = dot(jnp.where(row > column, 1.0, 0.0).astype(BF), hot.astype(BF))
        slot = jnp.sum(before * hot, axis=1, keepdims=True).astype(jnp.int32)
        target = expert * capacity + slot
        place = lax.broadcasted_iota(jnp.int32, (rows, slots), 1)
        spot = jnp.where(place == target, 1.0, 0.0).astype(BF)
        placing[...] = spot
        moved[...] = dot_tn(spot, g[...]).astype(BF)

    outs = [shape((rows, slots), BF), shape((slots, width), BF), shape((copies, *piece.shape), BF)]
    return run(body, outs, [routing.reshape(1, rows), cotangent, piece], "place_cotangent")


def second_norm(x, halves, vectors, side, stat, placing, routing, where, dims):
    narrow, experts, total, side_at = dims
    rows, width = x.shape
    slots = placing.shape[1]
    count = len(halves)

    def body(where_ref, x_ref, *refs):
        vec, side_ref, stat_ref, placing_ref, route = refs[count : count + 5]
        mixed_ref, moved, gate_ref, info = refs[count + 5 :]
        mixed = x_ref[...].astype(F32)
        for ref in refs[:count]:
            mixed = mixed + ref[...].astype(F32)
        mixed_ref[...] = mixed
        unit, _ = norm_parts(mixed)
        low = (unit * vec[2:3] + vec[3:4]).astype(BF)
        moved[...] = dot_tn(placing_ref[...], low).astype(BF)
        logits = dot(low, side_ref[...])
        lane = lax.broadcasted_iota(jnp.int32, (rows, 128), 1)
        expert = turned(route[...].astype(F32)).astype(jnp.int32)
        chosen = jnp.where(lane - (side_at + 4) == expert, logits, 0.0)
        gate = 1.0 / (1.0 + jnp.exp(-jnp.sum(chosen, axis=1, keepdims=True)))
        gate_ref[...] = gate
        first = side_at + 4 + experts
        sums = jnp.sum(jnp.where(lane - first == expert, gate, 0.0), axis=0, keepdims=True)
        lane = lax.broadcasted_iota(jnp.int32, (1, 128), 1)
        counts = stat_ref[narrow : narrow + 1]
        deviation = (counts - float(total) / experts) * (experts / float(total))
        kept = (lane >= first) & (lane < first + experts)
        balance = experts / float(total) * jnp.sum(
            jnp.where(kept, deviation * sums, 0.0), axis=1, keepdims=True
        )
        own = jnp.sum(
            jnp.where(lane == first + where_ref[0], deviation, 0.0), axis=1, keepdims=True
        )
        core = jnp.where(where_ref[1] % 2 == 0, BALANCE_WEIGHT * (experts / float(total)), 0.0)
        info[...] = jnp.where(lane == 0, balance, own * core) + jnp.zeros((8, 128), F32)

    outs = [shape((rows, width), F32), shape((slots, width), BF), shape((rows, 1), F32)]
    outs.append(shape((8, 128), F32))
    ins = [where, x, *halves, vectors, side, stat, placing, routing.reshape(1, rows)]
    return run(body, outs, ins, "second_norm", first_smem=True)


def second_back(returned, placing, mixed, cotangent, vectors):
    rows, width = mixed.shape

    def body(ret, placing_ref, mixed_ref, g, vec, dr_ref, low_ref, sums):
        incoming = dot(placing_ref[...], ret[...])
        unit, inverse = norm_parts(mixed_ref[...])
        gain = jnp.sum(incoming * unit, axis=0, keepdims=True)
        bias = jnp.sum(incoming, axis=0, keepdims=True)
        dr = g[...].astype(F32) + norm_back(incoming, unit, inverse, vec[2:3])
        dr_ref[...] = dr
        low_ref[...] = dr.astype(BF)
        which = lax.broadcasted_iota(jnp.int32, (8, width), 0)
        sums[...] = jnp.where(which == 2, gain, jnp.where(which == 3, bias, 0.0))

    outs = [shape((rows, width), F32), shape((rows, width), BF), shape((8, width), F32)]
    return run(body, outs, [returned, placing, mixed, cotangent, vectors], "second_back")


def finish_rows(returned, placing, mixed, gates):
    def body(ret, placing_ref, mixed_ref, gate, out):
        out[...] = mixed_ref[...] + gate[...] * dot(placing_ref[...], ret[...])

    ins = [returned, placing, mixed, gates]
    return run(body, [shape(mixed.shape, F32)], ins, "finish_rows")[0]


def first_back(halves, x, dr, vectors):
    count = len(halves)

    def body(*refs):
        x_ref, dr_ref, vec, out = refs[count:]
        incoming = refs[0][...].astype(F32)
        for ref in refs[1:count]:
            incoming = incoming + ref[...].astype(F32)
        unit, inverse = norm_parts(x_ref[...].astype(F32))
        out[...] = dr_ref[...] + norm_back(incoming, unit, inverse, vec[0:1])

    return run(body, [shape(x.shape, F32)], [*halves, x, dr, vectors], "first_back")[0]


def unpack(came, wide, narrow, own_width, width, experts):
    piece, columns = came.shape[1:]
    start = 3 * own_width
    side_block, side_at = start // 128, start % 128

    def as_row(column):
        row = lax.broadcasted_iota(jnp.int32, (piece, piece), 0)
        other = lax.broadcasted_iota(jnp.int32, (piece, piece), 1)
        return jnp.sum(jnp.where(row == other, column, 0.0), axis=0, keepdims=True)

    def body(came_ref, gq, gk, gv, va, vb, vc, vd, gr, balance):
        every = jnp.zeros((piece, 128), F32)
        routers = []
        for n in range(narrow):
            total = jnp.zeros((piece, columns), F32)
            for w in range(wide):
                total = total + came_ref[w * narrow + n].astype(F32)
            every = every + total[:, side_block * 128 : side_block * 128 + 128]
            low, high = n * own_width, min((n + 1) * own_width, width)
            if low < high:
                for i, ref in enumerate((gq, gk, gv)):
                    ref[:, low:high] = total[:, i * own_width : i * own_width + high - low]
        for w in range(wide):
            column = jnp.zeros((piece, 1), F32)
            at = start + 4
            for n in range(narrow):
                column = column + came_ref[w * narrow + n, :, at : at + 1].astype(F32)
            gr[w : w + 1] = as_row(column)
        for i, ref in enumerate((va, vb, vc, vd)):
            ref[...] = as_row(every[:, side_at + i : side_at + i + 1])
        balance[...] = every[0:1, side_at + 5 : side_at + 6] + every[0:1, side_at + 6 : side_at + 7]

    outs = [shape((piece, width), F32)] * 3 + [shape((1, piece), F32)] * 4
    outs += [shape((experts, piece), F32), shape((1, 1), F32)]
    return run(body, outs, [came], "unpack")


def local(
    hidden_in,
    segments,
    routing,
    first_gain,
    first_bias,
    second_gain,
    second_bias,
    w_query,
    w_key,
    w_value,
    w_out,
    w_router,
    w_in,
    w_back,
    cotangent,
):
    wide = lax.axis_size("wide")
    narrow = lax.axis_size("narrow")
    devices = wide * narrow
    rows, width = hidden_in.shape
    piece = w_query.shape[0]
    experts = w_router.shape[1]
    capacity = max(2, 2 * rows // experts)
    total = rows * devices
    own_heads = -(-HEADS // narrow)
    own_width = own_heads * HEAD_DIM
    aligned = own_width * narrow == width and own_width == piece * wide
    at_wide = lax.axis_index("wide")
    at_narrow = lax.axis_index("narrow")
    where = jnp.stack([at_wide, at_narrow]).astype(jnp.int32)
    bits = [1 << level for level in range(narrow.bit_length() - 1)]
    core_bit, chip_bits = bits[:1], bits[1:]
    side_start = 3 * own_width
    side_block, side_at = side_start // 128, side_start % 128
    seg_lane = side_at + 4 + 2 * experts
    assert seg_lane < 128
    columns = side_block * 128 + 128
    gate = lax.optimization_barrier

    def swap(values, bit):
        return lax.ppermute(values, "narrow", [(i, i ^ bit) for i in range(narrow)])

    def gather_blocks(block, over):
        blocks = {0: block}
        for bit in reversed(over):
            for place in list(blocks):
                blocks[place ^ bit] = swap(blocks[place], bit)
        return blocks

    def reduce_blocks(blocks, over):
        blocks = dict(blocks)
        for bit in over:
            for place in sorted(blocks, reverse=True):
                if place & bit:
                    moved = swap(blocks.pop(place).astype(BF), bit).astype(F32)
                    blocks[place ^ bit] = blocks[place ^ bit] + moved
        return blocks

    def exchange(values):
        values = values.reshape(experts, capacity, width)
        return to_all(values, "wide").reshape(experts * capacity, width)

    sent = pack(
        [w_query, w_key, w_value], [first_gain, first_bias, second_gain, second_bias],
        w_router, routing, segments, wide, narrow, own_width, columns,
    )
    x_blocks = gather_blocks(hidden_in, chip_bits)
    out_low = w_out.astype(BF)
    if aligned:
        out_low = lax.ppermute(
            out_low, BOTH, [(n * wide + j, j * narrow + n) for n in range(narrow) for j in range(wide)]
        )
    far = {i: x_blocks[i] for i in x_blocks if i >= 2 and not i & 1}
    *in_low, back_low = cast_weights(w_in[0], w_back[0], width // 2)
    sent, out_low, far, where = gate((sent, out_low, far, where))
    x_blocks.update(far)
    weights = to_all(sent, BOTH).reshape(width, columns)
    for place in list(x_blocks):
        x_blocks[place ^ 1] = swap(x_blocks[place], 1)
    partners = [i for i in range(2, narrow, 2)]
    in_upper = [swap(in_low[0], i) for i in partners]
    placing, g_moved, out_tiled = place_cotangent(
        routing, cotangent, experts, capacity, out_low, wide
    )
    weights, in_low, back_low, g_moved, in_upper, out_tiled = gate(
        (weights, in_low, back_low, g_moved, in_upper, out_tiled)
    )
    back_came = [swap(back_low, i) for i in partners]
    if aligned:
        out_w = to_all(out_tiled, "wide").reshape(own_width, width)
    else:
        all_out = lax.all_gather(out_low, BOTH, axis=0, tiled=True)
        all_out = jnp.pad(all_out, ((0, own_width * narrow - width), (0, 0)))
        out_w = lax.dynamic_slice_in_dim(all_out, at_narrow * own_width, own_width, axis=0)

    x_list = [x_blocks[i] for i in range(narrow)]
    first, q, k, v, att, lse, vectors, stat, side = attention(
        where, x_list, weights, own_heads, piece, side_block, side_at, experts
    )
    att, g_moved = gate((att, g_moved))
    g_own = exchange(g_moved)
    parts = project(where, att, out_w, narrow)
    halves = reduce_blocks({i: parts[i] for i in range(narrow)}, core_bit)
    halves, back_came = gate((halves, back_came))
    halves = {i: swap(halves[i].astype(BF), i) if i else halves[i] for i in sorted(halves)}

    halves, g_own, in_low = gate((halves, g_own, in_low))
    in_lower = [swap(in_low[1], i) for i in partners]
    mixed, x_moved, gates, info = second_norm(
        hidden_in, [halves[i] for i in sorted(halves)], vectors, side, stat, placing, routing,
        where, (narrow, experts, total, side_at),
    )
    g_other = swap(g_own, 1)
    x_own = exchange(x_moved)
    x_own, in_lower = gate((x_own, in_lower))
    x_other = swap(x_own, 1)

    ins = [list(pair) for pair in zip(in_upper, in_lower)] + [in_low]
    backs = [*back_came, back_low]
    xs = [x_other, x_own]
    dx_o, dx_s, router, dy, acts, dzs, far_back = expert(info, xs, [g_other, g_own], vectors, ins, backs)

    def cross(cut):
        return [swap(value, place) for value, place in zip(cut, partners)]

    dx_sum = (dx_s + swap(dx_o, 1).astype(F32)).astype(BF)
    d_returned = exchange(dx_sum)
    acts, dx_sum = gate((acts, dx_sum))
    far_back = cross(far_back)
    y_o, y_s, made = partner_terms(xs, acts, dzs, backs, width // 3)
    made, far_back = gate((made, far_back))
    crossed = [cross(made[0])]
    y_sum = (y_s + swap(y_o, 1).astype(F32)).astype(BF)
    d_mixed, d_mixed_low, sums = second_back(d_returned, placing, mixed, cotangent, vectors)
    tied = (d_mixed_low, y_sum, crossed, dy, acts[-1], dzs[-1])
    d_mixed_low, y_sum, crossed, dy, own_act, own_dz = gate(tied)
    own_back, own_in = own_terms(xs, dy, own_act, own_dz)
    returned = exchange(y_sum)
    dr_blocks = gather_blocks(d_mixed_low, chip_bits)
    dr_blocks, own_back, own_in = gate((dr_blocks, own_back, own_in))
    for place in list(dr_blocks):
        dr_blocks[place ^ 1] = swap(dr_blocks[place], 1)
    dr_blocks, made = gate((dr_blocks, made))
    crossed.append(cross(made[1]))
    dr_list = [dr_blocks[i] for i in range(narrow)]

    d_qkv, terms_out = attention_back(
        where, dr_list, out_w, q, k, v, lse, stat, att, columns, seg_lane
    )
    d_qkv, crossed, terms_out, returned = gate((d_qkv, crossed, terms_out, returned))
    if aligned:
        terms_out = to_all(terms_out.reshape(wide, piece, width), "wide")
    terms, d_parts = weight_terms(
        where, d_qkv, first, weights, info, sums, [router], narrow, side_block, side_at
    )

    terms, terms_out = gate((terms, terms_out))
    terms = to_all(terms.reshape(devices, piece, columns), BOTH)
    d_halves = reduce_blocks({i: d_parts[i] for i in range(narrow)}, core_bit)
    d_halves = [swap(d_halves[i].astype(BF), i) if i else d_halves[i] for i in sorted(d_halves)]
    if aligned:
        grad_out_w = lax.ppermute(
            jnp.sum(terms_out.astype(F32), axis=0),
            BOTH,
            [(j * narrow + n, n * wide + j) for n in range(narrow) for j in range(wide)],
        )
    else:
        spread = jnp.zeros((own_width * narrow, width), F32)
        spread = lax.dynamic_update_slice_in_dim(
            spread, terms_out.astype(F32), at_narrow * own_width, axis=0
        )
        grad_out_w = lax.psum_scatter(spread[:width], BOTH, scatter_dimension=0, tiled=True)
    block_out = finish_rows(returned, placing, mixed, gates)
    grad_hidden = first_back(d_halves, hidden_in, d_mixed, vectors)
    term_in = [jnp.concatenate(cuts, axis=0) for cuts in zip(*crossed)]

    def gathered(own, came):
        for value in came:
            own = own + value.astype(F32)
        return own

    done = unpack(terms, wide, narrow, own_width, width, experts)
    return (
        block_out,
        done[8].reshape(()),
        grad_hidden,
        *[done[i].reshape(piece) for i in range(3, 7)],
        *done[:3],
        grad_out_w,
        done[7].T,
        gathered(own_in, term_in)[None],
        gathered(own_back, far_back)[None],
    )


def solution(mesh):
    rows = P(BOTH, None)
    vector = P(BOTH)
    placed = (rows, vector, rows) + (vector,) * 4 + (rows,) * 5
    expert_specs = (P("wide", None, "narrow"), P("wide", "narrow", None))
    return jax.shard_map(
        local,
        mesh=mesh,
        in_specs=placed + expert_specs + (rows,),
        out_specs=(rows, P(), rows) + (vector,) * 4 + (rows,) * 5 + expert_specs,
        check_vma=False,
    )
```

```python
import jax
import jax.numpy as jnp
from jax import lax
from jax.experimental import pallas as pl
from jax.experimental.pallas import tpu as pltpu
from jax.sharding import PartitionSpec as P

HEADS = 12
HEAD_DIM = 64
EPSILON = 1e-05
FLOOR_SCORE = -1e30
SCALE_FACTOR = 0.125
BALANCE_WEIGHT = 0.01
BOTH = ("wide", "narrow")
BF = jnp.bfloat16
F32 = jnp.float32


def dot(left, right):
    return jnp.dot(left, right, preferred_element_type=F32)


def dot_nt(left, right):
    return lax.dot_general(left, right, (((1,), (1,)), ((), ())), preferred_element_type=F32)


def dot_tn(left, right):
    return lax.dot_general(left, right, (((0,), (0,)), ((), ())), preferred_element_type=F32)


def norm_parts(values):
    centered = values - jnp.mean(values, axis=1, keepdims=True)
    inverse = lax.rsqrt(jnp.mean(centered * centered, axis=1, keepdims=True) + EPSILON)
    return centered * inverse, inverse


def norm_back(incoming, unit, inverse, gain):
    scaled = incoming * gain
    return inverse * (
        scaled
        - jnp.mean(scaled, axis=1, keepdims=True)
        - unit * jnp.mean(scaled * unit, axis=1, keepdims=True)
    )


def to_all(values, axes):
    return lax.all_to_all(values, axes, split_axis=0, concat_axis=0, tiled=True)


SMALL = pl.CostEstimate(flops=1000, bytes_accessed=1000, transcendentals=0)
LARGE = pl.CostEstimate(flops=int(2.5e10), bytes_accessed=int(3e7), transcendentals=0)
FILLERS = ("place_cotangent", "cast_weights")


class Held:
    def __init__(self, ref, copies, fetched):
        self.ref, self.copies = ref, copies
        self.waiting = list(range(len(copies))) if fetched else []
        self.started = set(self.waiting)

    def get(self):
        for i in self.waiting:
            self.copies[i].wait()
        self.waiting = []
        return self.ref

    def push(self, part=None):
        for i in range(len(self.copies)) if part is None else [part]:
            if i not in self.started and i < len(self.copies):
                self.copies[i].start()
                self.waiting.append(i)
                self.started.add(i)

    @property
    def shape(self):
        return self.ref.shape

    @property
    def dtype(self):
        return self.ref.dtype

    def __getitem__(self, at):
        return self.get()[at]

    def __setitem__(self, at, value):
        self.ref[at] = value


def padded(value):
    lanes = -(-value.shape[-1] // 128) * 128
    rows = -(-value.shape[-2] // 16) * 16 if len(value.shape) > 1 else 16
    outer = 1
    for size in value.shape[:-2]:
        outer *= size
    return outer * rows * lanes * jnp.dtype(value.dtype).itemsize


def run(body, outs, ins, name, scratch=(), first_smem=False, pieces=None, close=(), close_outs=(), room=10):
    outs, ins = list(outs), list(ins)
    lead = 1 if first_smem else 0
    fetched, total = len(ins) - lead, len(ins) - lead + len(outs)
    arrays = ins[lead:] + outs
    near = [i in close if i < fetched else i - fetched in close_outs for i in range(total)]
    cuts = [(pieces or {}).get(i - fetched, [()]) for i in range(total)]
    slots, semaphores, used = {}, {}, 0
    for i in range(total):
        if not near[i]:
            slots[i], semaphores[i] = len(slots), used
            used += len(cuts[i])
    buffers = [pltpu.VMEM(arrays[i].shape, arrays[i].dtype) for i in slots]

    def kernel(*refs):
        smem_refs, given = refs[:lead], refs[lead : lead + total]
        own = refs[lead + total : lead + total + len(slots)]
        marks = refs[lead + total + len(slots)]
        held = []
        for i in range(total):
            if near[i]:
                held.append(Held(given[i], [], False))
                continue
            mine = own[slots[i]]
            source, target = (given[i], mine) if i < fetched else (mine, given[i])
            copies = []
            for j, at in enumerate(cuts[i]):
                ends = (source.at[at], target.at[at]) if at else (source, target)
                copies.append(pltpu.make_async_copy(*ends, marks.at[semaphores[i] + j]))
            if i < fetched:
                copies[0].start()
            held.append(Held(mine, copies, i < fetched))
        body(*smem_refs, *held, *refs[lead + total + len(slots) + 1 :])
        for item in held[fetched:]:
            item.push()
        for item in held:
            item.get()

    hbm, vmem = pl.BlockSpec(memory_space=pltpu.HBM), pl.BlockSpec(memory_space=pltpu.VMEM)
    ins = [
        value if i < lead or near[i - lead] else pltpu.with_memory_space_constraint(value, pltpu.HBM)
        for i, value in enumerate(ins)
    ]
    placed = [
        value if near[fetched + i] else pltpu.HBM(value.shape, value.dtype)
        for i, value in enumerate(outs)
    ]
    size = sum(padded(arrays[i]) for i in slots) + sum(padded(value) for value in scratch)
    limit = min(60, size // 2**20 + 1 + room)
    return pl.pallas_call(
        kernel,
        out_shape=placed,
        in_specs=([smem()] if first_smem else []) + [vmem if near[i] else hbm for i in range(fetched)],
        out_specs=[vmem if near[fetched + i] else hbm for i in range(len(outs))],
        scratch_shapes=[*buffers, pltpu.SemaphoreType.DMA((max(1, used),)), *scratch],
        compiler_params=pltpu.CompilerParams(vmem_limit_bytes=limit * 1024 * 1024),
        cost_estimate=LARGE if name in FILLERS else SMALL,
        name=name,
    )(*ins)


def shape(dims, dtype):
    return jax.ShapeDtypeStruct(dims, dtype)


def smem():
    return pl.BlockSpec(memory_space=pltpu.SMEM)


def earlier_keys(size):
    key = lax.broadcasted_iota(jnp.int32, (size, size), 0)
    query = lax.broadcasted_iota(jnp.int32, (size, size), 1)
    return key <= query


def attention_kernel(
    narrow, own_heads, piece, side_block, side_at, experts,
    where_ref, x_refs, weights_ref,
    first_ref, q_ref, k_ref, v_ref, att_ref, lse_ref, rows_ref, stat_ref, side_ref,
):
    rows, width = x_refs[0].shape
    at_wide, at_narrow = where_ref[0], where_ref[1]
    side = weights_ref[:, side_block * 128 : side_block * 128 + 128]
    side_ref[...] = side
    lane = lax.broadcasted_iota(jnp.int32, (8, 128), 1)
    which = lax.broadcasted_iota(jnp.int32, (8, 128), 0)
    wanted = jnp.where(which < 4, side_at + which, side_at + 4 + at_wide)
    pick = jnp.where(lane == wanted, 1.0, 0.0)
    vectors = dot_nt(pick, side.astype(F32))
    rows_ref[...] = vectors
    stat_rows = stat_ref.shape[0]
    column = lax.broadcasted_iota(jnp.int32, (stat_rows, width), 1)
    which = lax.broadcasted_iota(jnp.int32, (stat_rows, width), 0)
    segment_row = (at_wide * narrow + which) * piece
    wanted = jnp.where(which < narrow, segment_row, column - lax.rem(column, piece))
    stat = dot(jnp.where(column == wanted, 1.0, 0.0), side.astype(F32))
    stat_ref[...] = stat
    seg_lane = side_at + 4 + 2 * experts
    segs = [stat[i : i + 1, seg_lane : seg_lane + 1] for i in range(narrow)]
    gain, bias = vectors[0:1], vectors[1:2]
    for place in range(narrow):
        unit, _ = norm_parts(x_refs[place][...].astype(F32))
        first_ref[at_narrow ^ place] = (unit * gain + bias).astype(BF)
    first_ref.push()
    own_width = own_heads * HEAD_DIM
    for block in range(narrow):
        at = pl.ds(block * rows, rows)
        qkv = dot(first_ref.ref[block], weights_ref[...])
        for head in range(own_heads):
            low, high = head * HEAD_DIM, (head + 1) * HEAD_DIM
            q_ref[head, at] = (qkv[:, low:high].astype(BF).astype(F32) * SCALE_FACTOR).astype(BF)
            k_ref[head, at] = qkv[:, own_width + low : own_width + high].astype(BF)
            v_ref[head, at] = qkv[:, 2 * own_width + low : 2 * own_width + high].astype(BF)
    for ref in (q_ref, k_ref, v_ref):
        ref.push()
    mask = earlier_keys(rows)
    for head in range(own_heads):
        for block in range(narrow):
            at = pl.ds(block * rows, rows)
            query = q_ref.ref[head, at]
            scores = []
            for other in range(block + 1):
                score = dot_nt(k_ref.ref[head, pl.ds(other * rows, rows)], query)
                if other == block:
                    score = jnp.where(mask, score, FLOOR_SCORE)
                else:
                    score = score + jnp.where(segs[block] == segs[other], 0.0, FLOOR_SCORE)
                scores.append(score)
            top = scores[0].max(axis=0, keepdims=True)
            for score in scores[1:]:
                top = jnp.maximum(top, score.max(axis=0, keepdims=True))
            exps = [jnp.exp(score - top) for score in scores]
            total = exps[0].sum(axis=0, keepdims=True)
            for value in exps[1:]:
                total = total + value.sum(axis=0, keepdims=True)
            share = 1.0 / total
            att = None
            for other, value in enumerate(exps):
                term = dot_tn((value * share).astype(BF), v_ref.ref[head, pl.ds(other * rows, rows)])
                att = term if att is None else att + term
            att_ref[at, head * HEAD_DIM : (head + 1) * HEAD_DIM] = att.astype(BF)
            lse_ref[head, :, at] = top + jnp.log(total)


def project(where, att, out_w, narrow):
    rows, width = att.shape[0] // narrow, out_w.shape[1]

    def body(where_ref, att_ref, out_w_ref, *parts):
        for place in reversed(range(narrow)):
            at = pl.ds(pl.multiple_of((where_ref[1] ^ place) * rows, rows), rows)
            parts[place][...] = dot(att_ref[at], out_w_ref[...]).astype(parts[place].dtype)
            parts[place].push()

    outs = [shape((rows, width), BF if i & 1 else F32) for i in range(narrow)]
    return run(
        body, outs, [where, att, out_w], "project", first_smem=True, close=(0,), close_outs=range(narrow)
    )


def attention(where, x_blocks, weights, own_heads, piece, side_block, side_at, experts):
    narrow = len(x_blocks)
    rows, width = x_blocks[0].shape
    group = rows * narrow
    stat_rows = -(-(narrow + 1) // 8) * 8
    head_shape = jax.ShapeDtypeStruct((own_heads, group, HEAD_DIM), BF)
    outs = (
        [jax.ShapeDtypeStruct((narrow, rows, width), BF)]
        + [head_shape] * 3
        + [shape((group, own_heads * HEAD_DIM), BF)]
        + [jax.ShapeDtypeStruct((own_heads, 1, group), F32)]
        + [shape((8, width), F32), shape((stat_rows, 128), F32), shape((width, 128), BF)]
    )

    def body(where_ref, *refs):
        attention_kernel(
            narrow, own_heads, piece, side_block, side_at, experts,
            where_ref, refs[:narrow], *refs[narrow:],
        )

    ins = [where, *x_blocks, weights]
    near = range(narrow + 1)
    return run(body, outs, ins, "attention_forward", first_smem=True, close=near, close_outs=(4,))


def gelu_pieces(z):
    size = jnp.abs(z)
    fall = jnp.exp(z * z * -0.5)
    t = 1.0 / (1.0 + size * (0.3275911 * 0.7071067811865476))
    tail = 1.061405429 * 0.5
    for term in (-1.453152027, 1.421413741, -0.284496736, 0.254829592):
        tail = tail * t + term * 0.5
    tail = tail * t * fall
    upper = jnp.where(z < 0.0, tail, 1.0 - tail)
    return upper, z * fall * 0.3989422804014327


def expert_share(x, dy, w_in, w_back, act_ref, dz_ref, at):
    z, low = None, 0
    for cut in w_in:
        term = dot(x[:, low : low + cut.shape[0]], cut[...])
        z = term if z is None else z + term
        low += cut.shape[0]
    upper, bump = gelu_pieces(z)
    act = (z * upper).astype(BF)
    act_ref[at] = act
    du = dot_nt(dy, w_back[...])
    dz = (du * (upper + bump)).astype(BF)
    dz_ref[at] = dz
    dx = [dot_nt(dz, cut[...]) for cut in w_in]
    dx = dx[0] if len(dx) == 1 else jnp.concatenate(dx, axis=1)
    return dx, jnp.sum(act.astype(F32) * du, axis=1, keepdims=True)


def row_gate(x, vectors):
    score = jnp.sum(x.astype(F32) * vectors[4:5], axis=1, keepdims=True)
    return 1.0 / (1.0 + jnp.exp(-score))


STEP = 256


def expert(info, xs, gs, vectors, ins, backs):
    count, width = xs[0].shape
    hidden = backs[0].shape[0]
    shares, cuts = len(backs), len(ins[0])
    blocks = [(half, start) for half in range(2) for start in range(0, count, STEP)]

    def body(info_ref, vec, *refs):
        x_refs, w1_first, w2_first, g_refs = refs[:2], refs[2 : 2 + cuts], refs[2 + cuts], refs[3 + cuts : 5 + cuts]
        rest, o = refs[5 + cuts : 4 + shares * (cuts + 1)], refs[4 + shares * (cuts + 1) :]
        w1 = [w1_first] + [rest[i * (cuts + 1) : i * (cuts + 1) + cuts] for i in range(shares - 1)]
        w2 = [w2_first] + [rest[i * (cuts + 1) + cuts] for i in range(shares - 1)]
        dx_refs, router, dy, acts, dzs = o[:2], o[2], o[3], o[4 : 4 + shares], o[4 + shares : 4 + 2 * shares]
        back_refs = o[4 + 2 * shares : 3 + 3 * shares]
        dx_acc, score_acc = o[3 + 3 * shares :]
        router_sum = jnp.zeros((1, width), F32)
        for i in range(shares):
            for number, (half, start) in enumerate(blocks):
                at = pl.ds(start, min(STEP, count))
                rows = x_refs[half][at]
                if i == 0:
                    gate = row_gate(rows, vec)
                    dy[half, at] = (gate * g_refs[half][at].astype(F32)).astype(BF)
                    dy.push(number)
                dx, score = expert_share(
                    rows, dy.ref[half, at], w1[i], w2[i], acts[i].ref.at[half], dzs[i].ref.at[half], at
                )
                acts[i].push(number)
                dzs[i].push(number)
                if i > 0:
                    dx, score = dx + dx_acc[half, at], score + score_acc[half, at]
                if i < shares - 1:
                    dx_acc[half, at], score_acc[half, at] = dx, score
                else:
                    gate = row_gate(rows, vec)
                    dlogit = (score + info_ref[0:1, 1:2] * gate) * (1.0 - gate)
                    router_sum = router_sum + jnp.sum(
                        rows.astype(F32) * dlogit, axis=0, keepdims=True
                    )
                    dx_refs[half][at] = (dx + dlogit * vec[4:5]).astype(dx_refs[half].dtype)
                    if start + STEP >= count:
                        dx_refs[half].push()
            if i < shares - 1:
                act, grad = acts[i].ref, dy.ref
                back_refs[i][...] = (dot_tn(act[0], grad[0]) + dot_tn(act[1], grad[1])).astype(BF)
                back_refs[i].push()
        router[...] = router_sum

    outs = [shape((count, width), BF), shape((count, width), F32), shape((1, width), F32)]
    outs += [shape((2, count, width), BF)] + [shape((2, count, hidden), BF)] * (2 * shares)
    parts = len(outs)
    outs += [shape((hidden, width), BF)] * (shares - 1)
    cut = [(half, pl.ds(start, min(STEP, count))) for half, start in blocks]
    operands = [info, vectors, *xs, *ins[0], backs[0], *gs]
    for i in range(1, shares):
        operands += [*ins[i], backs[i]]
    scratch = [pltpu.VMEM((2, count, width), F32), pltpu.VMEM((2, count, 1), F32)]
    pieces = {i: cut for i in range(3, parts)}
    near = (2, 3)
    res = run(body, outs, operands, "expert", scratch, pieces=pieces, close=near, close_outs=(0, 1))
    res = list(res)
    acts, dzs = res[4 : 4 + shares], res[4 + shares : parts]
    return res[0], res[1], res[2], res[3], acts, dzs, res[parts:]


def partner_terms(xs, acts, dzs, backs, ends):
    shares = len(acts)
    count, width, hidden = shares - 1, xs[0].shape[1], acts[0].shape[2]
    cuts = [slice(*pair) for pair in zip(ends, ends[1:])]

    def body(*refs):
        x_refs, dz, act, back = refs[:2], refs[2 : 2 + count], refs[2 + count :][:shares], refs[2 + count + shares :][:shares]
        y_refs, outs = refs[2 + count + 2 * shares :][:2], list(refs[4 + count + 2 * shares :])
        for at in cuts:
            for i in range(count):
                out = outs.pop(0)
                term = dot_tn(x_refs[0][:, at], dz[i][0]) + dot_tn(x_refs[1][:, at], dz[i][1])
                out[...] = term.astype(BF)
                out.push()
        for half, out in enumerate(y_refs):
            total = dot(act[0][half], back[0][...])
            for i in range(1, shares):
                total = total + dot(act[i][half], back[i][...])
            out[...] = total.astype(out.dtype)
            out.push()

    outs = [shape(xs[0].shape, BF), shape(xs[0].shape, F32)]
    outs += [shape((at.stop - at.start, hidden), BF) for at in cuts for _ in range(count)]
    res = run(body, outs, [*xs, *dzs[:-1], *acts, *backs], "partner_terms")
    return res[0], res[1], [list(res[i : i + count]) for i in range(2, len(outs), count)]


def own_terms(xs, dy, act, dz):
    def body(act, dy, x_a, x_b, dz, own_back, own_in):
        own_back[...] = dot_tn(act[0], dy[0]) + dot_tn(act[1], dy[1])
        own_back.push()
        own_in[...] = dot_tn(x_a[...], dz[0]) + dot_tn(x_b[...], dz[1])

    width, hidden = xs[0].shape[1], act.shape[2]
    outs = [shape((hidden, width), F32), shape((width, hidden), F32)]
    return run(body, outs, [act, dy, *xs, dz], "own_terms")


def attention_back_kernel(
    narrow, own_heads, columns, seg_lane,
    where_ref, dr_refs, out_w_ref, q_ref, k_ref, v_ref, lse_ref, stat_ref, att_ref,
    dqkv_ref, out_terms_ref,
    dr_all, da, dk_acc, dv_acc,
):
    rows, width = dr_refs[0].shape
    group = rows * narrow
    own_width = own_heads * HEAD_DIM
    at_narrow = where_ref[1]
    for place in range(narrow):
        dr_all[at_narrow ^ place] = dr_refs[place][...]
    dqkv = dqkv_ref.ref
    segs = [stat_ref[i : i + 1, seg_lane : seg_lane + 1] for i in range(narrow)]
    mask = earlier_keys(rows)
    dqkv[:, columns - 128 :] = jnp.zeros((group, 128), BF)
    for block in range(narrow):
        at = pl.ds(block * rows, rows)
        d_att = dot_nt(dr_all[block], out_w_ref[...]).astype(BF)
        for head in range(own_heads):
            da[head, at] = d_att[:, head * HEAD_DIM : (head + 1) * HEAD_DIM]
    for head in range(own_heads):
        low, high = head * HEAD_DIM, (head + 1) * HEAD_DIM
        for block in reversed(range(narrow)):
            at = pl.ds(block * rows, rows)
            query, d_att, lse = q_ref[head, at], da[head, at], lse_ref[head, :, at]
            probs, d_probs, delta = [], [], None
            for other in range(block + 1):
                keys = pl.ds(other * rows, rows)
                score = dot_nt(k_ref[head, keys], query)
                if other == block:
                    prob = jnp.where(mask, jnp.exp(score - lse), 0.0)
                else:
                    prob = jnp.exp(
                        score - (lse + jnp.where(segs[block] == segs[other], 0.0, -FLOOR_SCORE))
                    )
                d_prob = dot_nt(v_ref[head, keys], d_att)
                part = jnp.sum(prob * d_prob, axis=0, keepdims=True)
                delta = part if delta is None else delta + part
                probs.append(prob)
                d_probs.append(d_prob)
            dq = None
            for other in range(block + 1):
                keys = pl.ds(other * rows, rows)
                d_score = (probs[other] * (d_probs[other] - delta)).astype(BF)
                term = dot_tn(d_score, k_ref[head, keys])
                dq = term if dq is None else dq + term
                dk = dot(d_score, query)
                dv = dot(probs[other].astype(BF), d_att)
                if block == narrow - 1:
                    dk_acc[keys] = dk
                    dv_acc[keys] = dv
                else:
                    dk_acc[keys] += dk
                    dv_acc[keys] += dv
            dqkv[at, low:high] = (dq * SCALE_FACTOR).astype(BF)
        dqkv[:, own_width + low : own_width + high] = dk_acc[...].astype(BF)
        dqkv[:, 2 * own_width + low : 2 * own_width + high] = dv_acc[...].astype(BF)
    dqkv_ref.push()
    out_terms_ref[...] = dot_tn(att_ref[...], dr_all[...].reshape(group, width)).astype(BF)


def attention_back(where, dr_blocks, out_w, q, k, v, lse, stat, att, columns, seg_lane):
    narrow = len(dr_blocks)
    rows, width = dr_blocks[0].shape
    group = rows * narrow
    own_heads = q.shape[0]
    outs = [shape((group, columns), BF), shape((own_heads * HEAD_DIM, width), BF)]

    def body(where_ref, *refs):
        attention_back_kernel(
            narrow, own_heads, columns, seg_lane, where_ref, refs[:narrow], *refs[narrow:]
        )

    scratch = [
        pltpu.VMEM((narrow, rows, width), BF),
        pltpu.VMEM((own_heads, group, HEAD_DIM), BF),
        pltpu.VMEM((group, HEAD_DIM), F32),
        pltpu.VMEM((group, HEAD_DIM), F32),
    ]
    ins = [where, *dr_blocks, out_w, q, k, v, lse, stat, att]
    near = range(narrow)
    return run(body, outs, ins, "attention_backward", scratch, first_smem=True, close=near)


def weight_terms(where, dqkv, first, weights, info, sums, routers, narrow, side_block, side_at):
    group, columns = dqkv.shape
    width = weights.shape[0]
    rows = group // narrow

    def body(where_ref, dqkv_ref, first_ref, weights_ref, info_ref, sums_ref, router,
             terms_ref, *parts):
        first = first_ref[...].reshape(group, width)
        side = weights_ref[:, side_block * 128 : side_block * 128 + 128].astype(F32)
        gain, bias = side[:, side_at : side_at + 1], side[:, side_at + 1 : side_at + 2]
        gain_sum, bias_sum, last = None, None, None
        for block in range(columns // 128):
            cut = slice(block * 128, block * 128 + 128)
            term = dot_tn(first, dqkv_ref[:, cut])
            weight = weights_ref[:, cut].astype(F32)
            total = jnp.sum(dqkv_ref[:, cut].astype(F32), axis=0, keepdims=True)
            gain_part, bias_part = weight * (term - bias * total), weight * total
            gain_sum = gain_part if gain_sum is None else gain_sum + gain_part
            bias_sum = bias_part if bias_sum is None else bias_sum + bias_part
            if block == side_block:
                last = term
            else:
                terms_ref[:, cut] = term.astype(BF)
        gain_sum = jnp.sum(gain_sum, axis=1, keepdims=True) / gain
        bias_sum = jnp.sum(bias_sum, axis=1, keepdims=True)
        which = lax.broadcasted_iota(jnp.int32, (8, width), 0)
        extra = jnp.where(which == 4, router[...], sums_ref[...])
        balance = info_ref[0:1, 0:1]
        high = balance.astype(BF).astype(F32)
        extra = jnp.where(which == 5, high, jnp.where(which == 6, balance - high, extra))
        lane = lax.broadcasted_iota(jnp.int32, (8, 128), 1)
        which = lax.broadcasted_iota(jnp.int32, (8, 128), 0)
        spread = jnp.where(lane == side_at + which, 1.0, 0.0)
        lane = lax.broadcasted_iota(jnp.int32, (width, 128), 1)
        last = jnp.where(lane == side_at, gain_sum, jnp.where(lane == side_at + 1, bias_sum, last))
        last = last + dot_tn(extra, spread)
        terms_ref[:, side_block * 128 : side_block * 128 + 128] = last.astype(BF)
        terms_ref.push()
        for place in reversed(range(narrow)):
            at = pl.ds(pl.multiple_of((where_ref[1] ^ place) * rows, rows), rows)
            parts[place][...] = dot_nt(dqkv_ref[at], weights_ref[...]).astype(parts[place].dtype)
            parts[place].push()

    outs = [shape((width, columns), BF)]
    outs += [shape((rows, width), BF if i & 1 else F32) for i in range(narrow)]
    ins = [where, dqkv, first, weights, info, sums, *routers]
    res = run(body, outs, ins, "weight_terms", first_smem=True)
    return res[0], list(res[1:])


def sum_terms(owns, cuts):
    counts = [len(cut) for cut in cuts]

    def body(*refs):
        sources, rest = refs[: len(owns)], list(refs[len(owns) :])
        outs = rest[sum(counts) :]
        for source, count, out in zip(sources, counts, outs):
            low = 0
            for _ in range(count):
                ref = rest.pop(0)
                at = pl.ds(low, ref.shape[0])
                out[at] = source[at] + ref[...].astype(F32)
                low += ref.shape[0]
            out.push()

    outs = [shape(value.shape, F32) for value in owns]
    return run(body, outs, [*owns, *[v for cut in cuts for v in cut]], "sum_terms")


def turned(row):
    count = row.shape[1]
    at = lax.broadcasted_iota(jnp.int32, (count, count), 0)
    other = lax.broadcasted_iota(jnp.int32, (count, count), 1)
    return jnp.sum(jnp.where(at == other, row, 0.0), axis=1, keepdims=True)


def pack(weights, vectors, w_router, routing, segments, wide, narrow, own_width, columns):
    piece, width = weights[0].shape
    experts = w_router.shape[1]
    rows = routing.shape[0]
    start = 3 * own_width

    def body(wq, wk, wv, va, vb, vc, vd, wr, route, segment, sent, held):
        held[...] = jnp.zeros_like(held)
        ids = lax.broadcasted_iota(jnp.int32, (experts, rows), 0)
        counts = jnp.sum(jnp.where(route[...] == ids, 1.0, 0.0), axis=1, keepdims=True)
        sides = [turned(ref[...]) for ref in (va, vb, vc, vd)]
        sides += [turned(wr[i : i + 1]) for i in range(experts)]
        sides += [counts[i : i + 1] for i in range(experts)]
        sides += [segment[0:1, 0:1].astype(F32)]
        lane = lax.broadcasted_iota(jnp.int32, (piece, 128), 1)
        block = jnp.zeros((piece, 128), F32)
        for i, value in enumerate(sides):
            block = jnp.where(lane == start % 128 + i, value, block)
        for n in range(narrow):
            held[n, :, columns - 128 :] = block
            low, high = n * own_width, min((n + 1) * own_width, width)
            for i, ref in enumerate((wq, wk, wv)):
                if low < high:
                    held[n, :, i * own_width : i * own_width + high - low] = ref[:, low:high]

        def send(w, carry):
            for n in range(narrow):
                sent[w * narrow + n] = held[n].astype(BF)
            return carry

        lax.fori_loop(0, wide, send, 0)

    outs = [shape((wide * narrow, piece, columns), BF)]
    ins = [*weights, *[v.reshape(1, piece) for v in vectors], w_router.T]
    ins += [routing.reshape(1, rows), segments.reshape(1, rows)]
    return run(body, outs, ins, "pack", [pltpu.VMEM((narrow, piece, columns), F32)])[0]


def cast_weights(w_in, w_back, cut):
    def body(first, second, upper, lower, back):
        upper[...] = first[:cut].astype(BF)
        upper.push()
        lower[...] = first[cut:].astype(BF)
        lower.push()
        back[...] = second[...].astype(BF)

    width, hidden = w_in.shape
    outs = [shape((cut, hidden), BF), shape((width - cut, hidden), BF), shape(w_back.shape, BF)]
    return run(body, outs, [w_in, w_back], "cast_weights")


def place_cotangent(routing, cotangent, experts, capacity, piece, copies):
    rows, width = cotangent.shape
    slots = experts * capacity

    def body(route, g, piece_ref, placing, moved, tiled):
        for i in range(copies):
            tiled[i] = piece_ref[...]
        tiled.push()
        ids = lax.broadcasted_iota(jnp.int32, (rows, experts), 1)
        expert = turned(route[...].astype(F32)).astype(jnp.int32)
        hot = jnp.where(expert == ids, 1.0, 0.0)
        row = lax.broadcasted_iota(jnp.int32, (rows, rows), 0)
        column = lax.broadcasted_iota(jnp.int32, (rows, rows), 1)
        before = dot(jnp.where(row > column, 1.0, 0.0).astype(BF), hot.astype(BF))
        slot = jnp.sum(before * hot, axis=1, keepdims=True).astype(jnp.int32)
        target = expert * capacity + slot
        place = lax.broadcasted_iota(jnp.int32, (rows, slots), 1)
        spot = jnp.where(place == target, 1.0, 0.0).astype(BF)
        placing[...] = spot
        moved[...] = dot_tn(spot, g[...]).astype(BF)

    outs = [shape((rows, slots), BF), shape((slots, width), BF), shape((copies, *piece.shape), BF)]
    return run(body, outs, [routing.reshape(1, rows), cotangent, piece], "place_cotangent")


def second_norm(x, halves, vectors, side, stat, placing, routing, where, dims):
    narrow, experts, total, side_at = dims
    rows, width = x.shape
    slots = placing.shape[1]
    count = len(halves)

    def body(where_ref, x_ref, *refs):
        vec, side_ref, stat_ref, placing_ref, route = refs[count : count + 5]
        mixed_ref, moved, gate_ref, info = refs[count + 5 :]
        mixed = x_ref[...].astype(F32)
        for ref in refs[:count]:
            mixed = mixed + ref[...].astype(F32)
        mixed_ref[...] = mixed
        unit, _ = norm_parts(mixed)
        low = (unit * vec[2:3] + vec[3:4]).astype(BF)
        moved[...] = dot_tn(placing_ref[...], low).astype(BF)
        logits = dot(low, side_ref[...])
        lane = lax.broadcasted_iota(jnp.int32, (rows, 128), 1)
        expert = turned(route[...].astype(F32)).astype(jnp.int32)
        chosen = jnp.where(lane - (side_at + 4) == expert, logits, 0.0)
        gate = 1.0 / (1.0 + jnp.exp(-jnp.sum(chosen, axis=1, keepdims=True)))
        gate_ref[...] = gate
        first = side_at + 4 + experts
        sums = jnp.sum(jnp.where(lane - first == expert, gate, 0.0), axis=0, keepdims=True)
        lane = lax.broadcasted_iota(jnp.int32, (1, 128), 1)
        counts = stat_ref[narrow : narrow + 1]
        deviation = (counts - float(total) / experts) * (experts / float(total))
        kept = (lane >= first) & (lane < first + experts)
        balance = experts / float(total) * jnp.sum(
            jnp.where(kept, deviation * sums, 0.0), axis=1, keepdims=True
        )
        own = jnp.sum(
            jnp.where(lane == first + where_ref[0], deviation, 0.0), axis=1, keepdims=True
        )
        core = jnp.where(where_ref[1] % 2 == 0, BALANCE_WEIGHT * (experts / float(total)), 0.0)
        info[...] = jnp.where(lane == 0, balance, own * core) + jnp.zeros((8, 128), F32)

    outs = [shape((rows, width), F32), shape((slots, width), BF), shape((rows, 1), F32)]
    outs.append(shape((8, 128), F32))
    ins = [where, x, *halves, vectors, side, stat, placing, routing.reshape(1, rows)]
    near = range(1, 1 + count)
    return run(body, outs, ins, "second_norm", first_smem=True, close=near)


def second_back(returned, placing, mixed, cotangent, vectors):
    rows, width = mixed.shape

    def body(ret, placing_ref, mixed_ref, g, vec, dr_ref, low_ref, sums):
        incoming = dot(placing_ref[...], ret[...])
        unit, inverse = norm_parts(mixed_ref[...])
        gain = jnp.sum(incoming * unit, axis=0, keepdims=True)
        bias = jnp.sum(incoming, axis=0, keepdims=True)
        dr = g[...].astype(F32) + norm_back(incoming, unit, inverse, vec[2:3])
        dr_ref[...] = dr
        low_ref[...] = dr.astype(BF)
        which = lax.broadcasted_iota(jnp.int32, (8, width), 0)
        sums[...] = jnp.where(which == 2, gain, jnp.where(which == 3, bias, 0.0))

    outs = [shape((rows, width), F32), shape((rows, width), BF), shape((8, width), F32)]
    ins = [returned, placing, mixed, cotangent, vectors]
    return run(body, outs, ins, "second_back", close=(0,), close_outs=(1,))


def finish_rows(returned, placing, mixed, gates):
    def body(ret, placing_ref, mixed_ref, gate, out):
        out[...] = mixed_ref[...] + gate[...] * dot(placing_ref[...], ret[...])

    ins = [returned, placing, mixed, gates]
    return run(body, [shape(mixed.shape, F32)], ins, "finish_rows")[0]


def first_back(halves, x, dr, vectors):
    count = len(halves)

    def body(*refs):
        x_ref, dr_ref, vec, out = refs[count:]
        incoming = refs[0][...].astype(F32)
        for ref in refs[1:count]:
            incoming = incoming + ref[...].astype(F32)
        unit, inverse = norm_parts(x_ref[...].astype(F32))
        out[...] = dr_ref[...] + norm_back(incoming, unit, inverse, vec[0:1])

    return run(body, [shape(x.shape, F32)], [*halves, x, dr, vectors], "first_back")[0]


def unpack(came, wide, narrow, own_width, width, experts):
    piece, columns = came.shape[1:]
    start = 3 * own_width
    side_block, side_at = start // 128, start % 128

    def as_row(column):
        row = lax.broadcasted_iota(jnp.int32, (piece, piece), 0)
        other = lax.broadcasted_iota(jnp.int32, (piece, piece), 1)
        return jnp.sum(jnp.where(row == other, column, 0.0), axis=0, keepdims=True)

    def body(came_ref, gq, gk, gv, va, vb, vc, vd, gr, balance):
        every = jnp.zeros((piece, 128), F32)
        routers = []
        for n in range(narrow):
            total = jnp.zeros((piece, columns), F32)
            for w in range(wide):
                total = total + came_ref[w * narrow + n].astype(F32)
            every = every + total[:, side_block * 128 : side_block * 128 + 128]
            low, high = n * own_width, min((n + 1) * own_width, width)
            if low < high:
                for i, ref in enumerate((gq, gk, gv)):
                    ref[:, low:high] = total[:, i * own_width : i * own_width + high - low]
        for w in range(wide):
            column = jnp.zeros((piece, 1), F32)
            at = start + 4
            for n in range(narrow):
                column = column + came_ref[w * narrow + n, :, at : at + 1].astype(F32)
            gr[w : w + 1] = as_row(column)
        for i, ref in enumerate((va, vb, vc, vd)):
            ref[...] = as_row(every[:, side_at + i : side_at + i + 1])
        balance[...] = every[0:1, side_at + 5 : side_at + 6] + every[0:1, side_at + 6 : side_at + 7]

    outs = [shape((piece, width), F32)] * 3 + [shape((1, piece), F32)] * 4
    outs += [shape((experts, piece), F32), shape((1, 1), F32)]
    return run(body, outs, [came], "unpack", close=(0,))


def local(
    hidden_in,
    segments,
    routing,
    first_gain,
    first_bias,
    second_gain,
    second_bias,
    w_query,
    w_key,
    w_value,
    w_out,
    w_router,
    w_in,
    w_back,
    cotangent,
):
    wide = lax.axis_size("wide")
    narrow = lax.axis_size("narrow")
    devices = wide * narrow
    rows, width = hidden_in.shape
    piece = w_query.shape[0]
    experts = w_router.shape[1]
    capacity = max(2, 2 * rows // experts)
    total = rows * devices
    own_heads = -(-HEADS // narrow)
    own_width = own_heads * HEAD_DIM
    aligned = own_width * narrow == width and own_width == piece * wide
    at_wide = lax.axis_index("wide")
    at_narrow = lax.axis_index("narrow")
    where = jnp.stack([at_wide, at_narrow]).astype(jnp.int32)
    bits = [1 << level for level in range(narrow.bit_length() - 1)]
    core_bit, chip_bits = bits[:1], bits[1:]
    side_start = 3 * own_width
    side_block, side_at = side_start // 128, side_start % 128
    seg_lane = side_at + 4 + 2 * experts
    assert seg_lane < 128
    columns = side_block * 128 + 128
    gate = lax.optimization_barrier

    def swap(values, bit):
        return lax.ppermute(values, "narrow", [(i, i ^ bit) for i in range(narrow)])

    def gather_blocks(block, over):
        blocks = {0: block}
        for bit in reversed(over):
            for place in list(blocks):
                blocks[place ^ bit] = swap(blocks[place], bit)
        return blocks

    def reduce_blocks(blocks, over):
        blocks = dict(blocks)
        for bit in over:
            for place in sorted(blocks, reverse=True):
                if place & bit:
                    moved = swap(blocks.pop(place).astype(BF), bit).astype(F32)
                    blocks[place ^ bit] = blocks[place ^ bit] + moved
        return blocks

    def exchange(values):
        values = values.reshape(experts, capacity, width)
        return to_all(values, "wide").reshape(experts * capacity, width)

    sent = pack(
        [w_query, w_key, w_value], [first_gain, first_bias, second_gain, second_bias],
        w_router, routing, segments, wide, narrow, own_width, columns,
    )
    x_blocks = gather_blocks(hidden_in, chip_bits)
    out_low = w_out.astype(BF)
    if aligned:
        out_low = lax.ppermute(
            out_low, BOTH, [(n * wide + j, j * narrow + n) for n in range(narrow) for j in range(wide)]
        )
    *in_low, back_low = cast_weights(w_in[0], w_back[0], width // 3)
    sent, out_low, where = gate((sent, out_low, where))
    weights = to_all(sent, BOTH).reshape(width, columns)
    for place in list(x_blocks):
        x_blocks[place ^ 1] = swap(x_blocks[place], 1)
    partners = [i for i in range(2, narrow, 2)]
    in_upper = [swap(in_low[0], i) for i in partners]
    placing, g_moved, out_tiled = place_cotangent(
        routing, cotangent, experts, capacity, out_low, wide
    )
    weights, in_low, back_low, g_moved, in_upper, out_tiled = gate(
        (weights, in_low, back_low, g_moved, in_upper, out_tiled)
    )
    back_came = [swap(back_low, i) for i in partners]
    if aligned:
        out_w = to_all(out_tiled, "wide").reshape(own_width, width)
    else:
        all_out = lax.all_gather(out_low, BOTH, axis=0, tiled=True)
        all_out = jnp.pad(all_out, ((0, own_width * narrow - width), (0, 0)))
        out_w = lax.dynamic_slice_in_dim(all_out, at_narrow * own_width, own_width, axis=0)

    x_list = [x_blocks[i] for i in range(narrow)]
    first, q, k, v, att, lse, vectors, stat, side = attention(
        where, x_list, weights, own_heads, piece, side_block, side_at, experts
    )
    att, g_moved = gate((att, g_moved))
    g_own = exchange(g_moved)
    parts = project(where, att, out_w, narrow)
    halves = reduce_blocks({i: parts[i] for i in range(narrow)}, core_bit)
    halves, back_came = gate((halves, back_came))
    halves = {i: swap(halves[i].astype(BF), i) if i else halves[i] for i in sorted(halves)}

    halves, g_own, in_low = gate((halves, g_own, in_low))
    in_lower = [swap(in_low[1], i) for i in partners]
    mixed, x_moved, gates, info = second_norm(
        hidden_in, [halves[i] for i in sorted(halves)], vectors, side, stat, placing, routing,
        where, (narrow, experts, total, side_at),
    )
    g_other = swap(g_own, 1)
    x_own = exchange(x_moved)
    x_own, in_lower = gate((x_own, in_lower))
    x_other = swap(x_own, 1)

    ins = [list(pair) for pair in zip(in_upper, in_lower)] + [in_low]
    backs = [*back_came, back_low]
    xs = [x_other, x_own]
    dx_o, dx_s, router, dy, acts, dzs, far_back = expert(info, xs, [g_other, g_own], vectors, ins, backs)

    def cross(cut):
        return [swap(value, place) for value, place in zip(cut, partners)]

    dx_sum = (dx_s + swap(dx_o, 1).astype(F32)).astype(BF)
    d_returned = exchange(dx_sum)
    acts, dx_sum = gate((acts, dx_sum))
    far_back = cross(far_back)
    ends = (0, width // 6, width * 2 // 3, width)
    y_o, y_s, made = partner_terms(xs, acts, dzs, backs, ends)
    own_back, own_in = own_terms(xs, dy, acts[-1], dzs[-1])
    made, far_back, own_back, own_in = gate((made, far_back, own_back, own_in))
    crossed = [cross(made[0])]
    y_o = swap(y_o, 1)
    d_mixed, d_mixed_low, sums = second_back(d_returned, placing, mixed, cotangent, vectors)
    d_mixed_low, y_s, y_o, crossed = gate((d_mixed_low, y_s, y_o, crossed))
    y_sum = (y_s + y_o.astype(F32)).astype(BF)
    returned = exchange(y_sum)
    dr_blocks = gather_blocks(d_mixed_low, chip_bits)
    for place in list(dr_blocks):
        dr_blocks[place ^ 1] = swap(dr_blocks[place], 1)
    dr_blocks, made = gate((dr_blocks, made))
    crossed.append(cross(made[1]))
    dr_list = [dr_blocks[i] for i in range(narrow)]

    d_qkv, terms_out = attention_back(
        where, dr_list, out_w, q, k, v, lse, stat, att, columns, seg_lane
    )
    d_qkv, crossed, terms_out, returned, made = gate((d_qkv, crossed, terms_out, returned, made))
    last_cross = cross(made[2])
    if aligned:
        terms_out = to_all(terms_out.reshape(wide, piece, width), "wide")
    terms, d_parts = weight_terms(
        where, d_qkv, first, weights, info, sums, [router], narrow, side_block, side_at
    )

    tied = (terms, d_parts, returned, terms_out, last_cross)
    terms, d_parts, returned, terms_out, last_cross = gate(tied)
    crossed.append(last_cross)
    terms = to_all(terms.reshape(devices, piece, columns), BOTH)
    d_halves = reduce_blocks({i: d_parts[i] for i in range(narrow)}, core_bit)
    d_halves = [swap(d_halves[i].astype(BF), i) if i else d_halves[i] for i in sorted(d_halves)]
    if aligned:
        grad_out_w = lax.ppermute(
            jnp.sum(terms_out.astype(F32), axis=0),
            BOTH,
            [(j * narrow + n, n * wide + j) for n in range(narrow) for j in range(wide)],
        )
    else:
        spread = jnp.zeros((own_width * narrow, width), F32)
        spread = lax.dynamic_update_slice_in_dim(
            spread, terms_out.astype(F32), at_narrow * own_width, axis=0
        )
        grad_out_w = lax.psum_scatter(spread[:width], BOTH, scatter_dimension=0, tiled=True)
    block_out = finish_rows(returned, placing, mixed, gates)
    grad_hidden = first_back(d_halves, hidden_in, d_mixed, vectors)
    back_terms, in_terms = sum_terms([own_back, own_in], [far_back[:1], [cut[0] for cut in crossed]])
    for i in range(1, len(partners)):
        back_terms = back_terms + far_back[i].astype(F32)
        in_terms = in_terms + jnp.concatenate([cut[i] for cut in crossed], axis=0).astype(F32)

    done = unpack(terms, wide, narrow, own_width, width, experts)
    return (
        block_out,
        done[8].reshape(()),
        grad_hidden,
        *[done[i].reshape(piece) for i in range(3, 7)],
        *done[:3],
        grad_out_w,
        done[7].T,
        in_terms[None],
        back_terms[None],
    )


def solution(mesh):
    rows = P(BOTH, None)
    vector = P(BOTH)
    placed = (rows, vector, rows) + (vector,) * 4 + (rows,) * 5
    expert_specs = (P("wide", None, "narrow"), P("wide", "narrow", None))
    return jax.shard_map(
        local,
        mesh=mesh,
        in_specs=placed + expert_specs + (rows,),
        out_specs=(rows, P(), rows) + (vector,) * 4 + (rows,) * 5 + expert_specs,
        check_vma=False,
    )
```

```python
import jax
import jax.numpy as jnp
from jax import lax
from jax.experimental import pallas as pl
from jax.experimental.pallas import tpu as pltpu
from jax.sharding import PartitionSpec as P

HEADS = 12
HEAD_DIM = 64
EPSILON = 1e-05
FLOOR_SCORE = -1e30
SCALE_FACTOR = 0.125
BALANCE_WEIGHT = 0.01
BOTH = ("wide", "narrow")
BF = jnp.bfloat16
F32 = jnp.float32


def dot(left, right):
    return jnp.dot(left, right, preferred_element_type=F32)


def dot_nt(left, right):
    return lax.dot_general(left, right, (((1,), (1,)), ((), ())), preferred_element_type=F32)


def dot_tn(left, right):
    return lax.dot_general(left, right, (((0,), (0,)), ((), ())), preferred_element_type=F32)


def norm_parts(values):
    centered = values - jnp.mean(values, axis=1, keepdims=True)
    inverse = lax.rsqrt(jnp.mean(centered * centered, axis=1, keepdims=True) + EPSILON)
    return centered * inverse, inverse


def norm_back(incoming, unit, inverse, gain):
    scaled = incoming * gain
    return inverse * (
        scaled
        - jnp.mean(scaled, axis=1, keepdims=True)
        - unit * jnp.mean(scaled * unit, axis=1, keepdims=True)
    )


def to_all(values, axes):
    return lax.all_to_all(values, axes, split_axis=0, concat_axis=0, tiled=True)


SMALL = pl.CostEstimate(flops=1000, bytes_accessed=1000, transcendentals=0)
LARGE = pl.CostEstimate(flops=int(2.5e10), bytes_accessed=int(3e7), transcendentals=0)
FILLERS = ("place_cotangent", "cast_weights")


class Held:
    def __init__(self, ref, copies, fetched):
        self.ref, self.copies = ref, copies
        self.waiting = list(range(len(copies))) if fetched else []
        self.started = set(self.waiting)

    def get(self):
        for i in self.waiting:
            self.copies[i].wait()
        self.waiting = []
        return self.ref

    def push(self, part=None):
        for i in range(len(self.copies)) if part is None else [part]:
            if i not in self.started and i < len(self.copies):
                self.copies[i].start()
                self.waiting.append(i)
                self.started.add(i)

    @property
    def shape(self):
        return self.ref.shape

    @property
    def dtype(self):
        return self.ref.dtype

    def __getitem__(self, at):
        return self.get()[at]

    def __setitem__(self, at, value):
        self.ref[at] = value


def padded(value):
    lanes = -(-value.shape[-1] // 128) * 128
    rows = -(-value.shape[-2] // 16) * 16 if len(value.shape) > 1 else 16
    outer = 1
    for size in value.shape[:-2]:
        outer *= size
    return outer * rows * lanes * jnp.dtype(value.dtype).itemsize


def run(body, outs, ins, name, scratch=(), first_smem=False, pieces=None, close=(), close_outs=(), room=10):
    outs, ins = list(outs), list(ins)
    lead = 1 if first_smem else 0
    fetched, total = len(ins) - lead, len(ins) - lead + len(outs)
    arrays = ins[lead:] + outs
    near = [i in close if i < fetched else i - fetched in close_outs for i in range(total)]
    cuts = [(pieces or {}).get(i - fetched, [()]) for i in range(total)]
    slots, semaphores, used = {}, {}, 0
    for i in range(total):
        if not near[i]:
            slots[i], semaphores[i] = len(slots), used
            used += len(cuts[i])
    buffers = [pltpu.VMEM(arrays[i].shape, arrays[i].dtype) for i in slots]

    def kernel(*refs):
        smem_refs, given = refs[:lead], refs[lead : lead + total]
        own = refs[lead + total : lead + total + len(slots)]
        marks = refs[lead + total + len(slots)]
        held = []
        for i in range(total):
            if near[i]:
                held.append(Held(given[i], [], False))
                continue
            mine = own[slots[i]]
            source, target = (given[i], mine) if i < fetched else (mine, given[i])
            copies = []
            for j, at in enumerate(cuts[i]):
                ends = (source.at[at], target.at[at]) if at else (source, target)
                copies.append(pltpu.make_async_copy(*ends, marks.at[semaphores[i] + j]))
            if i < fetched:
                copies[0].start()
            held.append(Held(mine, copies, i < fetched))
        body(*smem_refs, *held, *refs[lead + total + len(slots) + 1 :])
        for item in held[fetched:]:
            item.push()
        for item in held:
            item.get()

    hbm, vmem = pl.BlockSpec(memory_space=pltpu.HBM), pl.BlockSpec(memory_space=pltpu.VMEM)
    ins = [
        value if i < lead or near[i - lead] else pltpu.with_memory_space_constraint(value, pltpu.HBM)
        for i, value in enumerate(ins)
    ]
    placed = [
        value if near[fetched + i] else pltpu.HBM(value.shape, value.dtype)
        for i, value in enumerate(outs)
    ]
    size = sum(padded(arrays[i]) for i in slots) + sum(padded(value) for value in scratch)
    limit = min(60, size // 2**20 + 1 + room)
    return pl.pallas_call(
        kernel,
        out_shape=placed,
        in_specs=([smem()] if first_smem else []) + [vmem if near[i] else hbm for i in range(fetched)],
        out_specs=[vmem if near[fetched + i] else hbm for i in range(len(outs))],
        scratch_shapes=[*buffers, pltpu.SemaphoreType.DMA((max(1, used),)), *scratch],
        compiler_params=pltpu.CompilerParams(vmem_limit_bytes=limit * 1024 * 1024),
        cost_estimate=LARGE if name in FILLERS else SMALL,
        name=name,
    )(*ins)


def shape(dims, dtype):
    return jax.ShapeDtypeStruct(dims, dtype)


def smem():
    return pl.BlockSpec(memory_space=pltpu.SMEM)


def earlier_keys(size):
    key = lax.broadcasted_iota(jnp.int32, (size, size), 0)
    query = lax.broadcasted_iota(jnp.int32, (size, size), 1)
    return key <= query


def attention_kernel(
    narrow, own_heads, piece, side_block, side_at, experts,
    where_ref, x_refs, weights_ref,
    first_ref, q_ref, k_ref, v_ref, att_ref, lse_ref, rows_ref, stat_ref, side_ref,
):
    rows, width = x_refs[0].shape
    at_wide, at_narrow = where_ref[0], where_ref[1]
    side = weights_ref[:, side_block * 128 : side_block * 128 + 128]
    side_ref[...] = side
    lane = lax.broadcasted_iota(jnp.int32, (8, 128), 1)
    which = lax.broadcasted_iota(jnp.int32, (8, 128), 0)
    wanted = jnp.where(which < 4, side_at + which, side_at + 4 + at_wide)
    pick = jnp.where(lane == wanted, 1.0, 0.0)
    vectors = dot_nt(pick, side.astype(F32))
    rows_ref[...] = vectors
    stat_rows = stat_ref.shape[0]
    column = lax.broadcasted_iota(jnp.int32, (stat_rows, width), 1)
    which = lax.broadcasted_iota(jnp.int32, (stat_rows, width), 0)
    segment_row = (at_wide * narrow + which) * piece
    wanted = jnp.where(which < narrow, segment_row, column - lax.rem(column, piece))
    stat = dot(jnp.where(column == wanted, 1.0, 0.0), side.astype(F32))
    stat_ref[...] = stat
    seg_lane = side_at + 4 + 2 * experts
    segs = [stat[i : i + 1, seg_lane : seg_lane + 1] for i in range(narrow)]
    gain, bias = vectors[0:1], vectors[1:2]
    for place in range(narrow):
        unit, _ = norm_parts(x_refs[place][...].astype(F32))
        first_ref[at_narrow ^ place] = (unit * gain + bias).astype(BF)
    first_ref.push()
    own_width = own_heads * HEAD_DIM
    for block in range(narrow):
        at = pl.ds(block * rows, rows)
        qkv = dot(first_ref.ref[block], weights_ref[...])
        for head in range(own_heads):
            low, high = head * HEAD_DIM, (head + 1) * HEAD_DIM
            q_ref[head, at] = (qkv[:, low:high].astype(BF).astype(F32) * SCALE_FACTOR).astype(BF)
            k_ref[head, at] = qkv[:, own_width + low : own_width + high].astype(BF)
            v_ref[head, at] = qkv[:, 2 * own_width + low : 2 * own_width + high].astype(BF)
    for ref in (q_ref, k_ref, v_ref):
        ref.push()
    mask = earlier_keys(rows)
    for head in range(own_heads):
        for block in range(narrow):
            at = pl.ds(block * rows, rows)
            query = q_ref.ref[head, at]
            scores = []
            for other in range(block + 1):
                score = dot_nt(k_ref.ref[head, pl.ds(other * rows, rows)], query)
                if other == block:
                    score = jnp.where(mask, score, FLOOR_SCORE)
                else:
                    score = score + jnp.where(segs[block] == segs[other], 0.0, FLOOR_SCORE)
                scores.append(score)
            top = scores[0].max(axis=0, keepdims=True)
            for score in scores[1:]:
                top = jnp.maximum(top, score.max(axis=0, keepdims=True))
            exps = [jnp.exp(score - top) for score in scores]
            total = exps[0].sum(axis=0, keepdims=True)
            for value in exps[1:]:
                total = total + value.sum(axis=0, keepdims=True)
            share = 1.0 / total
            att = None
            for other, value in enumerate(exps):
                term = dot_tn((value * share).astype(BF), v_ref.ref[head, pl.ds(other * rows, rows)])
                att = term if att is None else att + term
            att_ref[at, head * HEAD_DIM : (head + 1) * HEAD_DIM] = att.astype(BF)
            lse_ref[head, :, at] = top + jnp.log(total)


def project(where, att, out_w, narrow):
    rows, width = att.shape[0] // narrow, out_w.shape[1]

    def body(where_ref, att_ref, out_w_ref, *parts):
        for place in reversed(range(narrow)):
            at = pl.ds(pl.multiple_of((where_ref[1] ^ place) * rows, rows), rows)
            parts[place][...] = dot(att_ref[at], out_w_ref[...]).astype(parts[place].dtype)
            parts[place].push()

    outs = [shape((rows, width), BF if i & 1 else F32) for i in range(narrow)]
    return run(
        body, outs, [where, att, out_w], "project", first_smem=True, close=(0,), close_outs=range(narrow)
    )


def attention(where, x_blocks, weights, own_heads, piece, side_block, side_at, experts):
    narrow = len(x_blocks)
    rows, width = x_blocks[0].shape
    group = rows * narrow
    stat_rows = -(-(narrow + 1) // 8) * 8
    head_shape = jax.ShapeDtypeStruct((own_heads, group, HEAD_DIM), BF)
    outs = (
        [jax.ShapeDtypeStruct((narrow, rows, width), BF)]
        + [head_shape] * 3
        + [shape((group, own_heads * HEAD_DIM), BF)]
        + [jax.ShapeDtypeStruct((own_heads, 1, group), F32)]
        + [shape((8, width), F32), shape((stat_rows, 128), F32), shape((width, 128), BF)]
    )

    def body(where_ref, *refs):
        attention_kernel(
            narrow, own_heads, piece, side_block, side_at, experts,
            where_ref, refs[:narrow], *refs[narrow:],
        )

    ins = [where, *x_blocks, weights]
    near = range(narrow + 1)
    return run(body, outs, ins, "attention_forward", first_smem=True, close=near, close_outs=(4,))


def gelu_pieces(z):
    size = jnp.abs(z)
    fall = jnp.exp(z * z * -0.5)
    t = 1.0 / (1.0 + size * (0.3275911 * 0.7071067811865476))
    tail = 1.061405429 * 0.5
    for term in (-1.453152027, 1.421413741, -0.284496736, 0.254829592):
        tail = tail * t + term * 0.5
    tail = tail * t * fall
    upper = jnp.where(z < 0.0, tail, 1.0 - tail)
    return upper, z * fall * 0.3989422804014327


def expert_share(x, dy, w_in, w_back, act_ref, dz_ref, at):
    z, low = None, 0
    for cut in w_in:
        term = dot(x[:, low : low + cut.shape[0]], cut[...])
        z = term if z is None else z + term
        low += cut.shape[0]
    upper, bump = gelu_pieces(z)
    act = (z * upper).astype(BF)
    act_ref[at] = act
    du = dot_nt(dy, w_back[...])
    dz = (du * (upper + bump)).astype(BF)
    dz_ref[at] = dz
    dx = [dot_nt(dz, cut[...]) for cut in w_in]
    dx = dx[0] if len(dx) == 1 else jnp.concatenate(dx, axis=1)
    return dx, jnp.sum(act.astype(F32) * du, axis=1, keepdims=True)


def row_gate(x, vectors):
    score = jnp.sum(x.astype(F32) * vectors[4:5], axis=1, keepdims=True)
    return 1.0 / (1.0 + jnp.exp(-score))


STEP = 256


def expert(info, xs, gs, vectors, ins, backs):
    count, width = xs[0].shape
    hidden = backs[0].shape[0]
    shares, cuts = len(backs), len(ins[0])
    blocks = [(half, start) for half in range(2) for start in range(0, count, STEP)]

    def body(info_ref, vec, *refs):
        x_refs, w1_first, w2_first, g_refs = refs[:2], refs[2 : 2 + cuts], refs[2 + cuts], refs[3 + cuts : 5 + cuts]
        rest, o = refs[5 + cuts : 4 + shares * (cuts + 1)], refs[4 + shares * (cuts + 1) :]
        w1 = [w1_first] + [rest[i * (cuts + 1) : i * (cuts + 1) + cuts] for i in range(shares - 1)]
        w2 = [w2_first] + [rest[i * (cuts + 1) + cuts] for i in range(shares - 1)]
        dx_refs, router, dy, acts, dzs = o[:2], o[2], o[3], o[4 : 4 + shares], o[4 + shares : 4 + 2 * shares]
        back_refs = o[4 + 2 * shares : 3 + 3 * shares]
        dx_acc, score_acc = o[3 + 3 * shares :]
        router_sum = jnp.zeros((1, width), F32)
        for i in range(shares):
            for number, (half, start) in enumerate(blocks):
                at = pl.ds(start, min(STEP, count))
                rows = x_refs[half][at]
                if i == 0:
                    gate = row_gate(rows, vec)
                    dy[half, at] = (gate * g_refs[half][at].astype(F32)).astype(BF)
                    dy.push(number)
                dx, score = expert_share(
                    rows, dy.ref[half, at], w1[i], w2[i], acts[i].ref.at[half], dzs[i].ref.at[half], at
                )
                acts[i].push(number)
                dzs[i].push(number)
                if i > 0:
                    dx, score = dx + dx_acc[half, at], score + score_acc[half, at]
                if i < shares - 1:
                    dx_acc[half, at], score_acc[half, at] = dx, score
                else:
                    gate = row_gate(rows, vec)
                    dlogit = (score + info_ref[0:1, 1:2] * gate) * (1.0 - gate)
                    router_sum = router_sum + jnp.sum(
                        rows.astype(F32) * dlogit, axis=0, keepdims=True
                    )
                    dx_refs[half][at] = (dx + dlogit * vec[4:5]).astype(dx_refs[half].dtype)
                    if start + STEP >= count:
                        dx_refs[half].push()
            if i < shares - 1:
                act, grad = acts[i].ref, dy.ref
                back_refs[i][...] = (dot_tn(act[0], grad[0]) + dot_tn(act[1], grad[1])).astype(BF)
                back_refs[i].push()
        router[...] = router_sum

    outs = [shape((count, width), BF), shape((count, width), F32), shape((1, width), F32)]
    outs += [shape((2, count, width), BF)] + [shape((2, count, hidden), BF)] * (2 * shares)
    parts = len(outs)
    outs += [shape((hidden, width), BF)] * (shares - 1)
    cut = [(half, pl.ds(start, min(STEP, count))) for half, start in blocks]
    operands = [info, vectors, *xs, *ins[0], backs[0], *gs]
    for i in range(1, shares):
        operands += [*ins[i], backs[i]]
    scratch = [pltpu.VMEM((2, count, width), F32), pltpu.VMEM((2, count, 1), F32)]
    pieces = {i: cut for i in range(3, parts)}
    near = (2, 3)
    res = run(body, outs, operands, "expert", scratch, pieces=pieces, close=near, close_outs=(0, 1))
    res = list(res)
    acts, dzs = res[4 : 4 + shares], res[4 + shares : parts]
    return res[0], res[1], res[2], res[3], acts, dzs, res[parts:]


def partner_terms(xs, acts, dzs, backs, ends):
    shares = len(acts)
    count, width, hidden = shares - 1, xs[0].shape[1], acts[0].shape[2]
    cuts = [slice(*pair) for pair in zip(ends, ends[1:])]

    def body(*refs):
        x_refs, dz, act, back = refs[:2], refs[2 : 2 + count], refs[2 + count :][:shares], refs[2 + count + shares :][:shares]
        y_refs, outs = refs[2 + count + 2 * shares :][:2], list(refs[4 + count + 2 * shares :])
        for at in cuts:
            for i in range(count):
                out = outs.pop(0)
                term = dot_tn(x_refs[0][:, at], dz[i][0]) + dot_tn(x_refs[1][:, at], dz[i][1])
                out[...] = term.astype(BF)
                out.push()
        for half, out in enumerate(y_refs):
            total = dot(act[0][half], back[0][...])
            for i in range(1, shares):
                total = total + dot(act[i][half], back[i][...])
            out[...] = total.astype(out.dtype)
            out.push()

    outs = [shape(xs[0].shape, BF), shape(xs[0].shape, F32)]
    outs += [shape((at.stop - at.start, hidden), BF) for at in cuts for _ in range(count)]
    res = run(body, outs, [*xs, *dzs[:-1], *acts, *backs], "partner_terms")
    return res[0], res[1], [list(res[i : i + count]) for i in range(2, len(outs), count)]


def own_terms(xs, dy, act, dz):
    def body(act, dy, x_a, x_b, dz, own_back, own_in):
        own_back[...] = dot_tn(act[0], dy[0]) + dot_tn(act[1], dy[1])
        own_back.push()
        own_in[...] = dot_tn(x_a[...], dz[0]) + dot_tn(x_b[...], dz[1])

    width, hidden = xs[0].shape[1], act.shape[2]
    outs = [shape((hidden, width), F32), shape((width, hidden), F32)]
    return run(body, outs, [act, dy, *xs, dz], "own_terms")


def attention_back_kernel(
    narrow, own_heads, columns, seg_lane,
    where_ref, dr_refs, out_w_ref, q_ref, k_ref, v_ref, lse_ref, stat_ref, att_ref,
    dqkv_ref, out_terms_ref,
    dr_all, da, dk_acc, dv_acc,
):
    rows, width = dr_refs[0].shape
    group = rows * narrow
    own_width = own_heads * HEAD_DIM
    at_narrow = where_ref[1]
    for place in range(narrow):
        dr_all[at_narrow ^ place] = dr_refs[place][...]
    dqkv = dqkv_ref.ref
    segs = [stat_ref[i : i + 1, seg_lane : seg_lane + 1] for i in range(narrow)]
    mask = earlier_keys(rows)
    dqkv[:, columns - 128 :] = jnp.zeros((group, 128), BF)
    for block in range(narrow):
        at = pl.ds(block * rows, rows)
        d_att = dot_nt(dr_all[block], out_w_ref[...]).astype(BF)
        for head in range(own_heads):
            da[head, at] = d_att[:, head * HEAD_DIM : (head + 1) * HEAD_DIM]
    for head in range(own_heads):
        low, high = head * HEAD_DIM, (head + 1) * HEAD_DIM
        for block in reversed(range(narrow)):
            at = pl.ds(block * rows, rows)
            query, d_att, lse = q_ref[head, at], da[head, at], lse_ref[head, :, at]
            probs, d_probs, delta = [], [], None
            for other in range(block + 1):
                keys = pl.ds(other * rows, rows)
                score = dot_nt(k_ref[head, keys], query)
                if other == block:
                    prob = jnp.where(mask, jnp.exp(score - lse), 0.0)
                else:
                    prob = jnp.exp(
                        score - (lse + jnp.where(segs[block] == segs[other], 0.0, -FLOOR_SCORE))
                    )
                d_prob = dot_nt(v_ref[head, keys], d_att)
                part = jnp.sum(prob * d_prob, axis=0, keepdims=True)
                delta = part if delta is None else delta + part
                probs.append(prob)
                d_probs.append(d_prob)
            dq = None
            for other in range(block + 1):
                keys = pl.ds(other * rows, rows)
                d_score = (probs[other] * (d_probs[other] - delta)).astype(BF)
                term = dot_tn(d_score, k_ref[head, keys])
                dq = term if dq is None else dq + term
                dk = dot(d_score, query)
                dv = dot(probs[other].astype(BF), d_att)
                if block == narrow - 1:
                    dk_acc[keys] = dk
                    dv_acc[keys] = dv
                else:
                    dk_acc[keys] += dk
                    dv_acc[keys] += dv
            dqkv[at, low:high] = (dq * SCALE_FACTOR).astype(BF)
        dqkv[:, own_width + low : own_width + high] = dk_acc[...].astype(BF)
        dqkv[:, 2 * own_width + low : 2 * own_width + high] = dv_acc[...].astype(BF)
    dqkv_ref.push()
    out_terms_ref[...] = dot_tn(att_ref[...], dr_all[...].reshape(group, width)).astype(BF)


def attention_back(where, dr_blocks, out_w, q, k, v, lse, stat, att, columns, seg_lane):
    narrow = len(dr_blocks)
    rows, width = dr_blocks[0].shape
    group = rows * narrow
    own_heads = q.shape[0]
    outs = [shape((group, columns), BF), shape((own_heads * HEAD_DIM, width), BF)]

    def body(where_ref, *refs):
        attention_back_kernel(
            narrow, own_heads, columns, seg_lane, where_ref, refs[:narrow], *refs[narrow:]
        )

    scratch = [
        pltpu.VMEM((narrow, rows, width), BF),
        pltpu.VMEM((own_heads, group, HEAD_DIM), BF),
        pltpu.VMEM((group, HEAD_DIM), F32),
        pltpu.VMEM((group, HEAD_DIM), F32),
    ]
    ins = [where, *dr_blocks, out_w, q, k, v, lse, stat, att]
    near = range(narrow)
    return run(body, outs, ins, "attention_backward", scratch, first_smem=True, close=near)


def weight_terms(dqkv, first, weights, info, sums, routers, side_block, side_at):
    group, columns = dqkv.shape
    width = weights.shape[0]
    def body(dqkv_ref, first_ref, weights_ref, info_ref, sums_ref, router, terms_ref):
        first = first_ref[...].reshape(group, width)
        side = weights_ref[:, side_block * 128 : side_block * 128 + 128].astype(F32)
        gain, bias = side[:, side_at : side_at + 1], side[:, side_at + 1 : side_at + 2]
        gain_sum, bias_sum, last = None, None, None
        for block in range(columns // 128):
            cut = slice(block * 128, block * 128 + 128)
            term = dot_tn(first, dqkv_ref[:, cut])
            weight = weights_ref[:, cut].astype(F32)
            total = jnp.sum(dqkv_ref[:, cut].astype(F32), axis=0, keepdims=True)
            gain_part, bias_part = weight * (term - bias * total), weight * total
            gain_sum = gain_part if gain_sum is None else gain_sum + gain_part
            bias_sum = bias_part if bias_sum is None else bias_sum + bias_part
            if block == side_block:
                last = term
            else:
                terms_ref[:, cut] = term.astype(BF)
        gain_sum = jnp.sum(gain_sum, axis=1, keepdims=True) / gain
        bias_sum = jnp.sum(bias_sum, axis=1, keepdims=True)
        which = lax.broadcasted_iota(jnp.int32, (8, width), 0)
        extra = jnp.where(which == 4, router[...], sums_ref[...])
        balance = info_ref[0:1, 0:1]
        high = balance.astype(BF).astype(F32)
        extra = jnp.where(which == 5, high, jnp.where(which == 6, balance - high, extra))
        lane = lax.broadcasted_iota(jnp.int32, (8, 128), 1)
        which = lax.broadcasted_iota(jnp.int32, (8, 128), 0)
        spread = jnp.where(lane == side_at + which, 1.0, 0.0)
        lane = lax.broadcasted_iota(jnp.int32, (width, 128), 1)
        last = jnp.where(lane == side_at, gain_sum, jnp.where(lane == side_at + 1, bias_sum, last))
        last = last + dot_tn(extra, spread)
        terms_ref[:, side_block * 128 : side_block * 128 + 128] = last.astype(BF)

    ins = [dqkv, first, weights, info, sums, *routers]
    return run(body, [shape((width, columns), BF)], ins, "weight_terms")[0]


def first_parts(where, dqkv, weights, narrow):
    rows, width = dqkv.shape[0] // narrow, weights.shape[0]

    def body(where_ref, dqkv_ref, weights_ref, *parts):
        for place in reversed(range(narrow)):
            at = pl.ds(pl.multiple_of((where_ref[1] ^ place) * rows, rows), rows)
            parts[place][...] = dot_nt(dqkv_ref[at], weights_ref[...]).astype(parts[place].dtype)
            parts[place].push()

    outs = [shape((rows, width), BF if i & 1 else F32) for i in range(narrow)]
    return run(body, outs, [where, dqkv, weights], "first_parts", first_smem=True)


def sum_terms(owns, cuts):
    counts = [len(cut) for cut in cuts]

    def body(*refs):
        sources, rest = refs[: len(owns)], list(refs[len(owns) :])
        outs = rest[sum(counts) :]
        for source, count, out in zip(sources, counts, outs):
            low = 0
            for _ in range(count):
                ref = rest.pop(0)
                at = pl.ds(low, ref.shape[0])
                out[at] = source[at] + ref[...].astype(F32)
                low += ref.shape[0]
            out.push()

    outs = [shape(value.shape, F32) for value in owns]
    return run(body, outs, [*owns, *[v for cut in cuts for v in cut]], "sum_terms")


def turned(row):
    count = row.shape[1]
    at = lax.broadcasted_iota(jnp.int32, (count, count), 0)
    other = lax.broadcasted_iota(jnp.int32, (count, count), 1)
    return jnp.sum(jnp.where(at == other, row, 0.0), axis=1, keepdims=True)


def pack(weights, vectors, w_router, routing, segments, wide, narrow, own_width, columns):
    piece, width = weights[0].shape
    experts = w_router.shape[1]
    rows = routing.shape[0]
    start = 3 * own_width

    def body(wq, wk, wv, va, vb, vc, vd, wr, route, segment, sent, held):
        held[...] = jnp.zeros_like(held)
        ids = lax.broadcasted_iota(jnp.int32, (experts, rows), 0)
        counts = jnp.sum(jnp.where(route[...] == ids, 1.0, 0.0), axis=1, keepdims=True)
        sides = [turned(ref[...]) for ref in (va, vb, vc, vd)]
        sides += [turned(wr[i : i + 1]) for i in range(experts)]
        sides += [counts[i : i + 1] for i in range(experts)]
        sides += [segment[0:1, 0:1].astype(F32)]
        lane = lax.broadcasted_iota(jnp.int32, (piece, 128), 1)
        block = jnp.zeros((piece, 128), F32)
        for i, value in enumerate(sides):
            block = jnp.where(lane == start % 128 + i, value, block)
        for n in range(narrow):
            held[n, :, columns - 128 :] = block
            low, high = n * own_width, min((n + 1) * own_width, width)
            for i, ref in enumerate((wq, wk, wv)):
                if low < high:
                    held[n, :, i * own_width : i * own_width + high - low] = ref[:, low:high]

        def send(w, carry):
            for n in range(narrow):
                sent[w * narrow + n] = held[n].astype(BF)
            return carry

        lax.fori_loop(0, wide, send, 0)

    outs = [shape((wide * narrow, piece, columns), BF)]
    ins = [*weights, *[v.reshape(1, piece) for v in vectors], w_router.T]
    ins += [routing.reshape(1, rows), segments.reshape(1, rows)]
    return run(body, outs, ins, "pack", [pltpu.VMEM((narrow, piece, columns), F32)])[0]


def cast_weights(w_in, w_back, cut):
    def body(first, second, upper, lower, back):
        upper[...] = first[:cut].astype(BF)
        upper.push()
        lower[...] = first[cut:].astype(BF)
        lower.push()
        back[...] = second[...].astype(BF)

    width, hidden = w_in.shape
    outs = [shape((cut, hidden), BF), shape((width - cut, hidden), BF), shape(w_back.shape, BF)]
    return run(body, outs, [w_in, w_back], "cast_weights")


def place_cotangent(routing, cotangent, experts, capacity, piece, copies):
    rows, width = cotangent.shape
    slots = experts * capacity

    def body(route, g, piece_ref, placing, moved, tiled):
        for i in range(copies):
            tiled[i] = piece_ref[...]
        tiled.push()
        ids = lax.broadcasted_iota(jnp.int32, (rows, experts), 1)
        expert = turned(route[...].astype(F32)).astype(jnp.int32)
        hot = jnp.where(expert == ids, 1.0, 0.0)
        row = lax.broadcasted_iota(jnp.int32, (rows, rows), 0)
        column = lax.broadcasted_iota(jnp.int32, (rows, rows), 1)
        before = dot(jnp.where(row > column, 1.0, 0.0).astype(BF), hot.astype(BF))
        slot = jnp.sum(before * hot, axis=1, keepdims=True).astype(jnp.int32)
        target = expert * capacity + slot
        place = lax.broadcasted_iota(jnp.int32, (rows, slots), 1)
        spot = jnp.where(place == target, 1.0, 0.0).astype(BF)
        placing[...] = spot
        moved[...] = dot_tn(spot, g[...]).astype(BF)

    outs = [shape((rows, slots), BF), shape((slots, width), BF), shape((copies, *piece.shape), BF)]
    return run(body, outs, [routing.reshape(1, rows), cotangent, piece], "place_cotangent")


def second_norm(x, halves, vectors, side, stat, placing, routing, where, dims):
    narrow, experts, total, side_at = dims
    rows, width = x.shape
    slots = placing.shape[1]
    count = len(halves)

    def body(where_ref, x_ref, *refs):
        vec, side_ref, stat_ref, placing_ref, route = refs[count : count + 5]
        mixed_ref, moved, gate_ref, info = refs[count + 5 :]
        mixed = x_ref[...].astype(F32)
        for ref in refs[:count]:
            mixed = mixed + ref[...].astype(F32)
        mixed_ref[...] = mixed
        unit, _ = norm_parts(mixed)
        low = (unit * vec[2:3] + vec[3:4]).astype(BF)
        moved[...] = dot_tn(placing_ref[...], low).astype(BF)
        logits = dot(low, side_ref[...])
        lane = lax.broadcasted_iota(jnp.int32, (rows, 128), 1)
        expert = turned(route[...].astype(F32)).astype(jnp.int32)
        chosen = jnp.where(lane - (side_at + 4) == expert, logits, 0.0)
        gate = 1.0 / (1.0 + jnp.exp(-jnp.sum(chosen, axis=1, keepdims=True)))
        gate_ref[...] = gate
        first = side_at + 4 + experts
        sums = jnp.sum(jnp.where(lane - first == expert, gate, 0.0), axis=0, keepdims=True)
        lane = lax.broadcasted_iota(jnp.int32, (1, 128), 1)
        counts = stat_ref[narrow : narrow + 1]
        deviation = (counts - float(total) / experts) * (experts / float(total))
        kept = (lane >= first) & (lane < first + experts)
        balance = experts / float(total) * jnp.sum(
            jnp.where(kept, deviation * sums, 0.0), axis=1, keepdims=True
        )
        own = jnp.sum(
            jnp.where(lane == first + where_ref[0], deviation, 0.0), axis=1, keepdims=True
        )
        core = jnp.where(where_ref[1] % 2 == 0, BALANCE_WEIGHT * (experts / float(total)), 0.0)
        info[...] = jnp.where(lane == 0, balance, own * core) + jnp.zeros((8, 128), F32)

    outs = [shape((rows, width), F32), shape((slots, width), BF), shape((rows, 1), F32)]
    outs.append(shape((8, 128), F32))
    ins = [where, x, *halves, vectors, side, stat, placing, routing.reshape(1, rows)]
    near = range(1, 1 + count)
    return run(body, outs, ins, "second_norm", first_smem=True, close=near)


def second_back(returned, placing, mixed, cotangent, vectors):
    rows, width = mixed.shape

    def body(ret, placing_ref, mixed_ref, g, vec, dr_ref, low_ref, sums):
        incoming = dot(placing_ref[...], ret[...])
        unit, inverse = norm_parts(mixed_ref[...])
        gain = jnp.sum(incoming * unit, axis=0, keepdims=True)
        bias = jnp.sum(incoming, axis=0, keepdims=True)
        dr = g[...].astype(F32) + norm_back(incoming, unit, inverse, vec[2:3])
        dr_ref[...] = dr
        low_ref[...] = dr.astype(BF)
        which = lax.broadcasted_iota(jnp.int32, (8, width), 0)
        sums[...] = jnp.where(which == 2, gain, jnp.where(which == 3, bias, 0.0))

    outs = [shape((rows, width), F32), shape((rows, width), BF), shape((8, width), F32)]
    ins = [returned, placing, mixed, cotangent, vectors]
    return run(body, outs, ins, "second_back", close=(0,), close_outs=(1,))


def finish_rows(returned, placing, mixed, gates):
    def body(ret, placing_ref, mixed_ref, gate, out):
        out[...] = mixed_ref[...] + gate[...] * dot(placing_ref[...], ret[...])

    ins = [returned, placing, mixed, gates]
    return run(body, [shape(mixed.shape, F32)], ins, "finish_rows")[0]


def first_back(halves, x, dr, vectors):
    count = len(halves)

    def body(*refs):
        x_ref, dr_ref, vec, out = refs[count:]
        incoming = refs[0][...].astype(F32)
        for ref in refs[1:count]:
            incoming = incoming + ref[...].astype(F32)
        unit, inverse = norm_parts(x_ref[...].astype(F32))
        out[...] = dr_ref[...] + norm_back(incoming, unit, inverse, vec[0:1])

    return run(body, [shape(x.shape, F32)], [*halves, x, dr, vectors], "first_back")[0]


def unpack(came, wide, narrow, own_width, width, experts):
    piece, columns = came.shape[1:]
    start = 3 * own_width
    side_block, side_at = start // 128, start % 128

    def as_row(column):
        row = lax.broadcasted_iota(jnp.int32, (piece, piece), 0)
        other = lax.broadcasted_iota(jnp.int32, (piece, piece), 1)
        return jnp.sum(jnp.where(row == other, column, 0.0), axis=0, keepdims=True)

    def body(came_ref, gq, gk, gv, va, vb, vc, vd, gr, balance):
        every = jnp.zeros((piece, 128), F32)
        routers = []
        for n in range(narrow):
            total = jnp.zeros((piece, columns), F32)
            for w in range(wide):
                total = total + came_ref[w * narrow + n].astype(F32)
            every = every + total[:, side_block * 128 : side_block * 128 + 128]
            low, high = n * own_width, min((n + 1) * own_width, width)
            if low < high:
                for i, ref in enumerate((gq, gk, gv)):
                    ref[:, low:high] = total[:, i * own_width : i * own_width + high - low]
        for w in range(wide):
            column = jnp.zeros((piece, 1), F32)
            at = start + 4
            for n in range(narrow):
                column = column + came_ref[w * narrow + n, :, at : at + 1].astype(F32)
            gr[w : w + 1] = as_row(column)
        for i, ref in enumerate((va, vb, vc, vd)):
            ref[...] = as_row(every[:, side_at + i : side_at + i + 1])
        balance[...] = every[0:1, side_at + 5 : side_at + 6] + every[0:1, side_at + 6 : side_at + 7]

    outs = [shape((piece, width), F32)] * 3 + [shape((1, piece), F32)] * 4
    outs += [shape((experts, piece), F32), shape((1, 1), F32)]
    return run(body, outs, [came], "unpack", close=(0,))


def local(
    hidden_in,
    segments,
    routing,
    first_gain,
    first_bias,
    second_gain,
    second_bias,
    w_query,
    w_key,
    w_value,
    w_out,
    w_router,
    w_in,
    w_back,
    cotangent,
):
    wide = lax.axis_size("wide")
    narrow = lax.axis_size("narrow")
    devices = wide * narrow
    rows, width = hidden_in.shape
    piece = w_query.shape[0]
    experts = w_router.shape[1]
    capacity = max(2, 2 * rows // experts)
    total = rows * devices
    own_heads = -(-HEADS // narrow)
    own_width = own_heads * HEAD_DIM
    aligned = own_width * narrow == width and own_width == piece * wide
    at_wide = lax.axis_index("wide")
    at_narrow = lax.axis_index("narrow")
    where = jnp.stack([at_wide, at_narrow]).astype(jnp.int32)
    bits = [1 << level for level in range(narrow.bit_length() - 1)]
    core_bit, chip_bits = bits[:1], bits[1:]
    side_start = 3 * own_width
    side_block, side_at = side_start // 128, side_start % 128
    seg_lane = side_at + 4 + 2 * experts
    assert seg_lane < 128
    columns = side_block * 128 + 128
    gate = lax.optimization_barrier

    def swap(values, bit):
        return lax.ppermute(values, "narrow", [(i, i ^ bit) for i in range(narrow)])

    def gather_blocks(block, over):
        blocks = {0: block}
        for bit in reversed(over):
            for place in list(blocks):
                blocks[place ^ bit] = swap(blocks[place], bit)
        return blocks

    def reduce_blocks(blocks, over):
        blocks = dict(blocks)
        for bit in over:
            for place in sorted(blocks, reverse=True):
                if place & bit:
                    moved = swap(blocks.pop(place).astype(BF), bit).astype(F32)
                    blocks[place ^ bit] = blocks[place ^ bit] + moved
        return blocks

    def exchange(values):
        values = values.reshape(experts, capacity, width)
        return to_all(values, "wide").reshape(experts * capacity, width)

    sent = pack(
        [w_query, w_key, w_value], [first_gain, first_bias, second_gain, second_bias],
        w_router, routing, segments, wide, narrow, own_width, columns,
    )
    x_blocks = gather_blocks(hidden_in, chip_bits)
    out_low = w_out.astype(BF)
    if aligned:
        out_low = lax.ppermute(
            out_low, BOTH, [(n * wide + j, j * narrow + n) for n in range(narrow) for j in range(wide)]
        )
    sent, out_low, where, first_w, second_w = gate((sent, out_low, where, w_in[0], w_back[0]))
    *in_low, back_low = cast_weights(first_w, second_w, width // 3)
    weights = to_all(sent, BOTH).reshape(width, columns)
    for place in list(x_blocks):
        x_blocks[place ^ 1] = swap(x_blocks[place], 1)
    partners = [i for i in range(2, narrow, 2)]
    in_upper = [swap(in_low[0], i) for i in partners]
    placing, g_moved, out_tiled = place_cotangent(
        routing, cotangent, experts, capacity, out_low, wide
    )
    weights, in_low, back_low, g_moved, in_upper, out_tiled = gate(
        (weights, in_low, back_low, g_moved, in_upper, out_tiled)
    )
    back_came = [swap(back_low, i) for i in partners]
    if aligned:
        out_w = to_all(out_tiled, "wide").reshape(own_width, width)
    else:
        all_out = lax.all_gather(out_low, BOTH, axis=0, tiled=True)
        all_out = jnp.pad(all_out, ((0, own_width * narrow - width), (0, 0)))
        out_w = lax.dynamic_slice_in_dim(all_out, at_narrow * own_width, own_width, axis=0)

    x_list = [x_blocks[i] for i in range(narrow)]
    first, q, k, v, att, lse, vectors, stat, side = attention(
        where, x_list, weights, own_heads, piece, side_block, side_at, experts
    )
    att, g_moved = gate((att, g_moved))
    g_own = exchange(g_moved)
    parts = project(where, att, out_w, narrow)
    halves = reduce_blocks({i: parts[i] for i in range(narrow)}, core_bit)
    halves, back_came = gate((halves, back_came))
    halves = {i: swap(halves[i].astype(BF), i) if i else halves[i] for i in sorted(halves)}

    halves, g_own, in_low = gate((halves, g_own, in_low))
    in_lower = [swap(in_low[1], i) for i in partners]
    mixed, x_moved, gates, info = second_norm(
        hidden_in, [halves[i] for i in sorted(halves)], vectors, side, stat, placing, routing,
        where, (narrow, experts, total, side_at),
    )
    g_other = swap(g_own, 1)
    x_own = exchange(x_moved)
    x_own, in_lower = gate((x_own, in_lower))
    x_other = swap(x_own, 1)

    ins = [list(pair) for pair in zip(in_upper, in_lower)] + [in_low]
    backs = [*back_came, back_low]
    xs = [x_other, x_own]
    dx_o, dx_s, router, dy, acts, dzs, far_back = expert(info, xs, [g_other, g_own], vectors, ins, backs)

    def cross(cut):
        return [swap(value, place) for value, place in zip(cut, partners)]

    dx_sum = (dx_s + swap(dx_o, 1).astype(F32)).astype(BF)
    d_returned = exchange(dx_sum)
    acts, dx_sum = gate((acts, dx_sum))
    far_back = cross(far_back)
    ends = (0, width // 6, width * 2 // 3, width)
    y_o, y_s, made = partner_terms(xs, acts, dzs, backs, ends)
    own_back, own_in = own_terms(xs, dy, acts[-1], dzs[-1])
    y_sum = (y_s + swap(y_o, 1).astype(F32)).astype(BF)
    made, far_back, own_back, own_in, y_sum = gate((made, far_back, own_back, own_in, y_sum))
    crossed = [cross(made[0])]
    d_mixed, d_mixed_low, sums = second_back(d_returned, placing, mixed, cotangent, vectors)
    d_mixed_low, y_sum, crossed = gate((d_mixed_low, y_sum, crossed))
    returned = exchange(y_sum)
    dr_blocks = gather_blocks(d_mixed_low, chip_bits)
    for place in list(dr_blocks):
        dr_blocks[place ^ 1] = swap(dr_blocks[place], 1)
    dr_blocks, made = gate((dr_blocks, made))
    crossed.append(cross(made[1]))
    dr_list = [dr_blocks[i] for i in range(narrow)]

    d_qkv, terms_out = attention_back(
        where, dr_list, out_w, q, k, v, lse, stat, att, columns, seg_lane
    )
    d_qkv, crossed, terms_out, returned, made = gate((d_qkv, crossed, terms_out, returned, made))
    last_cross = cross(made[2])
    if aligned:
        terms_out = to_all(terms_out.reshape(wide, piece, width), "wide")
    terms = weight_terms(d_qkv, first, weights, info, sums, [router], side_block, side_at)

    tied = (terms, d_qkv, returned, terms_out, last_cross)
    terms, d_qkv, returned, terms_out, last_cross = gate(tied)
    d_parts = first_parts(where, d_qkv, weights, narrow)
    crossed.append(last_cross)
    terms = to_all(terms.reshape(devices, piece, columns), BOTH)
    d_halves = reduce_blocks({i: d_parts[i] for i in range(narrow)}, core_bit)
    d_halves = [swap(d_halves[i].astype(BF), i) if i else d_halves[i] for i in sorted(d_halves)]
    if aligned:
        grad_out_w = lax.ppermute(
            jnp.sum(terms_out.astype(F32), axis=0),
            BOTH,
            [(j * narrow + n, n * wide + j) for n in range(narrow) for j in range(wide)],
        )
    else:
        spread = jnp.zeros((own_width * narrow, width), F32)
        spread = lax.dynamic_update_slice_in_dim(
            spread, terms_out.astype(F32), at_narrow * own_width, axis=0
        )
        grad_out_w = lax.psum_scatter(spread[:width], BOTH, scatter_dimension=0, tiled=True)
    block_out = finish_rows(returned, placing, mixed, gates)
    grad_hidden = first_back(d_halves, hidden_in, d_mixed, vectors)
    back_terms, in_terms = sum_terms([own_back, own_in], [far_back[:1], [cut[0] for cut in crossed]])
    for i in range(1, len(partners)):
        back_terms = back_terms + far_back[i].astype(F32)
        in_terms = in_terms + jnp.concatenate([cut[i] for cut in crossed], axis=0).astype(F32)

    done = unpack(terms, wide, narrow, own_width, width, experts)
    return (
        block_out,
        done[8].reshape(()),
        grad_hidden,
        *[done[i].reshape(piece) for i in range(3, 7)],
        *done[:3],
        grad_out_w,
        done[7].T,
        in_terms[None],
        back_terms[None],
    )


def solution(mesh):
    rows = P(BOTH, None)
    vector = P(BOTH)
    placed = (rows, vector, rows) + (vector,) * 4 + (rows,) * 5
    expert_specs = (P("wide", None, "narrow"), P("wide", "narrow", None))
    return jax.shard_map(
        local,
        mesh=mesh,
        in_specs=placed + expert_specs + (rows,),
        out_specs=(rows, P(), rows) + (vector,) * 4 + (rows,) * 5 + expert_specs,
        check_vma=False,
    )
```

```python
import jax
import jax.numpy as jnp
from jax import lax
from jax.experimental import pallas as pl
from jax.experimental.pallas import tpu as pltpu
from jax.sharding import PartitionSpec as P

HEADS = 12
HEAD_DIM = 64
EPSILON = 1e-05
FLOOR_SCORE = -1e30
SCALE_FACTOR = 0.125
BALANCE_WEIGHT = 0.01
BOTH = ("wide", "narrow")
BF = jnp.bfloat16
F32 = jnp.float32


def dot(left, right):
    return jnp.dot(left, right, preferred_element_type=F32)


def dot_nt(left, right):
    return lax.dot_general(left, right, (((1,), (1,)), ((), ())), preferred_element_type=F32)


def dot_tn(left, right):
    return lax.dot_general(left, right, (((0,), (0,)), ((), ())), preferred_element_type=F32)


def norm_parts(values):
    centered = values - jnp.mean(values, axis=1, keepdims=True)
    inverse = lax.rsqrt(jnp.mean(centered * centered, axis=1, keepdims=True) + EPSILON)
    return centered * inverse, inverse


def norm_back(incoming, unit, inverse, gain):
    scaled = incoming * gain
    return inverse * (
        scaled
        - jnp.mean(scaled, axis=1, keepdims=True)
        - unit * jnp.mean(scaled * unit, axis=1, keepdims=True)
    )


def to_all(values, axes):
    return lax.all_to_all(values, axes, split_axis=0, concat_axis=0, tiled=True)


SMALL = pl.CostEstimate(flops=1000, bytes_accessed=1000, transcendentals=0)
LARGE = pl.CostEstimate(flops=int(2.5e10), bytes_accessed=int(3e7), transcendentals=0)
FILLERS = ("place_cotangent", "cast_weights")


class Held:
    def __init__(self, ref, copies, fetched):
        self.ref, self.copies = ref, copies
        self.waiting = list(range(len(copies))) if fetched else []
        self.started = set(self.waiting)

    def get(self):
        for i in self.waiting:
            self.copies[i].wait()
        self.waiting = []
        return self.ref

    def push(self, part=None):
        for i in range(len(self.copies)) if part is None else [part]:
            if i not in self.started and i < len(self.copies):
                self.copies[i].start()
                self.waiting.append(i)
                self.started.add(i)

    @property
    def shape(self):
        return self.ref.shape

    @property
    def dtype(self):
        return self.ref.dtype

    def __getitem__(self, at):
        return self.get()[at]

    def __setitem__(self, at, value):
        self.ref[at] = value


def padded(value):
    lanes = -(-value.shape[-1] // 128) * 128
    rows = -(-value.shape[-2] // 16) * 16 if len(value.shape) > 1 else 16
    outer = 1
    for size in value.shape[:-2]:
        outer *= size
    return outer * rows * lanes * jnp.dtype(value.dtype).itemsize


def run(body, outs, ins, name, scratch=(), first_smem=False, pieces=None, close=(), close_outs=(), room=10):
    outs, ins = list(outs), list(ins)
    lead = 1 if first_smem else 0
    fetched, total = len(ins) - lead, len(ins) - lead + len(outs)
    arrays = ins[lead:] + outs
    near = [i in close if i < fetched else i - fetched in close_outs for i in range(total)]
    cuts = [(pieces or {}).get(i - fetched, [()]) for i in range(total)]
    slots, semaphores, used = {}, {}, 0
    for i in range(total):
        if not near[i]:
            slots[i], semaphores[i] = len(slots), used
            used += len(cuts[i])
    buffers = [pltpu.VMEM(arrays[i].shape, arrays[i].dtype) for i in slots]

    def kernel(*refs):
        smem_refs, given = refs[:lead], refs[lead : lead + total]
        own = refs[lead + total : lead + total + len(slots)]
        marks = refs[lead + total + len(slots)]
        held = []
        for i in range(total):
            if near[i]:
                held.append(Held(given[i], [], False))
                continue
            mine = own[slots[i]]
            source, target = (given[i], mine) if i < fetched else (mine, given[i])
            copies = []
            for j, at in enumerate(cuts[i]):
                ends = (source.at[at], target.at[at]) if at else (source, target)
                copies.append(pltpu.make_async_copy(*ends, marks.at[semaphores[i] + j]))
            if i < fetched:
                copies[0].start()
            held.append(Held(mine, copies, i < fetched))
        body(*smem_refs, *held, *refs[lead + total + len(slots) + 1 :])
        for item in held[fetched:]:
            item.push()
        for item in held:
            item.get()

    hbm, vmem = pl.BlockSpec(memory_space=pltpu.HBM), pl.BlockSpec(memory_space=pltpu.VMEM)
    ins = [
        value if i < lead or near[i - lead] else pltpu.with_memory_space_constraint(value, pltpu.HBM)
        for i, value in enumerate(ins)
    ]
    placed = [
        value if near[fetched + i] else pltpu.HBM(value.shape, value.dtype)
        for i, value in enumerate(outs)
    ]
    size = sum(padded(arrays[i]) for i in slots) + sum(padded(value) for value in scratch)
    limit = min(60, size // 2**20 + 1 + room)
    return pl.pallas_call(
        kernel,
        out_shape=placed,
        in_specs=([smem()] if first_smem else []) + [vmem if near[i] else hbm for i in range(fetched)],
        out_specs=[vmem if near[fetched + i] else hbm for i in range(len(outs))],
        scratch_shapes=[*buffers, pltpu.SemaphoreType.DMA((max(1, used),)), *scratch],
        compiler_params=pltpu.CompilerParams(vmem_limit_bytes=limit * 1024 * 1024),
        cost_estimate=LARGE if name in FILLERS else SMALL,
        name=name,
    )(*ins)


def shape(dims, dtype):
    return jax.ShapeDtypeStruct(dims, dtype)


def smem():
    return pl.BlockSpec(memory_space=pltpu.SMEM)


def earlier_keys(size):
    key = lax.broadcasted_iota(jnp.int32, (size, size), 0)
    query = lax.broadcasted_iota(jnp.int32, (size, size), 1)
    return key <= query


def attention_kernel(
    narrow, own_heads, piece, side_block, side_at, experts,
    where_ref, x_refs, weights_ref,
    first_ref, q_ref, k_ref, v_ref, att_ref, lse_ref, rows_ref, stat_ref, side_ref,
):
    rows, width = x_refs[0].shape
    at_wide, at_narrow = where_ref[0], where_ref[1]
    side = weights_ref[:, side_block * 128 : side_block * 128 + 128]
    side_ref[...] = side
    lane = lax.broadcasted_iota(jnp.int32, (8, 128), 1)
    which = lax.broadcasted_iota(jnp.int32, (8, 128), 0)
    wanted = jnp.where(which < 4, side_at + which, side_at + 4 + at_wide)
    pick = jnp.where(lane == wanted, 1.0, 0.0)
    vectors = dot_nt(pick, side.astype(F32))
    rows_ref[...] = vectors
    stat_rows = stat_ref.shape[0]
    column = lax.broadcasted_iota(jnp.int32, (stat_rows, width), 1)
    which = lax.broadcasted_iota(jnp.int32, (stat_rows, width), 0)
    segment_row = (at_wide * narrow + which) * piece
    wanted = jnp.where(which < narrow, segment_row, column - lax.rem(column, piece))
    stat = dot(jnp.where(column == wanted, 1.0, 0.0), side.astype(F32))
    stat_ref[...] = stat
    seg_lane = side_at + 4 + 2 * experts
    segs = [stat[i : i + 1, seg_lane : seg_lane + 1] for i in range(narrow)]
    gain, bias = vectors[0:1], vectors[1:2]
    for place in range(narrow):
        unit, _ = norm_parts(x_refs[place][...].astype(F32))
        first_ref[at_narrow ^ place] = (unit * gain + bias).astype(BF)
    first_ref.push()
    own_width = own_heads * HEAD_DIM
    for block in range(narrow):
        at = pl.ds(block * rows, rows)
        qkv = dot(first_ref.ref[block], weights_ref[...])
        for head in range(own_heads):
            low, high = head * HEAD_DIM, (head + 1) * HEAD_DIM
            q_ref[head, at] = (qkv[:, low:high].astype(BF).astype(F32) * SCALE_FACTOR).astype(BF)
            k_ref[head, at] = qkv[:, own_width + low : own_width + high].astype(BF)
            v_ref[head, at] = qkv[:, 2 * own_width + low : 2 * own_width + high].astype(BF)
    for ref in (q_ref, k_ref, v_ref):
        ref.push()
    mask = earlier_keys(rows)
    for head in range(own_heads):
        for block in range(narrow):
            at = pl.ds(block * rows, rows)
            query = q_ref.ref[head, at]
            keys = pl.ds(0, (block + 1) * rows)
            score = dot_nt(k_ref.ref[head, keys], query)
            scores = []
            for other in range(block + 1):
                piece = score[other * rows : (other + 1) * rows]
                if other == block:
                    scores.append(jnp.where(mask, piece, FLOOR_SCORE))
                else:
                    scores.append(piece + jnp.where(segs[block] == segs[other], 0.0, FLOOR_SCORE))
            score = scores[0] if block == 0 else jnp.concatenate(scores, axis=0)
            top = score.max(axis=0, keepdims=True)
            value = jnp.exp(score - top)
            total = value.sum(axis=0, keepdims=True)
            att = dot_tn((value * (1.0 / total)).astype(BF), v_ref.ref[head, keys])
            att_ref[at, head * HEAD_DIM : (head + 1) * HEAD_DIM] = att.astype(BF)
            lse_ref[head, :, at] = top + jnp.log(total)


def project(where, att, out_w, narrow):
    rows, width = att.shape[0] // narrow, out_w.shape[1]

    def body(where_ref, att_ref, out_w_ref, *parts):
        for place in reversed(range(narrow)):
            at = pl.ds(pl.multiple_of((where_ref[1] ^ place) * rows, rows), rows)
            parts[place][...] = dot(att_ref[at], out_w_ref[...]).astype(parts[place].dtype)
            parts[place].push()

    outs = [shape((rows, width), BF if i & 1 else F32) for i in range(narrow)]
    return run(
        body, outs, [where, att, out_w], "project", first_smem=True, close=(0,), close_outs=range(narrow)
    )


def attention(where, x_blocks, weights, own_heads, piece, side_block, side_at, experts):
    narrow = len(x_blocks)
    rows, width = x_blocks[0].shape
    group = rows * narrow
    stat_rows = -(-(narrow + 1) // 8) * 8
    head_shape = jax.ShapeDtypeStruct((own_heads, group, HEAD_DIM), BF)
    outs = (
        [jax.ShapeDtypeStruct((narrow, rows, width), BF)]
        + [head_shape] * 3
        + [shape((group, own_heads * HEAD_DIM), BF)]
        + [jax.ShapeDtypeStruct((own_heads, 1, group), F32)]
        + [shape((8, width), F32), shape((stat_rows, 128), F32), shape((width, 128), BF)]
    )

    def body(where_ref, *refs):
        attention_kernel(
            narrow, own_heads, piece, side_block, side_at, experts,
            where_ref, refs[:narrow], *refs[narrow:],
        )

    ins = [where, *x_blocks, weights]
    near = range(narrow + 1)
    return run(body, outs, ins, "attention_forward", first_smem=True, close=near, close_outs=(4,))


def gelu_pieces(z):
    size = jnp.abs(z)
    fall = jnp.exp(z * z * -0.5)
    t = 1.0 / (1.0 + size * (0.3275911 * 0.7071067811865476))
    tail = 1.061405429 * 0.5
    for term in (-1.453152027, 1.421413741, -0.284496736, 0.254829592):
        tail = tail * t + term * 0.5
    tail = tail * t * fall
    upper = jnp.where(z < 0.0, tail, 1.0 - tail)
    return upper, z * fall * 0.3989422804014327


def expert_share(x, dy, w_in, w_back, act_ref, dz_ref, at):
    z, low = None, 0
    for cut in w_in:
        term = dot(x[:, low : low + cut.shape[0]], cut[...])
        z = term if z is None else z + term
        low += cut.shape[0]
    upper, bump = gelu_pieces(z)
    act = (z * upper).astype(BF)
    act_ref[at] = act
    du = dot_nt(dy, w_back[...])
    dz = (du * (upper + bump)).astype(BF)
    dz_ref[at] = dz
    dx = [dot_nt(dz, cut[...]) for cut in w_in]
    dx = dx[0] if len(dx) == 1 else jnp.concatenate(dx, axis=1)
    return dx, jnp.sum(act.astype(F32) * du, axis=1, keepdims=True)


def row_gate(x, vectors):
    score = jnp.sum(x.astype(F32) * vectors[4:5], axis=1, keepdims=True)
    return 1.0 / (1.0 + jnp.exp(-score))


STEP = 256


def expert(info, xs, gs, vectors, ins, backs):
    count, width = xs[0].shape
    hidden = backs[0].shape[0]
    shares, cuts = len(backs), len(ins[0])
    blocks = [(half, start) for half in range(2) for start in range(0, count, STEP)]

    def body(info_ref, vec, *refs):
        x_refs, w1_first, w2_first, g_refs = refs[:2], refs[2 : 2 + cuts], refs[2 + cuts], refs[3 + cuts : 5 + cuts]
        rest, o = refs[5 + cuts : 4 + shares * (cuts + 1)], refs[4 + shares * (cuts + 1) :]
        w1 = [w1_first] + [rest[i * (cuts + 1) : i * (cuts + 1) + cuts] for i in range(shares - 1)]
        w2 = [w2_first] + [rest[i * (cuts + 1) + cuts] for i in range(shares - 1)]
        dx_refs, router, dy, acts, dzs = o[:2], o[2], o[3], o[4 : 4 + shares], o[4 + shares : 4 + 2 * shares]
        back_refs = o[4 + 2 * shares : 3 + 3 * shares]
        dx_acc, score_acc = o[3 + 3 * shares :]
        router_sum = jnp.zeros((1, width), F32)
        for i in range(shares):
            for number, (half, start) in enumerate(blocks):
                at = pl.ds(start, min(STEP, count))
                rows = x_refs[half][at]
                if i == 0:
                    gate = row_gate(rows, vec)
                    dy[half, at] = (gate * g_refs[half][at].astype(F32)).astype(BF)
                    dy.push(number)
                dx, score = expert_share(
                    rows, dy.ref[half, at], w1[i], w2[i], acts[i].ref.at[half], dzs[i].ref.at[half], at
                )
                acts[i].push(number)
                dzs[i].push(number)
                if i > 0:
                    dx, score = dx + dx_acc[half, at], score + score_acc[half, at]
                if i < shares - 1:
                    dx_acc[half, at], score_acc[half, at] = dx, score
                else:
                    gate = row_gate(rows, vec)
                    dlogit = (score + info_ref[0:1, 1:2] * gate) * (1.0 - gate)
                    router_sum = router_sum + jnp.sum(
                        rows.astype(F32) * dlogit, axis=0, keepdims=True
                    )
                    dx_refs[half][at] = (dx + dlogit * vec[4:5]).astype(dx_refs[half].dtype)
                    if start + STEP >= count:
                        dx_refs[half].push()
            if i < shares - 1:
                act, grad = acts[i].ref, dy.ref
                back_refs[i][...] = (dot_tn(act[0], grad[0]) + dot_tn(act[1], grad[1])).astype(BF)
                back_refs[i].push()
        router[...] = router_sum

    outs = [shape((count, width), BF), shape((count, width), F32), shape((1, width), F32)]
    outs += [shape((2, count, width), BF)] + [shape((2, count, hidden), BF)] * (2 * shares)
    parts = len(outs)
    outs += [shape((hidden, width), BF)] * (shares - 1)
    cut = [(half, pl.ds(start, min(STEP, count))) for half, start in blocks]
    operands = [info, vectors, *xs, *ins[0], backs[0], *gs]
    for i in range(1, shares):
        operands += [*ins[i], backs[i]]
    scratch = [pltpu.VMEM((2, count, width), F32), pltpu.VMEM((2, count, 1), F32)]
    pieces = {i: cut for i in range(3, parts)}
    near = (2, 3)
    res = run(body, outs, operands, "expert", scratch, pieces=pieces, close=near, close_outs=(0, 1))
    res = list(res)
    acts, dzs = res[4 : 4 + shares], res[4 + shares : parts]
    return res[0], res[1], res[2], res[3], acts, dzs, res[parts:]


def partner_terms(xs, acts, dzs, backs, ends):
    shares = len(acts)
    count, width, hidden = shares - 1, xs[0].shape[1], acts[0].shape[2]
    cuts = [slice(*pair) for pair in zip(ends, ends[1:])]

    def body(*refs):
        x_refs, dz, act, back = refs[:2], refs[2 : 2 + count], refs[2 + count :][:shares], refs[2 + count + shares :][:shares]
        y_refs, outs = refs[2 + count + 2 * shares :][:2], list(refs[4 + count + 2 * shares :])
        for at in cuts:
            for i in range(count):
                out = outs.pop(0)
                term = dot_tn(x_refs[0][:, at], dz[i][0]) + dot_tn(x_refs[1][:, at], dz[i][1])
                out[...] = term.astype(BF)
                out.push()
        for half, out in enumerate(y_refs):
            total = dot(act[0][half], back[0][...])
            for i in range(1, shares):
                total = total + dot(act[i][half], back[i][...])
            out[...] = total.astype(out.dtype)
            out.push()

    outs = [shape(xs[0].shape, BF), shape(xs[0].shape, F32)]
    outs += [shape((at.stop - at.start, hidden), BF) for at in cuts for _ in range(count)]
    res = run(body, outs, [*xs, *dzs[:-1], *acts, *backs], "partner_terms")
    return res[0], res[1], [list(res[i : i + count]) for i in range(2, len(outs), count)]


def own_terms(xs, dy, act, dz):
    def body(act, dy, x_a, x_b, dz, own_back, own_in):
        own_back[...] = dot_tn(act[0], dy[0]) + dot_tn(act[1], dy[1])
        own_back.push()
        own_in[...] = dot_tn(x_a[...], dz[0]) + dot_tn(x_b[...], dz[1])

    width, hidden = xs[0].shape[1], act.shape[2]
    outs = [shape((hidden, width), F32), shape((width, hidden), F32)]
    return run(body, outs, [act, dy, *xs, dz], "own_terms")


def attention_back_kernel(
    narrow, own_heads, columns, seg_lane,
    where_ref, dr_refs, out_w_ref, q_ref, k_ref, v_ref, lse_ref, stat_ref, att_ref,
    dqkv_ref, out_terms_ref,
    dr_all, da, dk_acc, dv_acc,
):
    rows, width = dr_refs[0].shape
    group = rows * narrow
    own_width = own_heads * HEAD_DIM
    at_narrow = where_ref[1]
    for place in range(narrow):
        dr_all[at_narrow ^ place] = dr_refs[place][...]
    dqkv = dqkv_ref.ref
    segs = [stat_ref[i : i + 1, seg_lane : seg_lane + 1] for i in range(narrow)]
    mask = earlier_keys(rows)
    dqkv[:, columns - 128 :] = jnp.zeros((group, 128), BF)
    for block in range(narrow):
        at = pl.ds(block * rows, rows)
        d_att = dot_nt(dr_all[block], out_w_ref[...]).astype(BF)
        for head in range(own_heads):
            da[head, at] = d_att[:, head * HEAD_DIM : (head + 1) * HEAD_DIM]
    for head in range(own_heads):
        low, high = head * HEAD_DIM, (head + 1) * HEAD_DIM
        for block in reversed(range(narrow)):
            at = pl.ds(block * rows, rows)
            query, d_att, lse = q_ref[head, at], da[head, at], lse_ref[head, :, at]
            probs, d_probs, delta = [], [], None
            for other in range(block + 1):
                keys = pl.ds(other * rows, rows)
                score = dot_nt(k_ref[head, keys], query)
                if other == block:
                    prob = jnp.where(mask, jnp.exp(score - lse), 0.0)
                else:
                    prob = jnp.exp(
                        score - (lse + jnp.where(segs[block] == segs[other], 0.0, -FLOOR_SCORE))
                    )
                d_prob = dot_nt(v_ref[head, keys], d_att)
                part = jnp.sum(prob * d_prob, axis=0, keepdims=True)
                delta = part if delta is None else delta + part
                probs.append(prob)
                d_probs.append(d_prob)
            dq = None
            for other in range(block + 1):
                keys = pl.ds(other * rows, rows)
                d_score = (probs[other] * (d_probs[other] - delta)).astype(BF)
                term = dot_tn(d_score, k_ref[head, keys])
                dq = term if dq is None else dq + term
                dk = dot(d_score, query)
                dv = dot(probs[other].astype(BF), d_att)
                if block == narrow - 1:
                    dk_acc[keys] = dk
                    dv_acc[keys] = dv
                else:
                    dk_acc[keys] += dk
                    dv_acc[keys] += dv
            dqkv[at, low:high] = (dq * SCALE_FACTOR).astype(BF)
        dqkv[:, own_width + low : own_width + high] = dk_acc[...].astype(BF)
        dqkv[:, 2 * own_width + low : 2 * own_width + high] = dv_acc[...].astype(BF)
    dqkv_ref.push()
    out_terms_ref[...] = dot_tn(att_ref[...], dr_all[...].reshape(group, width)).astype(BF)


def attention_back(where, dr_blocks, out_w, q, k, v, lse, stat, att, columns, seg_lane):
    narrow = len(dr_blocks)
    rows, width = dr_blocks[0].shape
    group = rows * narrow
    own_heads = q.shape[0]
    outs = [shape((group, columns), BF), shape((own_heads * HEAD_DIM, width), BF)]

    def body(where_ref, *refs):
        attention_back_kernel(
            narrow, own_heads, columns, seg_lane, where_ref, refs[:narrow], *refs[narrow:]
        )

    scratch = [
        pltpu.VMEM((narrow, rows, width), BF),
        pltpu.VMEM((own_heads, group, HEAD_DIM), BF),
        pltpu.VMEM((group, HEAD_DIM), F32),
        pltpu.VMEM((group, HEAD_DIM), F32),
    ]
    ins = [where, *dr_blocks, out_w, q, k, v, lse, stat, att]
    near = range(narrow)
    return run(body, outs, ins, "attention_backward", scratch, first_smem=True, close=near)


def weight_terms(dqkv, first, weights, info, sums, routers, side_block, side_at):
    group, columns = dqkv.shape
    width = weights.shape[0]
    def body(dqkv_ref, first_ref, weights_ref, info_ref, sums_ref, router, terms_ref):
        first = first_ref[...].reshape(group, width)
        side = weights_ref[:, side_block * 128 : side_block * 128 + 128].astype(F32)
        gain, bias = side[:, side_at : side_at + 1], side[:, side_at + 1 : side_at + 2]
        gain_sum, bias_sum, last = None, None, None
        for block in range(columns // 128):
            cut = slice(block * 128, block * 128 + 128)
            term = dot_tn(first, dqkv_ref[:, cut])
            weight = weights_ref[:, cut].astype(F32)
            total = jnp.sum(dqkv_ref[:, cut].astype(F32), axis=0, keepdims=True)
            gain_part, bias_part = weight * (term - bias * total), weight * total
            gain_sum = gain_part if gain_sum is None else gain_sum + gain_part
            bias_sum = bias_part if bias_sum is None else bias_sum + bias_part
            if block == side_block:
                last = term
            else:
                terms_ref[:, cut] = term.astype(BF)
        gain_sum = jnp.sum(gain_sum, axis=1, keepdims=True) / gain
        bias_sum = jnp.sum(bias_sum, axis=1, keepdims=True)
        which = lax.broadcasted_iota(jnp.int32, (8, width), 0)
        extra = jnp.where(which == 4, router[...], sums_ref[...])
        balance = info_ref[0:1, 0:1]
        high = balance.astype(BF).astype(F32)
        extra = jnp.where(which == 5, high, jnp.where(which == 6, balance - high, extra))
        lane = lax.broadcasted_iota(jnp.int32, (8, 128), 1)
        which = lax.broadcasted_iota(jnp.int32, (8, 128), 0)
        spread = jnp.where(lane == side_at + which, 1.0, 0.0)
        lane = lax.broadcasted_iota(jnp.int32, (width, 128), 1)
        last = jnp.where(lane == side_at, gain_sum, jnp.where(lane == side_at + 1, bias_sum, last))
        last = last + dot_tn(extra, spread)
        terms_ref[:, side_block * 128 : side_block * 128 + 128] = last.astype(BF)

    ins = [dqkv, first, weights, info, sums, *routers]
    return run(body, [shape((width, columns), BF)], ins, "weight_terms")[0]


def first_parts(where, dqkv, weights, narrow):
    rows, width = dqkv.shape[0] // narrow, weights.shape[0]

    def body(where_ref, dqkv_ref, weights_ref, *parts):
        for place in reversed(range(narrow)):
            at = pl.ds(pl.multiple_of((where_ref[1] ^ place) * rows, rows), rows)
            parts[place][...] = dot_nt(dqkv_ref[at], weights_ref[...]).astype(parts[place].dtype)
            parts[place].push()

    outs = [shape((rows, width), BF if i & 1 else F32) for i in range(narrow)]
    return run(body, outs, [where, dqkv, weights], "first_parts", first_smem=True)


def sum_terms(owns, cuts):
    counts = [len(cut) for cut in cuts]

    def body(*refs):
        sources, rest = refs[: len(owns)], list(refs[len(owns) :])
        outs = rest[sum(counts) :]
        for source, count, out in zip(sources, counts, outs):
            low = 0
            for _ in range(count):
                ref = rest.pop(0)
                at = pl.ds(low, ref.shape[0])
                out[at] = source[at] + ref[...].astype(F32)
                low += ref.shape[0]
            out.push()

    outs = [shape(value.shape, F32) for value in owns]
    return run(body, outs, [*owns, *[v for cut in cuts for v in cut]], "sum_terms")


def turned(row):
    count = row.shape[1]
    at = lax.broadcasted_iota(jnp.int32, (count, count), 0)
    other = lax.broadcasted_iota(jnp.int32, (count, count), 1)
    return jnp.sum(jnp.where(at == other, row, 0.0), axis=1, keepdims=True)


def pack(weights, vectors, w_router, routing, segments, wide, narrow, own_width, columns):
    piece, width = weights[0].shape
    experts = w_router.shape[1]
    rows = routing.shape[0]
    start = 3 * own_width

    def body(wq, wk, wv, va, vb, vc, vd, wr, route, segment, sent, held):
        held[...] = jnp.zeros_like(held)
        ids = lax.broadcasted_iota(jnp.int32, (experts, rows), 0)
        counts = jnp.sum(jnp.where(route[...] == ids, 1.0, 0.0), axis=1, keepdims=True)
        sides = [turned(ref[...]) for ref in (va, vb, vc, vd)]
        sides += [turned(wr[i : i + 1]) for i in range(experts)]
        sides += [counts[i : i + 1] for i in range(experts)]
        sides += [segment[0:1, 0:1].astype(F32)]
        lane = lax.broadcasted_iota(jnp.int32, (piece, 128), 1)
        block = jnp.zeros((piece, 128), F32)
        for i, value in enumerate(sides):
            block = jnp.where(lane == start % 128 + i, value, block)
        for n in range(narrow):
            held[n, :, columns - 128 :] = block
            low, high = n * own_width, min((n + 1) * own_width, width)
            for i, ref in enumerate((wq, wk, wv)):
                if low < high:
                    held[n, :, i * own_width : i * own_width + high - low] = ref[:, low:high]

        def send(w, carry):
            for n in range(narrow):
                sent[w * narrow + n] = held[n].astype(BF)
            return carry

        lax.fori_loop(0, wide, send, 0)

    outs = [shape((wide * narrow, piece, columns), BF)]
    ins = [*weights, *[v.reshape(1, piece) for v in vectors], w_router.T]
    ins += [routing.reshape(1, rows), segments.reshape(1, rows)]
    return run(body, outs, ins, "pack", [pltpu.VMEM((narrow, piece, columns), F32)])[0]


def cast_weights(w_in, w_back, cut):
    def body(first, second, upper, lower, back):
        upper[...] = first[:cut].astype(BF)
        upper.push()
        lower[...] = first[cut:].astype(BF)
        lower.push()
        back[...] = second[...].astype(BF)

    width, hidden = w_in.shape
    outs = [shape((cut, hidden), BF), shape((width - cut, hidden), BF), shape(w_back.shape, BF)]
    return run(body, outs, [w_in, w_back], "cast_weights")


def place_cotangent(routing, cotangent, experts, capacity, piece, copies):
    rows, width = cotangent.shape
    slots = experts * capacity

    def body(route, g, piece_ref, placing, moved, tiled):
        for i in range(copies):
            tiled[i] = piece_ref[...]
        tiled.push()
        ids = lax.broadcasted_iota(jnp.int32, (rows, experts), 1)
        expert = turned(route[...].astype(F32)).astype(jnp.int32)
        hot = jnp.where(expert == ids, 1.0, 0.0)
        row = lax.broadcasted_iota(jnp.int32, (rows, rows), 0)
        column = lax.broadcasted_iota(jnp.int32, (rows, rows), 1)
        before = dot(jnp.where(row > column, 1.0, 0.0).astype(BF), hot.astype(BF))
        slot = jnp.sum(before * hot, axis=1, keepdims=True).astype(jnp.int32)
        target = expert * capacity + slot
        place = lax.broadcasted_iota(jnp.int32, (rows, slots), 1)
        spot = jnp.where(place == target, 1.0, 0.0).astype(BF)
        placing[...] = spot
        moved[...] = dot_tn(spot, g[...]).astype(BF)

    outs = [shape((rows, slots), BF), shape((slots, width), BF), shape((copies, *piece.shape), BF)]
    return run(body, outs, [routing.reshape(1, rows), cotangent, piece], "place_cotangent")


def second_norm(x, halves, vectors, side, stat, placing, routing, where, dims):
    narrow, experts, total, side_at = dims
    rows, width = x.shape
    slots = placing.shape[1]
    count = len(halves)

    def body(where_ref, x_ref, *refs):
        vec, side_ref, stat_ref, placing_ref, route = refs[count : count + 5]
        mixed_ref, moved, gate_ref, info = refs[count + 5 :]
        mixed = x_ref[...].astype(F32)
        for ref in refs[:count]:
            mixed = mixed + ref[...].astype(F32)
        mixed_ref[...] = mixed
        unit, _ = norm_parts(mixed)
        low = (unit * vec[2:3] + vec[3:4]).astype(BF)
        moved[...] = dot_tn(placing_ref[...], low).astype(BF)
        logits = dot(low, side_ref[...])
        lane = lax.broadcasted_iota(jnp.int32, (rows, 128), 1)
        expert = turned(route[...].astype(F32)).astype(jnp.int32)
        chosen = jnp.where(lane - (side_at + 4) == expert, logits, 0.0)
        gate = 1.0 / (1.0 + jnp.exp(-jnp.sum(chosen, axis=1, keepdims=True)))
        gate_ref[...] = gate
        first = side_at + 4 + experts
        sums = jnp.sum(jnp.where(lane - first == expert, gate, 0.0), axis=0, keepdims=True)
        lane = lax.broadcasted_iota(jnp.int32, (1, 128), 1)
        counts = stat_ref[narrow : narrow + 1]
        deviation = (counts - float(total) / experts) * (experts / float(total))
        kept = (lane >= first) & (lane < first + experts)
        balance = experts / float(total) * jnp.sum(
            jnp.where(kept, deviation * sums, 0.0), axis=1, keepdims=True
        )
        own = jnp.sum(
            jnp.where(lane == first + where_ref[0], deviation, 0.0), axis=1, keepdims=True
        )
        core = jnp.where(where_ref[1] % 2 == 0, BALANCE_WEIGHT * (experts / float(total)), 0.0)
        info[...] = jnp.where(lane == 0, balance, own * core) + jnp.zeros((8, 128), F32)

    outs = [shape((rows, width), F32), shape((slots, width), BF), shape((rows, 1), F32)]
    outs.append(shape((8, 128), F32))
    ins = [where, x, *halves, vectors, side, stat, placing, routing.reshape(1, rows)]
    near = range(1, 1 + count)
    return run(body, outs, ins, "second_norm", first_smem=True, close=near)


def second_back(returned, placing, mixed, cotangent, vectors):
    rows, width = mixed.shape

    def body(ret, placing_ref, mixed_ref, g, vec, dr_ref, low_ref, sums):
        incoming = dot(placing_ref[...], ret[...])
        unit, inverse = norm_parts(mixed_ref[...])
        gain = jnp.sum(incoming * unit, axis=0, keepdims=True)
        bias = jnp.sum(incoming, axis=0, keepdims=True)
        dr = g[...].astype(F32) + norm_back(incoming, unit, inverse, vec[2:3])
        dr_ref[...] = dr
        low_ref[...] = dr.astype(BF)
        which = lax.broadcasted_iota(jnp.int32, (8, width), 0)
        sums[...] = jnp.where(which == 2, gain, jnp.where(which == 3, bias, 0.0))

    outs = [shape((rows, width), F32), shape((rows, width), BF), shape((8, width), F32)]
    ins = [returned, placing, mixed, cotangent, vectors]
    return run(body, outs, ins, "second_back", close=(0,), close_outs=(1,))


def finish_rows(returned, placing, mixed, gates):
    def body(ret, placing_ref, mixed_ref, gate, out):
        out[...] = mixed_ref[...] + gate[...] * dot(placing_ref[...], ret[...])

    ins = [returned, placing, mixed, gates]
    return run(body, [shape(mixed.shape, F32)], ins, "finish_rows")[0]


def first_back(halves, x, dr, vectors):
    count = len(halves)

    def body(*refs):
        x_ref, dr_ref, vec, out = refs[count:]
        incoming = refs[0][...].astype(F32)
        for ref in refs[1:count]:
            incoming = incoming + ref[...].astype(F32)
        unit, inverse = norm_parts(x_ref[...].astype(F32))
        out[...] = dr_ref[...] + norm_back(incoming, unit, inverse, vec[0:1])

    return run(body, [shape(x.shape, F32)], [*halves, x, dr, vectors], "first_back")[0]


def unpack(came, wide, narrow, own_width, width, experts):
    piece, columns = came.shape[1:]
    start = 3 * own_width
    side_block, side_at = start // 128, start % 128

    def as_row(column):
        row = lax.broadcasted_iota(jnp.int32, (piece, piece), 0)
        other = lax.broadcasted_iota(jnp.int32, (piece, piece), 1)
        return jnp.sum(jnp.where(row == other, column, 0.0), axis=0, keepdims=True)

    def body(came_ref, gq, gk, gv, va, vb, vc, vd, gr, balance):
        every = jnp.zeros((piece, 128), F32)
        routers = []
        for n in range(narrow):
            total = jnp.zeros((piece, columns), F32)
            for w in range(wide):
                total = total + came_ref[w * narrow + n].astype(F32)
            every = every + total[:, side_block * 128 : side_block * 128 + 128]
            low, high = n * own_width, min((n + 1) * own_width, width)
            if low < high:
                for i, ref in enumerate((gq, gk, gv)):
                    ref[:, low:high] = total[:, i * own_width : i * own_width + high - low]
        for w in range(wide):
            column = jnp.zeros((piece, 1), F32)
            at = start + 4
            for n in range(narrow):
                column = column + came_ref[w * narrow + n, :, at : at + 1].astype(F32)
            gr[w : w + 1] = as_row(column)
        for i, ref in enumerate((va, vb, vc, vd)):
            ref[...] = as_row(every[:, side_at + i : side_at + i + 1])
        balance[...] = every[0:1, side_at + 5 : side_at + 6] + every[0:1, side_at + 6 : side_at + 7]

    outs = [shape((piece, width), F32)] * 3 + [shape((1, piece), F32)] * 4
    outs += [shape((experts, piece), F32), shape((1, 1), F32)]
    return run(body, outs, [came], "unpack", close=(0,))


def local(
    hidden_in,
    segments,
    routing,
    first_gain,
    first_bias,
    second_gain,
    second_bias,
    w_query,
    w_key,
    w_value,
    w_out,
    w_router,
    w_in,
    w_back,
    cotangent,
):
    wide = lax.axis_size("wide")
    narrow = lax.axis_size("narrow")
    devices = wide * narrow
    rows, width = hidden_in.shape
    piece = w_query.shape[0]
    experts = w_router.shape[1]
    capacity = max(2, 2 * rows // experts)
    total = rows * devices
    own_heads = -(-HEADS // narrow)
    own_width = own_heads * HEAD_DIM
    aligned = own_width * narrow == width and own_width == piece * wide
    at_wide = lax.axis_index("wide")
    at_narrow = lax.axis_index("narrow")
    where = jnp.stack([at_wide, at_narrow]).astype(jnp.int32)
    bits = [1 << level for level in range(narrow.bit_length() - 1)]
    core_bit, chip_bits = bits[:1], bits[1:]
    side_start = 3 * own_width
    side_block, side_at = side_start // 128, side_start % 128
    seg_lane = side_at + 4 + 2 * experts
    assert seg_lane < 128
    columns = side_block * 128 + 128
    gate = lax.optimization_barrier

    def swap(values, bit):
        return lax.ppermute(values, "narrow", [(i, i ^ bit) for i in range(narrow)])

    def gather_blocks(block, over):
        blocks = {0: block}
        for bit in reversed(over):
            for place in list(blocks):
                blocks[place ^ bit] = swap(blocks[place], bit)
        return blocks

    def reduce_blocks(blocks, over):
        blocks = dict(blocks)
        for bit in over:
            for place in sorted(blocks, reverse=True):
                if place & bit:
                    moved = swap(blocks.pop(place).astype(BF), bit).astype(F32)
                    blocks[place ^ bit] = blocks[place ^ bit] + moved
        return blocks

    def exchange(values):
        values = values.reshape(experts, capacity, width)
        return to_all(values, "wide").reshape(experts * capacity, width)

    sent = pack(
        [w_query, w_key, w_value], [first_gain, first_bias, second_gain, second_bias],
        w_router, routing, segments, wide, narrow, own_width, columns,
    )
    x_blocks = gather_blocks(hidden_in, chip_bits)
    out_low = w_out.astype(BF)
    if aligned:
        out_low = lax.ppermute(
            out_low, BOTH, [(n * wide + j, j * narrow + n) for n in range(narrow) for j in range(wide)]
        )
    sent, out_low, where, first_w, second_w = gate((sent, out_low, where, w_in[0], w_back[0]))
    *in_low, back_low = cast_weights(first_w, second_w, width // 3)
    weights = to_all(sent, BOTH).reshape(width, columns)
    for place in list(x_blocks):
        x_blocks[place ^ 1] = swap(x_blocks[place], 1)
    partners = [i for i in range(2, narrow, 2)]
    in_upper = [swap(in_low[0], i) for i in partners]
    placing, g_moved, out_tiled = place_cotangent(
        routing, cotangent, experts, capacity, out_low, wide
    )
    weights, in_low, back_low, g_moved, in_upper, out_tiled = gate(
        (weights, in_low, back_low, g_moved, in_upper, out_tiled)
    )
    back_came = [swap(back_low, i) for i in partners]
    if aligned:
        out_w = to_all(out_tiled, "wide").reshape(own_width, width)
    else:
        all_out = lax.all_gather(out_low, BOTH, axis=0, tiled=True)
        all_out = jnp.pad(all_out, ((0, own_width * narrow - width), (0, 0)))
        out_w = lax.dynamic_slice_in_dim(all_out, at_narrow * own_width, own_width, axis=0)

    x_list = [x_blocks[i] for i in range(narrow)]
    first, q, k, v, att, lse, vectors, stat, side = attention(
        where, x_list, weights, own_heads, piece, side_block, side_at, experts
    )
    att, g_moved = gate((att, g_moved))
    g_own = exchange(g_moved)
    parts = project(where, att, out_w, narrow)
    halves = reduce_blocks({i: parts[i] for i in range(narrow)}, core_bit)
    halves, back_came = gate((halves, back_came))
    halves = {i: swap(halves[i].astype(BF), i) if i else halves[i] for i in sorted(halves)}

    halves, g_own, in_low = gate((halves, g_own, in_low))
    in_lower = [swap(in_low[1], i) for i in partners]
    mixed, x_moved, gates, info = second_norm(
        hidden_in, [halves[i] for i in sorted(halves)], vectors, side, stat, placing, routing,
        where, (narrow, experts, total, side_at),
    )
    g_other = swap(g_own, 1)
    x_own = exchange(x_moved)
    x_own, in_lower = gate((x_own, in_lower))
    x_other = swap(x_own, 1)

    ins = [list(pair) for pair in zip(in_upper, in_lower)] + [in_low]
    backs = [*back_came, back_low]
    xs = [x_other, x_own]
    dx_o, dx_s, router, dy, acts, dzs, far_back = expert(info, xs, [g_other, g_own], vectors, ins, backs)

    def cross(cut):
        return [swap(value, place) for value, place in zip(cut, partners)]

    dx_sum = (dx_s + swap(dx_o, 1).astype(F32)).astype(BF)
    d_returned = exchange(dx_sum)
    acts, dx_sum = gate((acts, dx_sum))
    far_back = cross(far_back)
    ends = (0, width // 6, width * 2 // 3, width)
    y_o, y_s, made = partner_terms(xs, acts, dzs, backs, ends)
    own_back, own_in = own_terms(xs, dy, acts[-1], dzs[-1])
    y_sum = (y_s + swap(y_o, 1).astype(F32)).astype(BF)
    made, far_back, own_back, own_in, y_sum = gate((made, far_back, own_back, own_in, y_sum))
    crossed = [cross(made[0])]
    d_mixed, d_mixed_low, sums = second_back(d_returned, placing, mixed, cotangent, vectors)
    d_mixed_low, y_sum, crossed = gate((d_mixed_low, y_sum, crossed))
    returned = exchange(y_sum)
    dr_blocks = gather_blocks(d_mixed_low, chip_bits)
    for place in list(dr_blocks):
        dr_blocks[place ^ 1] = swap(dr_blocks[place], 1)
    dr_blocks, made = gate((dr_blocks, made))
    crossed.append(cross(made[1]))
    dr_list = [dr_blocks[i] for i in range(narrow)]

    d_qkv, terms_out = attention_back(
        where, dr_list, out_w, q, k, v, lse, stat, att, columns, seg_lane
    )
    d_qkv, crossed, terms_out, returned, made = gate((d_qkv, crossed, terms_out, returned, made))
    last_cross = cross(made[2])
    if aligned:
        terms_out = to_all(terms_out.reshape(wide, piece, width), "wide")
    terms = weight_terms(d_qkv, first, weights, info, sums, [router], side_block, side_at)

    tied = (terms, d_qkv, returned, terms_out, last_cross)
    terms, d_qkv, returned, terms_out, last_cross = gate(tied)
    d_parts = first_parts(where, d_qkv, weights, narrow)
    crossed.append(last_cross)
    terms = to_all(terms.reshape(devices, piece, columns), BOTH)
    d_halves = reduce_blocks({i: d_parts[i] for i in range(narrow)}, core_bit)
    d_halves = [swap(d_halves[i].astype(BF), i) if i else d_halves[i] for i in sorted(d_halves)]
    if aligned:
        grad_out_w = lax.ppermute(
            jnp.sum(terms_out.astype(F32), axis=0),
            BOTH,
            [(j * narrow + n, n * wide + j) for n in range(narrow) for j in range(wide)],
        )
    else:
        spread = jnp.zeros((own_width * narrow, width), F32)
        spread = lax.dynamic_update_slice_in_dim(
            spread, terms_out.astype(F32), at_narrow * own_width, axis=0
        )
        grad_out_w = lax.psum_scatter(spread[:width], BOTH, scatter_dimension=0, tiled=True)
    block_out = finish_rows(returned, placing, mixed, gates)
    grad_hidden = first_back(d_halves, hidden_in, d_mixed, vectors)
    back_terms, in_terms = sum_terms([own_back, own_in], [far_back[:1], [cut[0] for cut in crossed]])
    for i in range(1, len(partners)):
        back_terms = back_terms + far_back[i].astype(F32)
        in_terms = in_terms + jnp.concatenate([cut[i] for cut in crossed], axis=0).astype(F32)

    done = unpack(terms, wide, narrow, own_width, width, experts)
    return (
        block_out,
        done[8].reshape(()),
        grad_hidden,
        *[done[i].reshape(piece) for i in range(3, 7)],
        *done[:3],
        grad_out_w,
        done[7].T,
        in_terms[None],
        back_terms[None],
    )


def solution(mesh):
    rows = P(BOTH, None)
    vector = P(BOTH)
    placed = (rows, vector, rows) + (vector,) * 4 + (rows,) * 5
    expert_specs = (P("wide", None, "narrow"), P("wide", "narrow", None))
    return jax.shard_map(
        local,
        mesh=mesh,
        in_specs=placed + expert_specs + (rows,),
        out_specs=(rows, P(), rows) + (vector,) * 4 + (rows,) * 5 + expert_specs,
        check_vma=False,
    )
```

```python
import jax
import jax.numpy as jnp
from jax import lax
from jax.experimental import pallas as pl
from jax.experimental.pallas import tpu as pltpu
from jax.sharding import PartitionSpec as P

HEADS = 12
HEAD_DIM = 64
EPSILON = 1e-05
FLOOR_SCORE = -1e30
SCALE_FACTOR = 0.125
BALANCE_WEIGHT = 0.01
BOTH = ("wide", "narrow")
BF = jnp.bfloat16
F32 = jnp.float32


def dot(left, right):
    return jnp.dot(left, right, preferred_element_type=F32)


def dot_nt(left, right):
    return lax.dot_general(left, right, (((1,), (1,)), ((), ())), preferred_element_type=F32)


def dot_tn(left, right):
    return lax.dot_general(left, right, (((0,), (0,)), ((), ())), preferred_element_type=F32)


def norm_parts(values):
    centered = values - jnp.mean(values, axis=1, keepdims=True)
    inverse = lax.rsqrt(jnp.mean(centered * centered, axis=1, keepdims=True) + EPSILON)
    return centered * inverse, inverse


def norm_back(incoming, unit, inverse, gain):
    scaled = incoming * gain
    return inverse * (
        scaled
        - jnp.mean(scaled, axis=1, keepdims=True)
        - unit * jnp.mean(scaled * unit, axis=1, keepdims=True)
    )


def to_all(values, axes):
    return lax.all_to_all(values, axes, split_axis=0, concat_axis=0, tiled=True)


SMALL = pl.CostEstimate(flops=1000, bytes_accessed=1000, transcendentals=0)
LARGE = pl.CostEstimate(flops=int(2.5e10), bytes_accessed=int(3e7), transcendentals=0)
FILLERS = ("place_cotangent", "cast_weights")


class Held:
    def __init__(self, ref, copies, fetched):
        self.ref, self.copies = ref, copies
        self.waiting = list(range(len(copies))) if fetched else []
        self.started = set(self.waiting)

    def get(self):
        for i in self.waiting:
            self.copies[i].wait()
        self.waiting = []
        return self.ref

    def push(self, part=None):
        for i in range(len(self.copies)) if part is None else [part]:
            if i not in self.started and i < len(self.copies):
                self.copies[i].start()
                self.waiting.append(i)
                self.started.add(i)

    @property
    def shape(self):
        return self.ref.shape

    @property
    def dtype(self):
        return self.ref.dtype

    def __getitem__(self, at):
        return self.get()[at]

    def __setitem__(self, at, value):
        self.ref[at] = value


def padded(value):
    lanes = -(-value.shape[-1] // 128) * 128
    rows = -(-value.shape[-2] // 16) * 16 if len(value.shape) > 1 else 16
    outer = 1
    for size in value.shape[:-2]:
        outer *= size
    return outer * rows * lanes * jnp.dtype(value.dtype).itemsize


def run(body, outs, ins, name, scratch=(), first_smem=False, pieces=None, close=(), close_outs=(), room=10):
    outs, ins = list(outs), list(ins)
    lead = 1 if first_smem else 0
    fetched, total = len(ins) - lead, len(ins) - lead + len(outs)
    arrays = ins[lead:] + outs
    near = [i in close if i < fetched else i - fetched in close_outs for i in range(total)]
    cuts = [(pieces or {}).get(i - fetched, [()]) for i in range(total)]
    slots, semaphores, used = {}, {}, 0
    for i in range(total):
        if not near[i]:
            slots[i], semaphores[i] = len(slots), used
            used += len(cuts[i])
    buffers = [pltpu.VMEM(arrays[i].shape, arrays[i].dtype) for i in slots]

    def kernel(*refs):
        smem_refs, given = refs[:lead], refs[lead : lead + total]
        own = refs[lead + total : lead + total + len(slots)]
        marks = refs[lead + total + len(slots)]
        held = []
        for i in range(total):
            if near[i]:
                held.append(Held(given[i], [], False))
                continue
            mine = own[slots[i]]
            source, target = (given[i], mine) if i < fetched else (mine, given[i])
            copies = []
            for j, at in enumerate(cuts[i]):
                ends = (source.at[at], target.at[at]) if at else (source, target)
                copies.append(pltpu.make_async_copy(*ends, marks.at[semaphores[i] + j]))
            if i < fetched:
                copies[0].start()
            held.append(Held(mine, copies, i < fetched))
        body(*smem_refs, *held, *refs[lead + total + len(slots) + 1 :])
        for item in held[fetched:]:
            item.push()
        for item in held:
            item.get()

    hbm, vmem = pl.BlockSpec(memory_space=pltpu.HBM), pl.BlockSpec(memory_space=pltpu.VMEM)
    ins = [
        value if i < lead or near[i - lead] else pltpu.with_memory_space_constraint(value, pltpu.HBM)
        for i, value in enumerate(ins)
    ]
    placed = [
        value if near[fetched + i] else pltpu.HBM(value.shape, value.dtype)
        for i, value in enumerate(outs)
    ]
    size = sum(padded(arrays[i]) for i in slots) + sum(padded(value) for value in scratch)
    limit = min(60, size // 2**20 + 1 + room)
    return pl.pallas_call(
        kernel,
        out_shape=placed,
        in_specs=([smem()] if first_smem else []) + [vmem if near[i] else hbm for i in range(fetched)],
        out_specs=[vmem if near[fetched + i] else hbm for i in range(len(outs))],
        scratch_shapes=[*buffers, pltpu.SemaphoreType.DMA((max(1, used),)), *scratch],
        compiler_params=pltpu.CompilerParams(vmem_limit_bytes=limit * 1024 * 1024),
        cost_estimate=LARGE if name in FILLERS else SMALL,
        name=name,
    )(*ins)


def shape(dims, dtype):
    return jax.ShapeDtypeStruct(dims, dtype)


def smem():
    return pl.BlockSpec(memory_space=pltpu.SMEM)


def earlier_keys(size):
    key = lax.broadcasted_iota(jnp.int32, (size, size), 0)
    query = lax.broadcasted_iota(jnp.int32, (size, size), 1)
    return key <= query


def attention_kernel(
    narrow, own_heads, piece, side_block, side_at, experts,
    where_ref, x_refs, weights_ref,
    first_ref, q_ref, k_ref, v_ref, att_ref, lse_ref, rows_ref, stat_ref, side_ref,
):
    rows, width = x_refs[0].shape
    at_wide, at_narrow = where_ref[0], where_ref[1]
    side = weights_ref[:, side_block * 128 : side_block * 128 + 128]
    side_ref[...] = side
    lane = lax.broadcasted_iota(jnp.int32, (8, 128), 1)
    which = lax.broadcasted_iota(jnp.int32, (8, 128), 0)
    wanted = jnp.where(which < 4, side_at + which, side_at + 4 + at_wide)
    pick = jnp.where(lane == wanted, 1.0, 0.0)
    vectors = dot_nt(pick, side.astype(F32))
    rows_ref[...] = vectors
    stat_rows = stat_ref.shape[0]
    column = lax.broadcasted_iota(jnp.int32, (stat_rows, width), 1)
    which = lax.broadcasted_iota(jnp.int32, (stat_rows, width), 0)
    segment_row = (at_wide * narrow + which) * piece
    wanted = jnp.where(which < narrow, segment_row, column - lax.rem(column, piece))
    stat = dot(jnp.where(column == wanted, 1.0, 0.0), side.astype(F32))
    stat_ref[...] = stat
    seg_lane = side_at + 4 + 2 * experts
    segs = [stat[i : i + 1, seg_lane : seg_lane + 1] for i in range(narrow)]
    gain, bias = vectors[0:1], vectors[1:2]
    for place in range(narrow):
        unit, _ = norm_parts(x_refs[place][...].astype(F32))
        first_ref[at_narrow ^ place] = (unit * gain + bias).astype(BF)
    first_ref.push()
    own_width = own_heads * HEAD_DIM
    for block in range(narrow):
        at = pl.ds(block * rows, rows)
        qkv = dot(first_ref.ref[block], weights_ref[...])
        for head in range(own_heads):
            low, high = head * HEAD_DIM, (head + 1) * HEAD_DIM
            q_ref[head, at] = (qkv[:, low:high].astype(BF).astype(F32) * SCALE_FACTOR).astype(BF)
            k_ref[head, at] = qkv[:, own_width + low : own_width + high].astype(BF)
            v_ref[head, at] = qkv[:, 2 * own_width + low : 2 * own_width + high].astype(BF)
    for ref in (q_ref, k_ref, v_ref):
        ref.push()
    mask = earlier_keys(rows)
    for head in range(own_heads):
        for block in range(narrow):
            at = pl.ds(block * rows, rows)
            query = q_ref.ref[head, at]
            keys = pl.ds(0, (block + 1) * rows)
            score = dot_nt(k_ref.ref[head, keys], query)
            scores = []
            for other in range(block + 1):
                piece = score[other * rows : (other + 1) * rows]
                if other == block:
                    scores.append(jnp.where(mask, piece, FLOOR_SCORE))
                else:
                    scores.append(piece + jnp.where(segs[block] == segs[other], 0.0, FLOOR_SCORE))
            score = scores[0] if block == 0 else jnp.concatenate(scores, axis=0)
            top = score.max(axis=0, keepdims=True)
            value = jnp.exp(score - top)
            total = value.sum(axis=0, keepdims=True)
            att = dot_tn((value * (1.0 / total)).astype(BF), v_ref.ref[head, keys])
            att_ref[at, head * HEAD_DIM : (head + 1) * HEAD_DIM] = att.astype(BF)
            lse_ref[head, :, at] = top + jnp.log(total)


def project(where, att, out_w, narrow):
    rows, width = att.shape[0] // narrow, out_w.shape[1]

    def body(where_ref, att_ref, out_w_ref, *parts):
        for place in reversed(range(narrow)):
            at = pl.ds(pl.multiple_of((where_ref[1] ^ place) * rows, rows), rows)
            parts[place][...] = dot(att_ref[at], out_w_ref[...]).astype(parts[place].dtype)
            parts[place].push()

    outs = [shape((rows, width), BF if i & 1 else F32) for i in range(narrow)]
    return run(
        body, outs, [where, att, out_w], "project", first_smem=True, close=(0,), close_outs=range(narrow)
    )


def attention(where, x_blocks, weights, own_heads, piece, side_block, side_at, experts):
    narrow = len(x_blocks)
    rows, width = x_blocks[0].shape
    group = rows * narrow
    stat_rows = -(-(narrow + 1) // 8) * 8
    head_shape = jax.ShapeDtypeStruct((own_heads, group, HEAD_DIM), BF)
    outs = (
        [jax.ShapeDtypeStruct((narrow, rows, width), BF)]
        + [head_shape] * 3
        + [shape((group, own_heads * HEAD_DIM), BF)]
        + [jax.ShapeDtypeStruct((own_heads, 1, group), F32)]
        + [shape((8, width), F32), shape((stat_rows, 128), F32), shape((width, 128), BF)]
    )

    def body(where_ref, *refs):
        attention_kernel(
            narrow, own_heads, piece, side_block, side_at, experts,
            where_ref, refs[:narrow], *refs[narrow:],
        )

    ins = [where, *x_blocks, weights]
    near = range(narrow + 1)
    return run(body, outs, ins, "attention_forward", first_smem=True, close=near, close_outs=(4,))


def gelu_pieces(z):
    size = jnp.abs(z)
    fall = jnp.exp(z * z * -0.5)
    t = 1.0 / (1.0 + size * (0.3275911 * 0.7071067811865476))
    tail = 1.061405429 * 0.5
    for term in (-1.453152027, 1.421413741, -0.284496736, 0.254829592):
        tail = tail * t + term * 0.5
    tail = tail * t * fall
    upper = jnp.where(z < 0.0, tail, 1.0 - tail)
    return upper, z * fall * 0.3989422804014327


def expert_share(x, dy, w_in, w_back, act_ref, dz_ref, at):
    first = w_in[0][...] if len(w_in) == 1 else jnp.concatenate([cut[...] for cut in w_in], axis=0)
    z = dot(x, first)
    upper, bump = gelu_pieces(z)
    act = (z * upper).astype(BF)
    act_ref[at] = act
    du = dot_nt(dy, w_back[...])
    dz = (du * (upper + bump)).astype(BF)
    dz_ref[at] = dz
    dx = dot_nt(dz, first)
    return dx, jnp.sum(act.astype(F32) * du, axis=1, keepdims=True)


def row_gate(x, vectors):
    score = jnp.sum(x.astype(F32) * vectors[4:5], axis=1, keepdims=True)
    return 1.0 / (1.0 + jnp.exp(-score))


STEP = 256


def expert(info, xs, gs, vectors, ins, backs):
    count, width = xs[0].shape
    hidden = backs[0].shape[0]
    shares, cuts = len(backs), len(ins[0])
    blocks = [(half, start) for half in range(2) for start in range(0, count, STEP)]

    def body(info_ref, vec, *refs):
        x_refs, w1_first, w2_first, g_refs = refs[:2], refs[2 : 2 + cuts], refs[2 + cuts], refs[3 + cuts : 5 + cuts]
        rest, o = refs[5 + cuts : 4 + shares * (cuts + 1)], refs[4 + shares * (cuts + 1) :]
        w1 = [w1_first] + [rest[i * (cuts + 1) : i * (cuts + 1) + cuts] for i in range(shares - 1)]
        w2 = [w2_first] + [rest[i * (cuts + 1) + cuts] for i in range(shares - 1)]
        dx_refs, router, dy, acts, dzs = o[:2], o[2], o[3], o[4 : 4 + shares], o[4 + shares : 4 + 2 * shares]
        back_refs = o[4 + 2 * shares : 3 + 3 * shares]
        dx_acc, score_acc = o[3 + 3 * shares :]
        router_sum = jnp.zeros((1, width), F32)
        for i in range(shares):
            for number, (half, start) in enumerate(blocks):
                at = pl.ds(start, min(STEP, count))
                rows = x_refs[half][at]
                if i == 0:
                    gate = row_gate(rows, vec)
                    dy[half, at] = (gate * g_refs[half][at].astype(F32)).astype(BF)
                    dy.push(number)
                dx, score = expert_share(
                    rows, dy.ref[half, at], w1[i], w2[i], acts[i].ref.at[half], dzs[i].ref.at[half], at
                )
                acts[i].push(number)
                dzs[i].push(number)
                if i > 0:
                    dx, score = dx + dx_acc[half, at], score + score_acc[half, at]
                if i < shares - 1:
                    dx_acc[half, at], score_acc[half, at] = dx, score
                else:
                    gate = row_gate(rows, vec)
                    dlogit = (score + info_ref[0:1, 1:2] * gate) * (1.0 - gate)
                    router_sum = router_sum + jnp.sum(
                        rows.astype(F32) * dlogit, axis=0, keepdims=True
                    )
                    dx_refs[half][at] = (dx + dlogit * vec[4:5]).astype(dx_refs[half].dtype)
                    if start + STEP >= count:
                        dx_refs[half].push()
            if i < shares - 1:
                act, grad = acts[i].ref, dy.ref
                back_refs[i][...] = (dot_tn(act[0], grad[0]) + dot_tn(act[1], grad[1])).astype(BF)
                back_refs[i].push()
        router[...] = router_sum

    outs = [shape((count, width), BF), shape((count, width), F32), shape((1, width), F32)]
    outs += [shape((2, count, width), BF)] + [shape((2, count, hidden), BF)] * (2 * shares)
    parts = len(outs)
    outs += [shape((hidden, width), BF)] * (shares - 1)
    cut = [(half, pl.ds(start, min(STEP, count))) for half, start in blocks]
    operands = [info, vectors, *xs, *ins[0], backs[0], *gs]
    for i in range(1, shares):
        operands += [*ins[i], backs[i]]
    scratch = [pltpu.VMEM((2, count, width), F32), pltpu.VMEM((2, count, 1), F32)]
    pieces = {i: cut for i in range(3, parts)}
    near = (2, 3)
    res = run(body, outs, operands, "expert", scratch, pieces=pieces, close=near, close_outs=(0, 1))
    res = list(res)
    acts, dzs = res[4 : 4 + shares], res[4 + shares : parts]
    return res[0], res[1], res[2], res[3], acts, dzs, res[parts:]


def partner_terms(xs, acts, dzs, backs, ends):
    shares = len(acts)
    count, width, hidden = shares - 1, xs[0].shape[1], acts[0].shape[2]
    cuts = [slice(*pair) for pair in zip(ends, ends[1:])]

    def body(*refs):
        x_refs, dz, act, back = refs[:2], refs[2 : 2 + count], refs[2 + count :][:shares], refs[2 + count + shares :][:shares]
        y_refs, outs = refs[2 + count + 2 * shares :][:2], list(refs[4 + count + 2 * shares :])
        for at in cuts:
            for i in range(count):
                out = outs.pop(0)
                term = dot_tn(x_refs[0][:, at], dz[i][0]) + dot_tn(x_refs[1][:, at], dz[i][1])
                out[...] = term.astype(BF)
                out.push()
        for half, out in enumerate(y_refs):
            total = dot(act[0][half], back[0][...])
            for i in range(1, shares):
                total = total + dot(act[i][half], back[i][...])
            out[...] = total.astype(out.dtype)
            out.push()

    outs = [shape(xs[0].shape, BF), shape(xs[0].shape, F32)]
    outs += [shape((at.stop - at.start, hidden), BF) for at in cuts for _ in range(count)]
    res = run(body, outs, [*xs, *dzs[:-1], *acts, *backs], "partner_terms")
    return res[0], res[1], [list(res[i : i + count]) for i in range(2, len(outs), count)]


def own_terms(xs, dy, act, dz):
    def body(act, dy, x_a, x_b, dz, own_back, own_in):
        own_back[...] = dot_tn(act[0], dy[0]) + dot_tn(act[1], dy[1])
        own_back.push()
        own_in[...] = dot_tn(x_a[...], dz[0]) + dot_tn(x_b[...], dz[1])

    width, hidden = xs[0].shape[1], act.shape[2]
    outs = [shape((hidden, width), F32), shape((width, hidden), F32)]
    return run(body, outs, [act, dy, *xs, dz], "own_terms")


def attention_back_kernel(
    narrow, own_heads, columns, seg_lane,
    where_ref, dr_refs, out_w_ref, q_ref, k_ref, v_ref, lse_ref, stat_ref, att_ref,
    dqkv_ref, out_terms_ref,
    dr_all, da, dk_acc, dv_acc,
):
    rows, width = dr_refs[0].shape
    group = rows * narrow
    own_width = own_heads * HEAD_DIM
    at_narrow = where_ref[1]
    for place in range(narrow):
        dr_all[at_narrow ^ place] = dr_refs[place][...]
    dqkv = dqkv_ref.ref
    segs = [stat_ref[i : i + 1, seg_lane : seg_lane + 1] for i in range(narrow)]
    mask = earlier_keys(rows)
    dqkv[:, columns - 128 :] = jnp.zeros((group, 128), BF)
    for block in range(narrow):
        at = pl.ds(block * rows, rows)
        d_att = dot_nt(dr_all[block], out_w_ref[...]).astype(BF)
        for head in range(own_heads):
            da[head, at] = d_att[:, head * HEAD_DIM : (head + 1) * HEAD_DIM]
    for head in range(own_heads):
        low, high = head * HEAD_DIM, (head + 1) * HEAD_DIM
        for block in reversed(range(narrow)):
            at = pl.ds(block * rows, rows)
            query, d_att, lse = q_ref[head, at], da[head, at], lse_ref[head, :, at]
            probs, d_probs, delta = [], [], None
            for other in range(block + 1):
                keys = pl.ds(other * rows, rows)
                score = dot_nt(k_ref[head, keys], query)
                if other == block:
                    prob = jnp.where(mask, jnp.exp(score - lse), 0.0)
                else:
                    prob = jnp.exp(
                        score - (lse + jnp.where(segs[block] == segs[other], 0.0, -FLOOR_SCORE))
                    )
                d_prob = dot_nt(v_ref[head, keys], d_att)
                part = jnp.sum(prob * d_prob, axis=0, keepdims=True)
                delta = part if delta is None else delta + part
                probs.append(prob)
                d_probs.append(d_prob)
            dq = None
            for other in range(block + 1):
                keys = pl.ds(other * rows, rows)
                d_score = (probs[other] * (d_probs[other] - delta)).astype(BF)
                term = dot_tn(d_score, k_ref[head, keys])
                dq = term if dq is None else dq + term
                dk = dot(d_score, query)
                dv = dot(probs[other].astype(BF), d_att)
                if block == narrow - 1:
                    dk_acc[keys] = dk
                    dv_acc[keys] = dv
                else:
                    dk_acc[keys] += dk
                    dv_acc[keys] += dv
            dqkv[at, low:high] = (dq * SCALE_FACTOR).astype(BF)
        dqkv[:, own_width + low : own_width + high] = dk_acc[...].astype(BF)
        dqkv[:, 2 * own_width + low : 2 * own_width + high] = dv_acc[...].astype(BF)
    dqkv_ref.push()
    out_terms_ref[...] = dot_tn(att_ref[...], dr_all[...].reshape(group, width)).astype(BF)


def attention_back(where, dr_blocks, out_w, q, k, v, lse, stat, att, columns, seg_lane):
    narrow = len(dr_blocks)
    rows, width = dr_blocks[0].shape
    group = rows * narrow
    own_heads = q.shape[0]
    outs = [shape((group, columns), BF), shape((own_heads * HEAD_DIM, width), BF)]

    def body(where_ref, *refs):
        attention_back_kernel(
            narrow, own_heads, columns, seg_lane, where_ref, refs[:narrow], *refs[narrow:]
        )

    scratch = [
        pltpu.VMEM((narrow, rows, width), BF),
        pltpu.VMEM((own_heads, group, HEAD_DIM), BF),
        pltpu.VMEM((group, HEAD_DIM), F32),
        pltpu.VMEM((group, HEAD_DIM), F32),
    ]
    ins = [where, *dr_blocks, out_w, q, k, v, lse, stat, att]
    near = range(narrow)
    return run(body, outs, ins, "attention_backward", scratch, first_smem=True, close=near)


def weight_terms(dqkv, first, weights, info, sums, routers, side_block, side_at):
    group, columns = dqkv.shape
    width = weights.shape[0]
    def body(dqkv_ref, first_ref, weights_ref, info_ref, sums_ref, router, terms_ref):
        first = first_ref[...].reshape(group, width)
        side = weights_ref[:, side_block * 128 : side_block * 128 + 128].astype(F32)
        gain, bias = side[:, side_at : side_at + 1], side[:, side_at + 1 : side_at + 2]
        gain_sum, bias_sum, last = None, None, None
        for block in range(columns // 128):
            cut = slice(block * 128, block * 128 + 128)
            term = dot_tn(first, dqkv_ref[:, cut])
            weight = weights_ref[:, cut].astype(F32)
            total = jnp.sum(dqkv_ref[:, cut].astype(F32), axis=0, keepdims=True)
            gain_part, bias_part = weight * (term - bias * total), weight * total
            gain_sum = gain_part if gain_sum is None else gain_sum + gain_part
            bias_sum = bias_part if bias_sum is None else bias_sum + bias_part
            if block == side_block:
                last = term
            else:
                terms_ref[:, cut] = term.astype(BF)
        gain_sum = jnp.sum(gain_sum, axis=1, keepdims=True) / gain
        bias_sum = jnp.sum(bias_sum, axis=1, keepdims=True)
        which = lax.broadcasted_iota(jnp.int32, (8, width), 0)
        extra = jnp.where(which == 4, router[...], sums_ref[...])
        balance = info_ref[0:1, 0:1]
        high = balance.astype(BF).astype(F32)
        extra = jnp.where(which == 5, high, jnp.where(which == 6, balance - high, extra))
        lane = lax.broadcasted_iota(jnp.int32, (8, 128), 1)
        which = lax.broadcasted_iota(jnp.int32, (8, 128), 0)
        spread = jnp.where(lane == side_at + which, 1.0, 0.0)
        lane = lax.broadcasted_iota(jnp.int32, (width, 128), 1)
        last = jnp.where(lane == side_at, gain_sum, jnp.where(lane == side_at + 1, bias_sum, last))
        last = last + dot_tn(extra, spread)
        terms_ref[:, side_block * 128 : side_block * 128 + 128] = last.astype(BF)

    ins = [dqkv, first, weights, info, sums, *routers]
    return run(body, [shape((width, columns), BF)], ins, "weight_terms")[0]


def first_parts(where, dqkv, weights, narrow):
    rows, width = dqkv.shape[0] // narrow, weights.shape[0]

    def body(where_ref, dqkv_ref, weights_ref, *parts):
        for place in reversed(range(narrow)):
            at = pl.ds(pl.multiple_of((where_ref[1] ^ place) * rows, rows), rows)
            parts[place][...] = dot_nt(dqkv_ref[at], weights_ref[...]).astype(parts[place].dtype)
            parts[place].push()

    outs = [shape((rows, width), BF if i & 1 else F32) for i in range(narrow)]
    return run(body, outs, [where, dqkv, weights], "first_parts", first_smem=True)


def sum_terms(owns, cuts):
    counts = [len(cut) for cut in cuts]

    def body(*refs):
        sources, rest = refs[: len(owns)], list(refs[len(owns) :])
        outs = rest[sum(counts) :]
        for source, count, out in zip(sources, counts, outs):
            low = 0
            for _ in range(count):
                ref = rest.pop(0)
                at = pl.ds(low, ref.shape[0])
                out[at] = source[at] + ref[...].astype(F32)
                low += ref.shape[0]
            out.push()

    outs = [shape(value.shape, F32) for value in owns]
    return run(body, outs, [*owns, *[v for cut in cuts for v in cut]], "sum_terms")


def turned(row):
    count = row.shape[1]
    at = lax.broadcasted_iota(jnp.int32, (count, count), 0)
    other = lax.broadcasted_iota(jnp.int32, (count, count), 1)
    return jnp.sum(jnp.where(at == other, row, 0.0), axis=1, keepdims=True)


def pack(weights, vectors, w_router, routing, segments, wide, narrow, own_width, columns):
    piece, width = weights[0].shape
    experts = w_router.shape[1]
    rows = routing.shape[0]
    start = 3 * own_width

    def body(wq, wk, wv, va, vb, vc, vd, wr, route, segment, sent, held):
        held[...] = jnp.zeros_like(held)
        ids = lax.broadcasted_iota(jnp.int32, (experts, rows), 0)
        counts = jnp.sum(jnp.where(route[...] == ids, 1.0, 0.0), axis=1, keepdims=True)
        sides = [turned(ref[...]) for ref in (va, vb, vc, vd)]
        sides += [turned(wr[i : i + 1]) for i in range(experts)]
        sides += [counts[i : i + 1] for i in range(experts)]
        sides += [segment[0:1, 0:1].astype(F32)]
        lane = lax.broadcasted_iota(jnp.int32, (piece, 128), 1)
        block = jnp.zeros((piece, 128), F32)
        for i, value in enumerate(sides):
            block = jnp.where(lane == start % 128 + i, value, block)
        for n in range(narrow):
            held[n, :, columns - 128 :] = block
            low, high = n * own_width, min((n + 1) * own_width, width)
            for i, ref in enumerate((wq, wk, wv)):
                if low < high:
                    held[n, :, i * own_width : i * own_width + high - low] = ref[:, low:high]

        def send(w, carry):
            for n in range(narrow):
                sent[w * narrow + n] = held[n].astype(BF)
            return carry

        lax.fori_loop(0, wide, send, 0)

    outs = [shape((wide * narrow, piece, columns), BF)]
    ins = [*weights, *[v.reshape(1, piece) for v in vectors], w_router.T]
    ins += [routing.reshape(1, rows), segments.reshape(1, rows)]
    return run(body, outs, ins, "pack", [pltpu.VMEM((narrow, piece, columns), F32)])[0]


def cast_weights(w_in, w_back, cut):
    def body(first, second, upper, lower, back):
        upper[...] = first[:cut].astype(BF)
        upper.push()
        lower[...] = first[cut:].astype(BF)
        lower.push()
        back[...] = second[...].astype(BF)

    width, hidden = w_in.shape
    outs = [shape((cut, hidden), BF), shape((width - cut, hidden), BF), shape(w_back.shape, BF)]
    return run(body, outs, [w_in, w_back], "cast_weights")


def place_cotangent(routing, cotangent, experts, capacity, piece, copies):
    rows, width = cotangent.shape
    slots = experts * capacity

    def body(route, g, piece_ref, placing, moved, tiled):
        for i in range(copies):
            tiled[i] = piece_ref[...]
        tiled.push()
        ids = lax.broadcasted_iota(jnp.int32, (rows, experts), 1)
        expert = turned(route[...].astype(F32)).astype(jnp.int32)
        hot = jnp.where(expert == ids, 1.0, 0.0)
        row = lax.broadcasted_iota(jnp.int32, (rows, rows), 0)
        column = lax.broadcasted_iota(jnp.int32, (rows, rows), 1)
        before = dot(jnp.where(row > column, 1.0, 0.0).astype(BF), hot.astype(BF))
        slot = jnp.sum(before * hot, axis=1, keepdims=True).astype(jnp.int32)
        target = expert * capacity + slot
        place = lax.broadcasted_iota(jnp.int32, (rows, slots), 1)
        spot = jnp.where(place == target, 1.0, 0.0).astype(BF)
        placing[...] = spot
        moved[...] = dot_tn(spot, g[...]).astype(BF)

    outs = [shape((rows, slots), BF), shape((slots, width), BF), shape((copies, *piece.shape), BF)]
    return run(body, outs, [routing.reshape(1, rows), cotangent, piece], "place_cotangent")


def second_norm(x, halves, vectors, side, stat, placing, routing, where, dims):
    narrow, experts, total, side_at = dims
    rows, width = x.shape
    slots = placing.shape[1]
    count = len(halves)

    def body(where_ref, x_ref, *refs):
        vec, side_ref, stat_ref, placing_ref, route = refs[count : count + 5]
        mixed_ref, moved, gate_ref, info = refs[count + 5 :]
        mixed = x_ref[...].astype(F32)
        for ref in refs[:count]:
            mixed = mixed + ref[...].astype(F32)
        mixed_ref[...] = mixed
        unit, _ = norm_parts(mixed)
        low = (unit * vec[2:3] + vec[3:4]).astype(BF)
        moved[...] = dot_tn(placing_ref[...], low).astype(BF)
        logits = dot(low, side_ref[...])
        lane = lax.broadcasted_iota(jnp.int32, (rows, 128), 1)
        expert = turned(route[...].astype(F32)).astype(jnp.int32)
        chosen = jnp.where(lane - (side_at + 4) == expert, logits, 0.0)
        gate = 1.0 / (1.0 + jnp.exp(-jnp.sum(chosen, axis=1, keepdims=True)))
        gate_ref[...] = gate
        first = side_at + 4 + experts
        sums = jnp.sum(jnp.where(lane - first == expert, gate, 0.0), axis=0, keepdims=True)
        lane = lax.broadcasted_iota(jnp.int32, (1, 128), 1)
        counts = stat_ref[narrow : narrow + 1]
        deviation = (counts - float(total) / experts) * (experts / float(total))
        kept = (lane >= first) & (lane < first + experts)
        balance = experts / float(total) * jnp.sum(
            jnp.where(kept, deviation * sums, 0.0), axis=1, keepdims=True
        )
        own = jnp.sum(
            jnp.where(lane == first + where_ref[0], deviation, 0.0), axis=1, keepdims=True
        )
        core = jnp.where(where_ref[1] % 2 == 0, BALANCE_WEIGHT * (experts / float(total)), 0.0)
        info[...] = jnp.where(lane == 0, balance, own * core) + jnp.zeros((8, 128), F32)

    outs = [shape((rows, width), F32), shape((slots, width), BF), shape((rows, 1), F32)]
    outs.append(shape((8, 128), F32))
    ins = [where, x, *halves, vectors, side, stat, placing, routing.reshape(1, rows)]
    near = range(1, 1 + count)
    return run(body, outs, ins, "second_norm", first_smem=True, close=near)


def second_back(returned, placing, mixed, cotangent, vectors):
    rows, width = mixed.shape

    def body(ret, placing_ref, mixed_ref, g, vec, dr_ref, low_ref, sums):
        incoming = dot(placing_ref[...], ret[...])
        unit, inverse = norm_parts(mixed_ref[...])
        gain = jnp.sum(incoming * unit, axis=0, keepdims=True)
        bias = jnp.sum(incoming, axis=0, keepdims=True)
        dr = g[...].astype(F32) + norm_back(incoming, unit, inverse, vec[2:3])
        dr_ref[...] = dr
        low_ref[...] = dr.astype(BF)
        which = lax.broadcasted_iota(jnp.int32, (8, width), 0)
        sums[...] = jnp.where(which == 2, gain, jnp.where(which == 3, bias, 0.0))

    outs = [shape((rows, width), F32), shape((rows, width), BF), shape((8, width), F32)]
    ins = [returned, placing, mixed, cotangent, vectors]
    return run(body, outs, ins, "second_back", close=(0,), close_outs=(1,))


def finish_rows(returned, placing, mixed, gates):
    def body(ret, placing_ref, mixed_ref, gate, out):
        out[...] = mixed_ref[...] + gate[...] * dot(placing_ref[...], ret[...])

    ins = [returned, placing, mixed, gates]
    return run(body, [shape(mixed.shape, F32)], ins, "finish_rows")[0]


def first_back(halves, x, dr, vectors):
    count = len(halves)

    def body(*refs):
        x_ref, dr_ref, vec, out = refs[count:]
        incoming = refs[0][...].astype(F32)
        for ref in refs[1:count]:
            incoming = incoming + ref[...].astype(F32)
        unit, inverse = norm_parts(x_ref[...].astype(F32))
        out[...] = dr_ref[...] + norm_back(incoming, unit, inverse, vec[0:1])

    return run(body, [shape(x.shape, F32)], [*halves, x, dr, vectors], "first_back")[0]


def unpack(came, wide, narrow, own_width, width, experts):
    piece, columns = came.shape[1:]
    start = 3 * own_width
    side_block, side_at = start // 128, start % 128

    def as_row(column):
        row = lax.broadcasted_iota(jnp.int32, (piece, piece), 0)
        other = lax.broadcasted_iota(jnp.int32, (piece, piece), 1)
        return jnp.sum(jnp.where(row == other, column, 0.0), axis=0, keepdims=True)

    def body(came_ref, gq, gk, gv, va, vb, vc, vd, gr, balance):
        every = jnp.zeros((piece, 128), F32)
        routers = []
        for n in range(narrow):
            total = jnp.zeros((piece, columns), F32)
            for w in range(wide):
                total = total + came_ref[w * narrow + n].astype(F32)
            every = every + total[:, side_block * 128 : side_block * 128 + 128]
            low, high = n * own_width, min((n + 1) * own_width, width)
            if low < high:
                for i, ref in enumerate((gq, gk, gv)):
                    ref[:, low:high] = total[:, i * own_width : i * own_width + high - low]
        for w in range(wide):
            column = jnp.zeros((piece, 1), F32)
            at = start + 4
            for n in range(narrow):
                column = column + came_ref[w * narrow + n, :, at : at + 1].astype(F32)
            gr[w : w + 1] = as_row(column)
        for i, ref in enumerate((va, vb, vc, vd)):
            ref[...] = as_row(every[:, side_at + i : side_at + i + 1])
        balance[...] = every[0:1, side_at + 5 : side_at + 6] + every[0:1, side_at + 6 : side_at + 7]

    outs = [shape((piece, width), F32)] * 3 + [shape((1, piece), F32)] * 4
    outs += [shape((experts, piece), F32), shape((1, 1), F32)]
    return run(body, outs, [came], "unpack", close=(0,))


def local(
    hidden_in,
    segments,
    routing,
    first_gain,
    first_bias,
    second_gain,
    second_bias,
    w_query,
    w_key,
    w_value,
    w_out,
    w_router,
    w_in,
    w_back,
    cotangent,
):
    wide = lax.axis_size("wide")
    narrow = lax.axis_size("narrow")
    devices = wide * narrow
    rows, width = hidden_in.shape
    piece = w_query.shape[0]
    experts = w_router.shape[1]
    capacity = max(2, 2 * rows // experts)
    total = rows * devices
    own_heads = -(-HEADS // narrow)
    own_width = own_heads * HEAD_DIM
    aligned = own_width * narrow == width and own_width == piece * wide
    at_wide = lax.axis_index("wide")
    at_narrow = lax.axis_index("narrow")
    where = jnp.stack([at_wide, at_narrow]).astype(jnp.int32)
    bits = [1 << level for level in range(narrow.bit_length() - 1)]
    core_bit, chip_bits = bits[:1], bits[1:]
    side_start = 3 * own_width
    side_block, side_at = side_start // 128, side_start % 128
    seg_lane = side_at + 4 + 2 * experts
    assert seg_lane < 128
    columns = side_block * 128 + 128
    gate = lax.optimization_barrier

    def swap(values, bit):
        return lax.ppermute(values, "narrow", [(i, i ^ bit) for i in range(narrow)])

    def gather_blocks(block, over):
        blocks = {0: block}
        for bit in reversed(over):
            for place in list(blocks):
                blocks[place ^ bit] = swap(blocks[place], bit)
        return blocks

    def reduce_blocks(blocks, over):
        blocks = dict(blocks)
        for bit in over:
            for place in sorted(blocks, reverse=True):
                if place & bit:
                    moved = swap(blocks.pop(place).astype(BF), bit).astype(F32)
                    blocks[place ^ bit] = blocks[place ^ bit] + moved
        return blocks

    def exchange(values):
        values = values.reshape(experts, capacity, width)
        return to_all(values, "wide").reshape(experts * capacity, width)

    sent = pack(
        [w_query, w_key, w_value], [first_gain, first_bias, second_gain, second_bias],
        w_router, routing, segments, wide, narrow, own_width, columns,
    )
    x_blocks = gather_blocks(hidden_in, chip_bits)
    out_low = w_out.astype(BF)
    if aligned:
        out_low = lax.ppermute(
            out_low, BOTH, [(n * wide + j, j * narrow + n) for n in range(narrow) for j in range(wide)]
        )
    sent, out_low, where, first_w, second_w = gate((sent, out_low, where, w_in[0], w_back[0]))
    *in_low, back_low = cast_weights(first_w, second_w, width // 3)
    weights = to_all(sent, BOTH).reshape(width, columns)
    for place in list(x_blocks):
        x_blocks[place ^ 1] = swap(x_blocks[place], 1)
    partners = [i for i in range(2, narrow, 2)]
    in_upper = [swap(in_low[0], i) for i in partners]
    placing, g_moved, out_tiled = place_cotangent(
        routing, cotangent, experts, capacity, out_low, wide
    )
    weights, in_low, back_low, g_moved, in_upper, out_tiled = gate(
        (weights, in_low, back_low, g_moved, in_upper, out_tiled)
    )
    back_came = [swap(back_low, i) for i in partners]
    if aligned:
        out_w = to_all(out_tiled, "wide").reshape(own_width, width)
    else:
        all_out = lax.all_gather(out_low, BOTH, axis=0, tiled=True)
        all_out = jnp.pad(all_out, ((0, own_width * narrow - width), (0, 0)))
        out_w = lax.dynamic_slice_in_dim(all_out, at_narrow * own_width, own_width, axis=0)

    x_list = [x_blocks[i] for i in range(narrow)]
    first, q, k, v, att, lse, vectors, stat, side = attention(
        where, x_list, weights, own_heads, piece, side_block, side_at, experts
    )
    att, g_moved = gate((att, g_moved))
    g_own = exchange(g_moved)
    parts = project(where, att, out_w, narrow)
    halves = reduce_blocks({i: parts[i] for i in range(narrow)}, core_bit)
    halves, back_came = gate((halves, back_came))
    halves = {i: swap(halves[i].astype(BF), i) if i else halves[i] for i in sorted(halves)}

    halves, g_own, in_low = gate((halves, g_own, in_low))
    in_lower = [swap(in_low[1], i) for i in partners]
    mixed, x_moved, gates, info = second_norm(
        hidden_in, [halves[i] for i in sorted(halves)], vectors, side, stat, placing, routing,
        where, (narrow, experts, total, side_at),
    )
    g_other = swap(g_own, 1)
    x_own = exchange(x_moved)
    x_own, in_lower = gate((x_own, in_lower))
    x_other = swap(x_own, 1)

    ins = [list(pair) for pair in zip(in_upper, in_lower)] + [in_low]
    backs = [*back_came, back_low]
    xs = [x_other, x_own]
    dx_o, dx_s, router, dy, acts, dzs, far_back = expert(info, xs, [g_other, g_own], vectors, ins, backs)

    def cross(cut):
        return [swap(value, place) for value, place in zip(cut, partners)]

    dx_sum = (dx_s + swap(dx_o, 1).astype(F32)).astype(BF)
    d_returned = exchange(dx_sum)
    acts, dx_sum = gate((acts, dx_sum))
    far_back = cross(far_back)
    ends = (0, width // 6, width * 2 // 3, width)
    y_o, y_s, made = partner_terms(xs, acts, dzs, backs, ends)
    own_back, own_in = own_terms(xs, dy, acts[-1], dzs[-1])
    y_sum = (y_s + swap(y_o, 1).astype(F32)).astype(BF)
    made, far_back, own_back, own_in, y_sum = gate((made, far_back, own_back, own_in, y_sum))
    crossed = [cross(made[0])]
    d_mixed, d_mixed_low, sums = second_back(d_returned, placing, mixed, cotangent, vectors)
    d_mixed_low, y_sum, crossed = gate((d_mixed_low, y_sum, crossed))
    returned = exchange(y_sum)
    dr_blocks = gather_blocks(d_mixed_low, chip_bits)
    for place in list(dr_blocks):
        dr_blocks[place ^ 1] = swap(dr_blocks[place], 1)
    dr_blocks, made = gate((dr_blocks, made))
    crossed.append(cross(made[1]))
    dr_list = [dr_blocks[i] for i in range(narrow)]

    d_qkv, terms_out = attention_back(
        where, dr_list, out_w, q, k, v, lse, stat, att, columns, seg_lane
    )
    d_qkv, crossed, terms_out, returned, made = gate((d_qkv, crossed, terms_out, returned, made))
    last_cross = cross(made[2])
    if aligned:
        terms_out = to_all(terms_out.reshape(wide, piece, width), "wide")
    terms = weight_terms(d_qkv, first, weights, info, sums, [router], side_block, side_at)

    tied = (terms, d_qkv, returned, terms_out, last_cross)
    terms, d_qkv, returned, terms_out, last_cross = gate(tied)
    d_parts = first_parts(where, d_qkv, weights, narrow)
    crossed.append(last_cross)
    terms = to_all(terms.reshape(devices, piece, columns), BOTH)
    d_halves = reduce_blocks({i: d_parts[i] for i in range(narrow)}, core_bit)
    d_halves = [swap(d_halves[i].astype(BF), i) if i else d_halves[i] for i in sorted(d_halves)]
    if aligned:
        grad_out_w = lax.ppermute(
            jnp.sum(terms_out.astype(F32), axis=0),
            BOTH,
            [(j * narrow + n, n * wide + j) for n in range(narrow) for j in range(wide)],
        )
    else:
        spread = jnp.zeros((own_width * narrow, width), F32)
        spread = lax.dynamic_update_slice_in_dim(
            spread, terms_out.astype(F32), at_narrow * own_width, axis=0
        )
        grad_out_w = lax.psum_scatter(spread[:width], BOTH, scatter_dimension=0, tiled=True)
    block_out = finish_rows(returned, placing, mixed, gates)
    grad_hidden = first_back(d_halves, hidden_in, d_mixed, vectors)
    back_terms, in_terms = sum_terms([own_back, own_in], [far_back[:1], [cut[0] for cut in crossed]])
    for i in range(1, len(partners)):
        back_terms = back_terms + far_back[i].astype(F32)
        in_terms = in_terms + jnp.concatenate([cut[i] for cut in crossed], axis=0).astype(F32)

    done = unpack(terms, wide, narrow, own_width, width, experts)
    return (
        block_out,
        done[8].reshape(()),
        grad_hidden,
        *[done[i].reshape(piece) for i in range(3, 7)],
        *done[:3],
        grad_out_w,
        done[7].T,
        in_terms[None],
        back_terms[None],
    )


def solution(mesh):
    rows = P(BOTH, None)
    vector = P(BOTH)
    placed = (rows, vector, rows) + (vector,) * 4 + (rows,) * 5
    expert_specs = (P("wide", None, "narrow"), P("wide", "narrow", None))
    return jax.shard_map(
        local,
        mesh=mesh,
        in_specs=placed + expert_specs + (rows,),
        out_specs=(rows, P(), rows) + (vector,) * 4 + (rows,) * 5 + expert_specs,
        check_vma=False,
    )
```
